32 devices in a mesh: seq: 8 (over z, x), head: 4 (over y, core).
Axes of the slice: x: 2, y: 2, z: 4, core: 2. Of those that a mesh axis runs over, the one named last changes fastest.
Arguments:
- tokens: bfloat16 [2, 2048, 768], P(None, ('seq', 'head')), may hold values from -6 to 6
- positions: int32 [2, 2048], P(None, 'seq'), may hold values from 0 to 2047, each once within a row
- w_qkv: bfloat16 [768, 2304], P(('seq', 'head')), may hold values from -0.21875 to 0.21875
- qv_bias: bfloat16 [2, 768], P(None, ('seq', 'head')), may hold values from -3 to 3
- w_attn_out: bfloat16 [768, 768], P(('seq', 'head')), may hold values from -0.875 to 0.875
- attn_out_bias: bfloat16 [768], P(('seq', 'head')), may hold values from -3 to 3
- norm1_gain: bfloat16 [768], P(('seq', 'head')), may hold values from 0.5 to 1.5
- norm1_bias: bfloat16 [768], P(('seq', 'head')), may hold values from -3 to 3
- w_in: bfloat16 [768, 6144], P(('seq', 'head')), may hold values from -0.21875 to 0.21875
- in_bias: bfloat16 [6144], P(('seq', 'head')), may hold values from -3 to 3
- w_out: bfloat16 [3072, 768], P(('seq', 'head')), may hold values from -0.109375 to 0.109375
- out_bias: bfloat16 [768], P(('seq', 'head')), may hold values from -3 to 3
- norm2_gain: bfloat16 [768], P(('seq', 'head')), may hold values from 0.5 to 1.5
- norm2_bias: bfloat16 [768], P(('seq', 'head')), may hold values from -3 to 3
- cotangent: bfloat16 [2, 2048, 768], P(None, ('seq', 'head')), may hold values from -6 to 6
Outputs:
- output: bfloat16 [2, 2048, 768], P(None, ('seq', 'head'))
- input_grad: float32 [2, 2048, 768], P(None, ('seq', 'head'))
- grad_w_qkv: float32 [768, 2304], P(('seq', 'head'))
- grad_qv_bias: float32 [2, 768], P(None, ('seq', 'head'))
- grad_w_attn_out: float32 [768, 768], P(('seq', 'head'))
- grad_attn_out_bias: float32 [768], P(('seq', 'head'))
- grad_norm1_gain: float32 [768], P(('seq', 'head'))
- grad_norm1_bias: float32 [768], P(('seq', 'head'))
- grad_w_in: float32 [768, 6144], P(('seq', 'head'))
- grad_in_bias: float32 [6144], P(('seq', 'head'))
- grad_w_out: float32 [3072, 768], P(('seq', 'head'))
- grad_out_bias: float32 [768], P(('seq', 'head'))
- grad_norm2_gain: float32 [768], P(('seq', 'head'))
- grad_norm2_bias: float32 [768], P(('seq', 'head'))
The draws below stay inside these ranges and needn't reach their ends.
Inputs may be any that keep to these rules, and one draw needn't show every extreme that they name: `positions`: each row holds every position 0 to 2047 exactly once.
All inputs are finite; a program needn't handle non-finite values.
Results may differ from the reference program's by a relative error of at most 0.039.
Values may be sent and summed in bfloat16 or wider, within the bound.
No kernel may reach another device: no remote copies, remote signals or barrier semaphores. Data moves between devices by JAX's collectives and lax.ppermute only.
A program may use at most 192 MiB of HBM per device.

```python
import jax
import jax.numpy as jnp
from jax import lax

D = 768
HEADS = 12
HEAD_DIM = 64
FF = 3072
SEQS = 2
LENGTH = 2048


def levels(stream_key, shape, pieces, least, largest):
    level, own = 1.0, jax.random.fold_in(stream_key, 6)
    for position, shards_of in pieces:
        steps = jnp.exp(jax.random.uniform(jax.random.fold_in(own, position), (shards_of,), jnp.float32, least / len(pieces), largest / len(pieces)))
        level = level * jnp.repeat(steps, shape[position] // shards_of).reshape([-1 if axis == position else 1 for axis in range(len(shape))])
    return level


def bell_draw(key, dims, spread, bound, shards=(), kind=jnp.bfloat16):
    values = spread * jax.random.normal(key, dims, jnp.float32)
    if shards:
        values = values * levels(key, dims, shards, -0.22, 0.18)
    return jnp.clip(values, -bound, bound).astype(kind)


def setup_inputs(seed: int = 0) -> dict:
    arg_keys = jax.random.split(jax.random.key(seed), 16)
    return {
        "tokens": bell_draw(arg_keys[0], (SEQS, LENGTH, D), 1.0, 6.0, ((1, 32),)),
        "positions": jax.vmap(lambda own: jax.random.permutation(own, LENGTH))(jax.random.split(arg_keys[1], SEQS)).reshape((SEQS, LENGTH)).astype(jnp.int32),
        "w_qkv": bell_draw(arg_keys[2], (D, 3 * HEADS * HEAD_DIM), D ** -0.5, 0.21875, ((0, 32),)),
        "qv_bias": bell_draw(arg_keys[3], (2, HEADS * HEAD_DIM), 0.5, 3.0, ((1, 32),)),
        "w_attn_out": bell_draw(arg_keys[4], (HEADS * HEAD_DIM, D), (HEADS * HEAD_DIM // 16) ** -0.5, 0.875, ((0, 32),)),
        "attn_out_bias": bell_draw(arg_keys[5], (D,), 0.5, 3.0, ((0, 32),)),
        "norm1_gain": jnp.clip(1.0 + 0.1 * jax.random.normal(arg_keys[6], (D,), jnp.float32), 0.5, 1.5).astype(jnp.bfloat16),
        "norm1_bias": bell_draw(arg_keys[7], (D,), 0.5, 3.0, ((0, 32),)),
        "w_in": bell_draw(arg_keys[8], (D, 2 * FF), D ** -0.5, 0.21875, ((0, 32),)),
        "in_bias": bell_draw(arg_keys[9], (2 * FF,), 0.5, 3.0, ((0, 32),)),
        "w_out": bell_draw(arg_keys[10], (FF, D), FF ** -0.5, 0.109375, ((0, 32),)),
        "out_bias": bell_draw(arg_keys[11], (D,), 0.5, 3.0, ((0, 32),)),
        "norm2_gain": jnp.clip(1.0 + 0.1 * jax.random.normal(arg_keys[12], (D,), jnp.float32), 0.5, 1.5).astype(jnp.bfloat16),
        "norm2_bias": bell_draw(arg_keys[13], (D,), 0.5, 3.0, ((0, 32),)),
        "cotangent": bell_draw(arg_keys[14], (SEQS, LENGTH, D), 1.0, 6.0, ((1, 32),)),
    }


FULL_ACCURACY = lax.Precision.HIGHEST
EPSILON = 1e-12
SCORE_SCALE = 0.125

@jax.custom_vjp
def low(v):
    return lax.optimization_barrier(v.astype(jnp.bfloat16)).astype(jnp.float32)

@jax.custom_vjp
def low_back(v):
    return v

def low_keep(v):
    return (low(v), None)

def low_pass(kept, grad):
    return (grad,)

def back_keep(v):
    return (v, None)

def back_low(kept, grad):
    return (low(grad),)
low.defvjp(low_keep, low_pass)
low_back.defvjp(back_keep, back_low)

def layer_norm(values, gain_vec, offsets):
    average = lax.optimization_barrier(jnp.mean(values, axis=-1, keepdims=True))
    centred = values - average
    variance = lax.optimization_barrier(jnp.mean(centred * centred, axis=-1, keepdims=True))
    return centred * lax.rsqrt(variance + EPSILON) * gain_vec + offsets

def geglu(merged_heads):
    half_width = merged_heads.shape[-1] // 2
    return jax.nn.gelu(merged_heads[..., :half_width], approximate=False) * merged_heads[..., half_width:]

def attend_sequence(qkv_row, position_row, slopes):
    inner_width = HEADS * HEAD_DIM
    query_heads = qkv_row[:, :inner_width].reshape(LENGTH, HEADS, HEAD_DIM)
    key_heads = qkv_row[:, inner_width:2 * inner_width].reshape(LENGTH, HEADS, HEAD_DIM)
    value_heads = qkv_row[:, 2 * inner_width:].reshape(LENGTH, HEADS, HEAD_DIM)
    stride = min(512, LENGTH)

    def one_block(member):
        query_block, pos_block = member
        scores = jnp.einsum('qhd,khd->hqk', query_block, key_heads, precision=FULL_ACCURACY) * SCORE_SCALE
        distances = jnp.abs(pos_block[:, None] - position_row[None, :]).astype(jnp.float32)
        scores = low_back(scores - slopes[:, None, None] * distances[None, :, :])
        weights = low(jax.nn.softmax(scores, axis=-1))
        return jnp.einsum('hqk,khd->qhd', weights, value_heads, precision=FULL_ACCURACY)
    outputs = lax.map(jax.checkpoint(one_block), (query_heads.reshape(LENGTH // stride, stride, HEADS, HEAD_DIM), position_row.reshape(LENGTH // stride, stride)))
    return outputs.reshape(LENGTH, inner_width)

def reference(tokens, positions, w_qkv, qv_bias, w_attn_out, attn_out_bias, norm1_gain, norm1_bias, w_in, in_bias, w_out, out_bias, norm2_gain, norm2_bias, cotangent):
    slopes = 2.0 ** (-8.0 * (jnp.arange(HEADS) + 1).astype(jnp.float32) / HEADS)
    inner_width = HEADS * HEAD_DIM

    def forward(input_rows, query_key_value_matrix, qv_offsets, attention_matrix, attention_shifts, first_gain, first_offsets, input_matrix, input_shifts, output_matrix, output_shifts, second_gain, second_offsets):
        column_bias_terms = jnp.concatenate([qv_offsets[0], jnp.zeros((inner_width,), jnp.float32), qv_offsets[1]])
        projection_result = jnp.einsum('waj,jr->war', input_rows, query_key_value_matrix, precision=FULL_ACCURACY) + column_bias_terms
        projection_result = low_back(low(projection_result))
        attention_result = lax.map(lambda member: attend_sequence(member[0], member[1], slopes), (projection_result, positions))
        attention_result = low_back(low(attention_result))
        attention_linear = jnp.einsum('thx,xn->thn', attention_result, attention_matrix, precision=FULL_ACCURACY) + attention_shifts
        attention_linear = low_back(attention_linear)
        hidden = layer_norm(input_rows + attention_linear, first_gain, first_offsets)
        hidden_reduced = low(hidden)
        merged_heads = jnp.einsum('nau,uy->nay', hidden_reduced, input_matrix, precision=FULL_ACCURACY) + input_shifts
        merged_heads = low_back(merged_heads)
        gelu_activations = low(geglu(merged_heads))
        feedforward_linear = jnp.einsum('tvj,jm->tvm', gelu_activations, output_matrix, precision=FULL_ACCURACY) + output_shifts
        feedforward_linear = low_back(feedforward_linear)
        return layer_norm(hidden + feedforward_linear, second_gain, second_offsets)
    floats = tuple((member.astype(jnp.float32) for member in (tokens, w_qkv, qv_bias, w_attn_out, attn_out_bias, norm1_gain, norm1_bias, w_in, in_bias, w_out, out_bias, norm2_gain, norm2_bias)))
    result, backward = jax.vjp(forward, *floats)
    grads = backward(cotangent.astype(jnp.float32))
    return (result.astype(jnp.bfloat16), grads[0], grads[1], grads[2], grads[3], grads[4], grads[5], grads[6], grads[7], grads[8], grads[9], grads[10], grads[11], grads[12])
```

```python
import jax
import jax.numpy as jnp
from jax import lax
from jax.experimental import pallas as pl
from jax.experimental.pallas import tpu as pltpu
from jax.sharding import Mesh
from jax.sharding import PartitionSpec as P

HEADS = 12
HEAD_DIM = 64
GROUPS = 4
GROUP_HEADS = HEADS // GROUPS
GROUP_WIDTH = GROUP_HEADS * HEAD_DIM
EPSILON = 1e-12
SCORE_SCALE = 0.125
LOG2E = 1.4426950408889634
LOWEST = -1e30
KEY_BLOCK = 512
SEQ_GROUP = ("s", "g")
TOKEN_GROUP = ("y", "c")
CHUNKS = ("e", "y", "c")
SEQ_AXIS = ("s", "e", "g")
EVERY = ("s", "e", "g", "y", "c")
SWAP = ((0, 1), (1, 0))
BF16 = jnp.bfloat16
F32 = jnp.float32
VMEM_BYTES = 60 * 2**20


def nt(a, b):
    return lax.dot_general(a, b, (((1,), (1,)), ((), ())), preferred_element_type=F32)


def tn(a, b):
    return lax.dot_general(a, b, (((0,), (0,)), ((), ())), preferred_element_type=F32)


def nn(a, b):
    return lax.dot_general(a, b, (((1,), (0,)), ((), ())), preferred_element_type=F32)


def head_cols(head, base=0):
    return slice(base + head * HEAD_DIM, base + (head + 1) * HEAD_DIM)


def log2_scores(keys, queries, slope, key_pos, query_pos):
    products = nt(keys, queries)
    distances = jnp.abs(key_pos * slope - query_pos * slope)
    return products * (SCORE_SCALE * LOG2E) - distances


def attend_kernel(slopes_ref, q_ref, kv_ref, pq_ref, pk_ref, low_ref, out_ref, lse_ref):
    rows = q_ref.shape[0]
    blocks = kv_ref.shape[0] // KEY_BLOCK
    query_pos = pq_ref[...]
    for head in range(GROUP_HEADS):
        slope = slopes_ref[head]
        queries = q_ref[:, head_cols(head)]

        def visit(block, carry):
            top, total, summed = carry
            at = pl.ds(pl.multiple_of(block * KEY_BLOCK, KEY_BLOCK), KEY_BLOCK)
            keys = kv_ref[at, head_cols(head)]
            values = kv_ref[at, head_cols(head, GROUP_WIDTH)]
            scores = log2_scores(keys, queries, slope, pk_ref[at, :], query_pos)
            new_top = jnp.maximum(top, jnp.max(scores, axis=0, keepdims=True))
            weights = jnp.exp2(scores - new_top)
            shrink = jnp.exp2(top - new_top)
            total = total * shrink + jnp.sum(weights, axis=0, keepdims=True)
            summed = summed * shrink + tn(values, weights.astype(BF16))
            return new_top, total, summed

        top, total, summed = lax.fori_loop(
            0,
            blocks,
            visit,
            (
                jnp.full((1, rows), LOWEST, F32),
                jnp.zeros((1, rows), F32),
                jnp.zeros((HEAD_DIM, rows), F32),
            ),
        )
        attended = summed / total
        out_ref[head_cols(head), :] = attended
        low_ref[:, head_cols(head)] = attended.T.astype(BF16)
        lse_ref[head : head + 1, :] = top + jnp.log2(total)


def attend(slopes, queries, key_values, query_pos, key_pos):
    rows, length = queries.shape[0], key_values.shape[0]
    vmem = pl.BlockSpec(memory_space=pltpu.VMEM)
    return pl.pallas_call(
        attend_kernel,
        out_shape=(
            jax.ShapeDtypeStruct((rows, GROUP_WIDTH), BF16),
            jax.ShapeDtypeStruct((GROUP_WIDTH, rows), F32),
            jax.ShapeDtypeStruct((GROUP_HEADS, rows), F32),
        ),
        in_specs=[pl.BlockSpec(memory_space=pltpu.SMEM)] + [vmem] * 4,
        out_specs=(vmem,) * 3,
        compiler_params=pltpu.CompilerParams(vmem_limit_bytes=VMEM_BYTES),
        cost_estimate=pl.CostEstimate(
            flops=4 * rows * length * GROUP_WIDTH,
            bytes_accessed=rows * length,
            transcendentals=rows * length * GROUP_HEADS,
        ),
        name="attend",
    )(slopes, queries, key_values, query_pos, key_pos)


def attend_back_kernel(
    slopes_ref, q_ref, kv_ref, pq_ref, pk_ref, do_ref, out_ref, lse_ref, dq_ref, dkv_ref
):
    rows = q_ref.shape[0]
    blocks = kv_ref.shape[0] // KEY_BLOCK
    query_pos = pq_ref[...]
    for head in range(GROUP_HEADS):
        slope = slopes_ref[head]
        queries = q_ref[:, head_cols(head)]
        out_grads = do_ref[:, head_cols(head)]
        log_sum = lse_ref[head : head + 1, :]
        delta = jnp.sum(
            out_grads.astype(F32).T * out_ref[head_cols(head), :], axis=0, keepdims=True
        )

        def visit(block, query_grads):
            at = pl.ds(pl.multiple_of(block * KEY_BLOCK, KEY_BLOCK), KEY_BLOCK)
            keys = kv_ref[at, head_cols(head)]
            values = kv_ref[at, head_cols(head, GROUP_WIDTH)]
            scores = log2_scores(keys, queries, slope, pk_ref[at, :], query_pos)
            probs = jnp.exp2(scores - log_sum)
            prob_grads = nt(values, out_grads)
            score_grads = (probs * (prob_grads - delta)).astype(BF16)
            dkv_ref[at, head_cols(head, GROUP_WIDTH)] = nn(
                probs.astype(BF16), out_grads
            ).astype(BF16)
            dkv_ref[at, head_cols(head)] = (nn(score_grads, queries) * SCORE_SCALE).astype(BF16)
            return query_grads + tn(keys, score_grads)

        query_grads = lax.fori_loop(0, blocks, visit, jnp.zeros((HEAD_DIM, rows), F32))
        dq_ref[:, head_cols(head)] = (query_grads * SCORE_SCALE).T.astype(BF16)


def attend_back(slopes, queries, key_values, query_pos, key_pos, out_grads, attended, log_sums):
    rows, length = queries.shape[0], key_values.shape[0]
    vmem = pl.BlockSpec(memory_space=pltpu.VMEM)
    return pl.pallas_call(
        attend_back_kernel,
        out_shape=(
            jax.ShapeDtypeStruct((rows, GROUP_WIDTH), BF16),
            jax.ShapeDtypeStruct((length, 2 * GROUP_WIDTH), BF16),
        ),
        in_specs=[pl.BlockSpec(memory_space=pltpu.SMEM)] + [vmem] * 7,
        out_specs=(vmem,) * 2,
        compiler_params=pltpu.CompilerParams(vmem_limit_bytes=VMEM_BYTES),
        cost_estimate=pl.CostEstimate(
            flops=10 * rows * length * GROUP_WIDTH,
            bytes_accessed=rows * length,
            transcendentals=rows * length * GROUP_HEADS,
        ),
        name="attend_back",
    )(slopes, queries, key_values, query_pos, key_pos, out_grads, attended, log_sums)


def layer_norm(values, gain_vec, offsets):
    average = jnp.mean(values, axis=-1, keepdims=True)
    centred = values - average
    variance = jnp.mean(centred * centred, axis=-1, keepdims=True)
    return centred * lax.rsqrt(variance + EPSILON) * gain_vec + offsets


def geglu(joined):
    half_width = joined.shape[-1] // 2
    return (
        jax.nn.gelu(joined[..., :half_width], approximate=False) * joined[..., half_width:]
    )


def gather_group(block):
    pair = jnp.concatenate([block, lax.ppermute(block, "y", SWAP)])
    return jnp.concatenate([pair, lax.ppermute(pair, "c", SWAP)])


def sum_group(parts):
    half = parts.shape[0] // 2
    quarter = half // 2
    pair = parts[:half].astype(F32) + lax.ppermute(
        parts[half:].astype(BF16), "c", SWAP
    ).astype(F32)
    return pair[:quarter] + lax.ppermute(pair[quarter:].astype(BF16), "y", SWAP).astype(F32)


def body(
    tokens,
    positions,
    w_qkv,
    qv_bias,
    w_attn_out,
    attn_out_bias,
    norm1_gain,
    norm1_bias,
    w_in,
    in_bias,
    w_out,
    out_bias,
    norm2_gain,
    norm2_bias,
    cotangent,
):
    seq_count, row_count, width = tokens.shape
    outer = lax.axis_size("e")
    seq_size = 2 * outer * GROUPS
    devices = seq_size * 4
    shard = w_qkv.shape[0]
    ff_shard = w_out.shape[0]
    group = lax.axis_index("g")
    place = lax.axis_index("y") * 2 + lax.axis_index("c")
    qkv_cols = 3 * GROUP_WIDTH

    with jax.named_scope("gather_tokens"):
        spread = jnp.broadcast_to(
            tokens[:, None], (2, GROUPS, row_count, width)
        ).reshape(8, row_count, width)
        chunk = lax.all_to_all(spread, SEQ_GROUP, 0, 0, tiled=True).reshape(8 * row_count, width)

    small_parts = [
        qv_bias.reshape(-1),
        attn_out_bias,
        norm1_gain,
        norm1_bias,
        out_bias,
        norm2_gain,
        norm2_bias,
        in_bias,
    ]
    small_sizes = [part.shape[0] for part in small_parts]
    small_total = sum(small_sizes)
    extra = -(-(small_total + 2 * row_count) // shard)
    wide = -(-(qkv_cols + extra) // 128) * 128
    spare = wide - qkv_cols

    with jax.named_scope("gather_qkv_weights"):
        own_pos = lax.dynamic_slice_in_dim(positions, place * row_count, row_count, 1)
        pos_parts = jnp.concatenate([own_pos >> 7, own_pos & 127], axis=1).astype(BF16)
        filling = jnp.zeros((2, shard * spare - small_total - 2 * row_count), BF16)
        smalls = jnp.concatenate(small_parts)
        row = jnp.concatenate(
            [pos_parts, jnp.broadcast_to(smalls, (2, small_total)), filling], axis=1
        ).reshape(2, 1, shard, spare)
        columns = (
            w_qkv.reshape(shard, 3, GROUPS, GROUP_WIDTH)
            .transpose(2, 0, 1, 3)
            .reshape(1, GROUPS, shard, qkv_cols)
        )
        parcel = jnp.concatenate(
            [
                jnp.broadcast_to(columns, (2, GROUPS, shard, qkv_cols)),
                jnp.broadcast_to(row, (2, GROUPS, shard, spare)),
            ],
            axis=3,
        ).reshape(8, shard, wide)
        parcel = lax.all_to_all(parcel, SEQ_GROUP, 0, 0, tiled=True)
        parcels = lax.all_gather(parcel, CHUNKS, axis=0, tiled=False).reshape(
            outer, 2, 2, 2, GROUPS, shard, wide
        )
        qkv_slice = (
            parcels[..., :qkv_cols].transpose(3, 0, 4, 1, 2, 5, 6).reshape(width, qkv_cols)
        )
        vectors = parcels[..., qkv_cols:].reshape(outer, 2, 2, 2, GROUPS, shard * spare)

        def vector(number):
            at = 2 * row_count + sum(small_sizes[:number])
            return (
                vectors[..., at : at + small_sizes[number]]
                .transpose(3, 0, 4, 1, 2, 5)
                .reshape(devices, small_sizes[number])
            )

        qv_full = vector(0).reshape(devices, 2, shard).transpose(1, 0, 2).reshape(2, width)
        attn_bias, first_gain, first_offset, out_shift, second_gain, second_offset, in_shift = (
            vector(number).reshape(-1).astype(F32) for number in range(1, 8)
        )
        chunk_pos = (
            vectors[..., :row_count].astype(F32) * 128.0
            + vectors[..., row_count : 2 * row_count].astype(F32)
        ).reshape(outer, 2, 2, 8 * row_count)

    with jax.named_scope("gather_ff_weights"):
        in_parts = (
            w_in.reshape(shard, 2 * seq_size, 4, ff_shard)
            .transpose(2, 0, 1, 3)
            .reshape(4, shard, 2 * seq_size * ff_shard)
        )
        in_parts = lax.all_to_all(in_parts, TOKEN_GROUP, 0, 0, tiled=True)
        in_slice = lax.all_gather(
            in_parts.reshape(4 * shard, 2 * seq_size * ff_shard), SEQ_AXIS, axis=0, tiled=True
        )
        out_slice = lax.all_gather(w_out, SEQ_AXIS, axis=0, tiled=True)
        attn_full = lax.all_gather(w_attn_out, EVERY, axis=0, tiled=True)
        in_shift_slice = lax.dynamic_index_in_dim(
            in_shift.reshape(2 * seq_size, 4, ff_shard), place, 1, keepdims=False
        ).reshape(-1)

    with jax.named_scope("project"):
        qv_slice = lax.dynamic_slice_in_dim(qv_full, group * GROUP_WIDTH, GROUP_WIDTH, 1).astype(
            F32
        )
        column_bias = jnp.concatenate(
            [qv_slice[0], jnp.zeros((GROUP_WIDTH,), F32), qv_slice[1]]
        )
        qkv = (
            jnp.dot(chunk, qkv_slice, preferred_element_type=F32) + column_bias
        ).astype(BF16)
        queries, own_kv = qkv[:, :GROUP_WIDTH], qkv[:, GROUP_WIDTH:]
    with jax.named_scope("gather_kv"):
        spans = [own_kv]
        if outer > 1:
            spans = [lax.all_gather(own_kv, "e", axis=0, tiled=True)]
        key_values = gather_group(spans[0])
    y_at, c_at = lax.axis_index("y"), lax.axis_index("c")
    ordered_pos = jnp.stack(
        [
            lax.dynamic_index_in_dim(
                lax.dynamic_index_in_dim(chunk_pos, y_at ^ ky, 1, keepdims=False),
                c_at ^ kc,
                1,
                keepdims=False,
            )
            for kc in (0, 1)
            for ky in (0, 1)
        ]
    )
    query_pos = lax.dynamic_index_in_dim(ordered_pos[0], lax.axis_index("e"), 0, keepdims=True)[0]
    query_pos = query_pos.reshape(1, -1)
    key_pos = ordered_pos.reshape(-1, 1)
    head_ids = group * GROUP_HEADS + jnp.arange(GROUP_HEADS)
    slopes = 2.0 ** (-8.0 * (head_ids + 1).astype(F32) / HEADS) * LOG2E

    with jax.named_scope("attention"):
        attended_low, attended, log_sums = attend(slopes, queries, key_values, query_pos, key_pos)

    with jax.named_scope("return_attended"):
        returned = lax.all_to_all(
            attended_low.reshape(8, row_count, GROUP_WIDTH), SEQ_GROUP, 0, 0, tiled=True
        )
        mixed = (
            returned.reshape(2, GROUPS, row_count, GROUP_WIDTH)
            .transpose(0, 2, 1, 3)
            .reshape(2 * row_count, width)
        )
    with jax.named_scope("first_norm"):
        rows = tokens.reshape(2 * row_count, width)
        attn_lin = jnp.dot(mixed, attn_full, preferred_element_type=F32) + attn_bias
        hidden, first_back = jax.vjp(
            layer_norm, rows.astype(F32) + attn_lin, first_gain, first_offset
        )
        hidden_low = hidden.astype(BF16)
    with jax.named_scope("gather_hidden"):
        hidden_group = gather_group(hidden_low)
    with jax.named_scope("ff_forward"):
        joined = jnp.dot(hidden_group, in_slice, preferred_element_type=F32) + in_shift_slice
        activated, gate_back = jax.vjp(geglu, joined)
        activated_low = activated.astype(BF16)
        ff_parts = jnp.dot(activated_low, out_slice, preferred_element_type=F32)
    with jax.named_scope("sum_ff"):
        ff_lin = sum_group(ff_parts) + out_shift
    with jax.named_scope("second_norm"):
        result, second_back = jax.vjp(layer_norm, hidden + ff_lin, second_gain, second_offset)
        second_grad, grad_gain_two, grad_offset_two = second_back(
            cotangent.reshape(2 * row_count, width).astype(F32)
        )
        ff_grad = second_grad.astype(BF16)
        grad_out_bias = jnp.sum(ff_grad.astype(F32), axis=0)
    with jax.named_scope("gather_ff_grad"):
        ff_grads = gather_group(ff_grad)
    with jax.named_scope("ff_backward"):
        act_grad = nt(ff_grads, out_slice)
        joined_grad = gate_back(act_grad)[0].astype(BF16)
        hidden_parts = nt(joined_grad, in_slice)
    with jax.named_scope("sum_hidden_grad"):
        hidden_grad = second_grad + sum_group(hidden_parts)
    with jax.named_scope("ff_weight_grads"):
        grad_out_slice = tn(activated_low, ff_grads).astype(BF16)
        grad_in_slice = tn(hidden_group, joined_grad).astype(BF16)
        grad_in_shift = jnp.sum(joined_grad.astype(F32), axis=0)
        grad_w_out = lax.psum_scatter(
            grad_out_slice, SEQ_AXIS, scatter_dimension=0, tiled=True
        ).astype(F32)
        grad_in_rows = lax.psum_scatter(
            grad_in_slice, SEQ_AXIS, scatter_dimension=0, tiled=True
        )
        grad_in_parts = lax.all_to_all(
            grad_in_rows.reshape(4, shard, 2 * seq_size * ff_shard), TOKEN_GROUP, 0, 0, tiled=True
        )
        grad_w_in = (
            grad_in_parts.reshape(4, shard, 2 * seq_size, ff_shard)
            .transpose(1, 2, 0, 3)
            .reshape(shard, 2 * devices * ff_shard)
            .astype(F32)
        )
    with jax.named_scope("first_norm_back"):
        first_grad, grad_gain_one, grad_offset_one = first_back(hidden_grad)
        attn_grad = first_grad.astype(BF16)
        grad_attn_bias = jnp.sum(attn_grad.astype(F32), axis=0)
        out_grad = nt(attn_grad, attn_full).astype(BF16)
    with jax.named_scope("send_out_grad"):
        out_grads = lax.all_to_all(
            out_grad.reshape(2, row_count, GROUPS, GROUP_WIDTH)
            .transpose(0, 2, 1, 3)
            .reshape(8, row_count, GROUP_WIDTH),
            SEQ_GROUP,
            0,
            0,
            tiled=True,
        ).reshape(8 * row_count, GROUP_WIDTH)
    with jax.named_scope("attn_weight_grad"):
        grad_attn = (
            tn(mixed, attn_grad)
            .astype(BF16)
            .reshape(seq_size, 4, shard, width)
            .transpose(1, 0, 2, 3)
            .reshape(width, width)
        )
        grad_attn = lax.psum_scatter(grad_attn, TOKEN_GROUP, scatter_dimension=0, tiled=True)
        grad_w_attn = lax.psum_scatter(
            grad_attn, SEQ_AXIS, scatter_dimension=0, tiled=True
        ).astype(F32)

    with jax.named_scope("attention_back"):
        query_grads, kv_parts = attend_back(
            slopes, queries, key_values, query_pos, key_pos, out_grads, attended, log_sums
        )
    with jax.named_scope("sum_kv_grads"):
        kv_grads = sum_group(kv_parts)
        if outer > 1:
            kv_grads = lax.psum_scatter(kv_grads, "e", scatter_dimension=0, tiled=True)
        qkv_grad = jnp.concatenate([query_grads, kv_grads.astype(BF16)], axis=1)

    with jax.named_scope("input_grad"):
        input_parts = nt(qkv_grad, qkv_slice).astype(BF16).reshape(8, row_count, width)
        input_parts = lax.all_to_all(input_parts, SEQ_GROUP, 0, 0, tiled=True)
        input_grad = first_grad.reshape(2, row_count, width) + jnp.sum(
            input_parts.reshape(2, GROUPS, row_count, width).astype(F32), axis=1
        )
    with jax.named_scope("qkv_weight_grad"):
        grad_qkv_cols = tn(chunk, qkv_grad)
        column_sums = jnp.sum(qkv_grad.astype(F32), axis=0)
        grad_qv = lax.dynamic_update_slice(
            jnp.zeros((2, width), F32),
            jnp.stack([column_sums[:GROUP_WIDTH], column_sums[2 * GROUP_WIDTH :]]),
            (0, group * GROUP_WIDTH),
        )
        grad_in_bias = lax.dynamic_update_slice(
            jnp.zeros((2 * seq_size, 4, ff_shard), F32),
            grad_in_shift.reshape(2 * seq_size, 1, ff_shard),
            (0, place, 0),
        )
        small_grads = jnp.concatenate(
            [
                grad_qv.reshape(2, devices, shard).transpose(1, 0, 2).reshape(devices, 2 * shard),
                grad_attn_bias.reshape(devices, shard),
                grad_gain_one.reshape(devices, shard),
                grad_offset_one.reshape(devices, shard),
                grad_out_bias.reshape(devices, shard),
                grad_gain_two.reshape(devices, shard),
                grad_offset_two.reshape(devices, shard),
                grad_in_bias.reshape(devices, 2 * ff_shard),
                jnp.zeros((devices, shard * spare - small_total), F32),
            ],
            axis=1,
        ).reshape(devices, shard, spare)
        bundle = jnp.concatenate(
            [grad_qkv_cols.reshape(devices, shard, qkv_cols), small_grads], axis=2
        ).reshape(2 * seq_size, 2, shard, wide)
        keep = lax.dynamic_index_in_dim(bundle, c_at, 1, keepdims=False)
        give = lax.dynamic_index_in_dim(bundle, 1 - c_at, 1, keepdims=False).astype(BF16)
        keep = keep + lax.ppermute(give, "c", SWAP).astype(F32)
        shares = lax.all_to_all(
            keep.astype(BF16), ("s", "e", "g", "y"), 0, 0, tiled=True
        ).astype(F32)
        grad_w_qkv = (
            jnp.sum(
                shares[..., :qkv_cols].reshape(2 * outer, GROUPS, 2, shard, 3, GROUP_WIDTH),
                axis=(0, 2),
            )
            .transpose(1, 2, 0, 3)
            .reshape(shard, 3 * width)
        )
        totals = jnp.sum(shares[..., qkv_cols:], axis=0).reshape(-1)
        vectors_out = []
        at = 0
        for size in small_sizes:
            vectors_out.append(totals[at : at + size])
            at += size

    return (
        result.reshape(2, row_count, width).astype(BF16),
        input_grad,
        grad_w_qkv,
        vectors_out[0].reshape(2, shard),
        grad_w_attn,
        vectors_out[1],
        vectors_out[2],
        vectors_out[3],
        grad_w_in,
        vectors_out[7],
        grad_w_out,
        vectors_out[4],
        vectors_out[5],
        vectors_out[6],
    )


def solution(mesh):
    seq_size = mesh.shape["seq"]
    split = Mesh(mesh.devices.reshape(2, seq_size // 8, 4, 2, 2), EVERY)
    tokens_at = P(None, EVERY, None)
    rows_at = P(EVERY, None)
    vector_at = P(EVERY)
    return jax.shard_map(
        body,
        mesh=split,
        in_specs=(
            tokens_at,
            P(None, SEQ_AXIS),
            rows_at,
            P(None, EVERY),
            rows_at,
            vector_at,
            vector_at,
            vector_at,
            rows_at,
            vector_at,
            rows_at,
            vector_at,
            vector_at,
            vector_at,
            tokens_at,
        ),
        out_specs=(
            tokens_at,
            tokens_at,
            rows_at,
            P(None, EVERY),
            rows_at,
            vector_at,
            vector_at,
            vector_at,
            rows_at,
            vector_at,
            rows_at,
            vector_at,
            vector_at,
            vector_at,
        ),
        check_vma=False,
    )
```

```python
import functools

import jax
import jax.numpy as jnp
from jax import lax
from jax.experimental import pallas as pl
from jax.experimental.pallas import tpu as pltpu
from jax.sharding import Mesh
from jax.sharding import PartitionSpec as P

HEADS = 12
HEAD_DIM = 64
GROUPS = 4
GROUP_HEADS = HEADS // GROUPS
GROUP_WIDTH = GROUP_HEADS * HEAD_DIM
EPSILON = 1e-12
SCORE_SCALE = 0.125
LOG2E = 1.4426950408889634
LOWEST = -1e30
KEY_BLOCK = 512
FF_TILE = 256
SEQ_GROUP = ("s", "r", "x")
CHUNKS = ("e", "y", "c")
RING = ("s", "e", "r")
PLANE = ("x", "y")
SEQ_AXIS = ("s", "e", "r", "x")
EVERY = ("s", "e", "r", "x", "y", "c")
SWAP = ((0, 1), (1, 0))
BF16 = jnp.bfloat16
F32 = jnp.float32
VMEM_BYTES = 60 * 2**20


def nt(a, b):
    return lax.dot_general(a, b, (((1,), (1,)), ((), ())), preferred_element_type=F32)


def tn(a, b):
    return lax.dot_general(a, b, (((0,), (0,)), ((), ())), preferred_element_type=F32)


def nn(a, b):
    return lax.dot_general(a, b, (((1,), (0,)), ((), ())), preferred_element_type=F32)


def head_cols(head, base=0):
    return slice(base + head * HEAD_DIM, base + (head + 1) * HEAD_DIM)


def log2_scores(keys, queries, slope, key_pos, query_pos):
    products = nt(keys, queries)
    distances = jnp.abs(key_pos * slope - query_pos * slope)
    return products * (SCORE_SCALE * LOG2E) - distances


def column(row):
    return jnp.broadcast_to(row, (8, row.shape[1])).T[:, :1]


def key_blocks(kv_refs):
    start = 0
    for piece in kv_refs:
        yield piece, start
        start += piece.shape[0]


def turn_positions(pk_ref, column_ref):
    def turn(block, carry):
        at = pl.ds(pl.multiple_of(block * KEY_BLOCK, KEY_BLOCK), KEY_BLOCK)
        column_ref[at, :] = column(pk_ref[pl.ds(block, 1), :])
        return carry

    lax.fori_loop(0, pk_ref.shape[0], turn, 0)


def attend_kernel(count, first, last, slopes_ref, q_ref, pq_ref, pk_ref, *refs):
    kv_refs, refs = refs[:count], refs[count:]
    if not first:
        (sum_in_ref, stat_in_ref), refs = refs[:2], refs[2:]
    sum_ref, stat_ref = refs[:2]
    column_ref = refs[-1]
    rows = q_ref.shape[0]
    query_pos = pq_ref[...]
    turn_positions(pk_ref, column_ref)
    for head in range(GROUP_HEADS):
        slope = slopes_ref[head]
        queries = q_ref[:, head_cols(head)]
        if first:
            carry = (
                jnp.full((1, rows), LOWEST, F32),
                jnp.zeros((1, rows), F32),
                jnp.zeros((HEAD_DIM, rows), F32),
            )
        else:
            carry = (
                stat_in_ref[head : head + 1, :],
                stat_in_ref[GROUP_HEADS + head : GROUP_HEADS + head + 1, :],
                sum_in_ref[head_cols(head), :],
            )
        for kv_ref, start in key_blocks(kv_refs):

            def visit(block, carry, kv_ref=kv_ref, start=start):
                top, total, summed = carry
                at = pl.ds(pl.multiple_of(block * KEY_BLOCK, KEY_BLOCK), KEY_BLOCK)
                pos_at = pl.ds(
                    pl.multiple_of(start + block * KEY_BLOCK, KEY_BLOCK), KEY_BLOCK
                )
                keys = kv_ref[at, head_cols(head)]
                values = kv_ref[at, head_cols(head, GROUP_WIDTH)]
                scores = log2_scores(keys, queries, slope, column_ref[pos_at, :], query_pos)
                new_top = jnp.maximum(top, jnp.max(scores, axis=0, keepdims=True))
                weights = jnp.exp2(scores - new_top)
                shrink = jnp.exp2(top - new_top)
                total = total * shrink + jnp.sum(weights, axis=0, keepdims=True)
                summed = summed * shrink + tn(values, weights.astype(BF16))
                return new_top, total, summed

            carry = lax.fori_loop(0, kv_ref.shape[0] // KEY_BLOCK, visit, carry)
        top, total, summed = carry
        if last:
            attended = summed / total
            sum_ref[head_cols(head), :] = attended
            refs[2][:, head_cols(head)] = attended.T.astype(BF16)
            stat_ref[head : head + 1, :] = top + jnp.log2(total)
        else:
            sum_ref[head_cols(head), :] = summed
            stat_ref[head : head + 1, :] = top
            stat_ref[GROUP_HEADS + head : GROUP_HEADS + head + 1, :] = total


def attend(slopes, queries, query_pos, key_pos, key_values, state, last):
    rows, length = queries.shape[0], key_pos.size
    vmem = pl.BlockSpec(memory_space=pltpu.VMEM)
    count = len(key_values)
    first = state is None
    state = () if first else state
    outs = [
        jax.ShapeDtypeStruct((GROUP_WIDTH, rows), F32),
        jax.ShapeDtypeStruct((GROUP_HEADS * (1 if last else 2), rows), F32),
    ]
    if last:
        outs.append(jax.ShapeDtypeStruct((rows, GROUP_WIDTH), BF16))
    return pl.pallas_call(
        functools.partial(attend_kernel, count, first, last),
        out_shape=tuple(outs),
        in_specs=[pl.BlockSpec(memory_space=pltpu.SMEM)] + [vmem] * (3 + count + len(state)),
        out_specs=(vmem,) * len(outs),
        scratch_shapes=[pltpu.VMEM((length, 1), F32)],
        compiler_params=pltpu.CompilerParams(vmem_limit_bytes=VMEM_BYTES),
        cost_estimate=pl.CostEstimate(
            flops=64 * rows * length * GROUP_WIDTH,
            bytes_accessed=rows * length,
            transcendentals=rows * length * GROUP_HEADS,
        ),
        name="attend",
    )(slopes, queries, query_pos, key_pos, *key_values, *state)


def attend_back_kernel(
    count, first, last, slopes_ref, q_ref, pq_ref, pk_ref, do_ref, out_ref, lse_ref, _, *refs
):
    kv_refs, refs = refs[:count], refs[count:]
    if not first:
        dq_in_ref, refs = refs[0], refs[1:]
    dq_ref, dkv_refs, column_ref = refs[0], refs[1 : count + 1], refs[-1]
    rows = q_ref.shape[0]
    query_pos = pq_ref[...]
    turn_positions(pk_ref, column_ref)
    for head in range(GROUP_HEADS):
        slope = slopes_ref[head]
        queries = q_ref[:, head_cols(head)]
        out_grads = do_ref[:, head_cols(head)]
        log_sum = lse_ref[head : head + 1, :]
        delta = jnp.sum(
            out_grads.astype(F32).T * out_ref[head_cols(head), :], axis=0, keepdims=True
        )
        if first:
            query_grads = jnp.zeros((HEAD_DIM, rows), F32)
        else:
            query_grads = dq_in_ref[head_cols(head), :]
        for (kv_ref, start), dkv_ref in zip(key_blocks(kv_refs), dkv_refs):

            def visit(block, query_grads, kv_ref=kv_ref, start=start, dkv_ref=dkv_ref):
                at = pl.ds(pl.multiple_of(block * KEY_BLOCK, KEY_BLOCK), KEY_BLOCK)
                pos_at = pl.ds(
                    pl.multiple_of(start + block * KEY_BLOCK, KEY_BLOCK), KEY_BLOCK
                )
                keys = kv_ref[at, head_cols(head)]
                values = kv_ref[at, head_cols(head, GROUP_WIDTH)]
                scores = log2_scores(keys, queries, slope, column_ref[pos_at, :], query_pos)
                probs = jnp.exp2(scores - log_sum)
                prob_grads = nt(values, out_grads)
                score_grads = (probs * (prob_grads - delta)).astype(BF16)
                dkv_ref[at, head_cols(head, GROUP_WIDTH)] = nn(
                    probs.astype(BF16), out_grads
                ).astype(BF16)
                dkv_ref[at, head_cols(head)] = (nn(score_grads, queries) * SCORE_SCALE).astype(
                    BF16
                )
                return query_grads + tn(keys, score_grads)

            query_grads = lax.fori_loop(0, kv_ref.shape[0] // KEY_BLOCK, visit, query_grads)
        if last:
            dq_ref[:, head_cols(head)] = (query_grads * SCORE_SCALE).T.astype(BF16)
        else:
            dq_ref[head_cols(head), :] = query_grads


def attend_back(
    slopes,
    queries,
    query_pos,
    key_pos,
    out_grads,
    attended,
    log_sums,
    key_values,
    state,
    last,
    earlier,
):
    rows, length = queries.shape[0], key_pos.size
    vmem = pl.BlockSpec(memory_space=pltpu.VMEM)
    count = len(key_values)
    first = state is None
    state = () if first else (state,)
    query_out = (
        jax.ShapeDtypeStruct((rows, GROUP_WIDTH), BF16)
        if last
        else jax.ShapeDtypeStruct((GROUP_WIDTH, rows), F32)
    )
    return pl.pallas_call(
        functools.partial(attend_back_kernel, count, first, last),
        out_shape=(query_out,)
        + tuple(jax.ShapeDtypeStruct(piece.shape, BF16) for piece in key_values),
        in_specs=[pl.BlockSpec(memory_space=pltpu.SMEM)]
        + [vmem] * 6
        + [pl.BlockSpec(memory_space=pl.ANY)]
        + [vmem] * (count + len(state)),
        out_specs=(vmem,) * (1 + count),
        scratch_shapes=[pltpu.VMEM((length, 1), F32)],
        compiler_params=pltpu.CompilerParams(vmem_limit_bytes=VMEM_BYTES),
        cost_estimate=pl.CostEstimate(
            flops=84 * rows * length * GROUP_WIDTH,
            bytes_accessed=rows * length,
            transcendentals=rows * length * GROUP_HEADS,
        ),
        name="attend_back",
    )(
        slopes,
        queries,
        query_pos,
        key_pos,
        out_grads,
        attended,
        log_sums,
        earlier,
        *key_values,
        *state,
    )


def assemble(core_ref, own_ref, swap_ref, columns, target, sems):
    core = core_ref[0]
    copies = []
    for which, (piece, half) in enumerate(((own_ref, core), (swap_ref, 1 - core))):
        copy = pltpu.make_async_copy(piece.at[:, columns], target.at[half], sems.at[which])
        copy.start()
        copies.append(copy)
    return copies


def first_norm_kernel(
    columns,
    core_ref,
    mixed_ref,
    rows_ref,
    vec_ref,
    own_ref,
    swap_ref,
    low_ref,
    hidden_ref,
    normal_ref,
    scale_ref,
    weight_ref,
    sems,
):
    for copy in assemble(core_ref, own_ref, swap_ref, columns, weight_ref, sems):
        copy.wait()
    mixed = mixed_ref[...]
    lin = jnp.concatenate([nn(mixed, weight_ref[0]), nn(mixed, weight_ref[1])], axis=1)
    total = rows_ref[...].astype(F32) + (lin + vec_ref[2:3, :])
    normal, scale = normalised(total)
    hidden = normal * vec_ref[3:4, :] + vec_ref[4:5, :]
    low_ref[...] = hidden.astype(BF16)
    hidden_ref[...] = hidden
    normal_ref[...] = normal
    scale_ref[...] = scale


def normalised(values):
    centred = values - jnp.mean(values, axis=1, keepdims=True)
    variance = jnp.mean(centred * centred, axis=1, keepdims=True)
    scale = lax.rsqrt(variance + EPSILON)
    return centred * scale, scale


def norm_back(grads, normal, scale, gain):
    scaled = grads * gain
    return (
        scaled
        - jnp.mean(scaled, axis=1, keepdims=True)
        - normal * jnp.mean(scaled * normal, axis=1, keepdims=True)
    ) * scale


def column_sum(values):
    return jnp.sum(values, axis=0, keepdims=True)


def first_norm(core, mixed, rows, vectors, own, swap, columns):
    tokens, width = mixed.shape
    vmem = pl.BlockSpec(memory_space=pltpu.VMEM)
    half = own.shape[1]
    return pl.pallas_call(
        functools.partial(first_norm_kernel, columns),
        out_shape=(
            jax.ShapeDtypeStruct((tokens, width), BF16),
            jax.ShapeDtypeStruct((tokens, width), F32),
            jax.ShapeDtypeStruct((tokens, width), F32),
            jax.ShapeDtypeStruct((tokens, 1), F32),
            jax.ShapeDtypeStruct((2, width, half), BF16),
        ),
        in_specs=[pl.BlockSpec(memory_space=pltpu.SMEM)]
        + [vmem] * 3
        + [pl.BlockSpec(memory_space=pl.ANY)] * 2,
        out_specs=(vmem,) * 5,
        scratch_shapes=[pltpu.SemaphoreType.DMA((2,))],
        compiler_params=pltpu.CompilerParams(vmem_limit_bytes=VMEM_BYTES),
        cost_estimate=pl.CostEstimate(
            flops=64 * tokens * width * width, bytes_accessed=4 * width * width, transcendentals=0
        ),
        name="first_norm",
    )(core, mixed, rows, vectors, own, swap)


def ff_forward_kernel(
    in_columns,
    out_columns,
    core_ref,
    hidden_ref,
    bias_ref,
    own_ref,
    swap_ref,
    act_ref,
    slope_ref,
    gelu_ref,
    parts_ref,
    w_in_ref,
    w_out_ref,
    sems,
):
    in_copies = assemble(core_ref, own_ref, swap_ref, in_columns, w_in_ref, sems.at[0])
    out_copies = assemble(core_ref, own_ref, swap_ref, out_columns, w_out_ref, sems.at[1])
    for copy in in_copies:
        copy.wait()
    tokens = hidden_ref.shape[0]

    def expand(tile, carry):
        at = pl.ds(pl.multiple_of(tile * FF_TILE, FF_TILE), FF_TILE)
        rows = hidden_ref[at, :]
        gate = nn(rows, w_in_ref[0]) + bias_ref[0:1, :]
        up = nn(rows, w_in_ref[1]) + bias_ref[1:2, :]
        cdf = 0.5 * (1.0 + lax.erf(gate * (0.5**0.5)))
        density = jnp.exp(-0.5 * gate * gate) * 0.3989422804014327
        gelu = gate * cdf
        act_ref[at, :] = (gelu * up).astype(BF16)
        gelu_ref[at, :] = gelu.astype(BF16)
        slope_ref[at, :] = (up * (cdf + gate * density)).astype(BF16)
        return carry

    lax.fori_loop(0, tokens // FF_TILE, expand, 0)
    for copy in out_copies:
        copy.wait()

    def contract(tile, carry):
        at = pl.ds(pl.multiple_of(tile * FF_TILE, FF_TILE), FF_TILE)
        rows = act_ref[at, :]
        parts_ref[at, :] = jnp.concatenate(
            [nn(rows, w_out_ref[0]), nn(rows, w_out_ref[1])], axis=1
        ).astype(BF16)
        return carry

    lax.fori_loop(0, tokens // FF_TILE, contract, 0)


def ff_forward(core, hidden, bias, own, swap, in_columns, out_columns):
    tokens, width = hidden.shape
    units = bias.shape[1]
    vmem = pl.BlockSpec(memory_space=pltpu.VMEM)
    return pl.pallas_call(
        functools.partial(ff_forward_kernel, in_columns, out_columns),
        out_shape=(
            jax.ShapeDtypeStruct((tokens, units), BF16),
            jax.ShapeDtypeStruct((tokens, units), BF16),
            jax.ShapeDtypeStruct((tokens, units), BF16),
            jax.ShapeDtypeStruct((tokens, width), BF16),
            jax.ShapeDtypeStruct((2, width, units), BF16),
            jax.ShapeDtypeStruct((2, units, width // 2), BF16),
        ),
        in_specs=[pl.BlockSpec(memory_space=pltpu.SMEM)]
        + [vmem] * 2
        + [pl.BlockSpec(memory_space=pl.ANY)] * 2,
        out_specs=(vmem,) * 6,
        scratch_shapes=[pltpu.SemaphoreType.DMA((2, 2))],
        compiler_params=pltpu.CompilerParams(vmem_limit_bytes=VMEM_BYTES),
        cost_estimate=pl.CostEstimate(
            flops=32 * tokens * width * units,
            bytes_accessed=6 * width * units,
            transcendentals=2 * tokens * units,
        ),
        name="ff_forward",
    )(core, hidden, bias, own, swap)


def second_norm_kernel(
    parts_ref, hidden_ref, cotangent_ref, vec_ref, result_ref, grad_ref, low_ref, sums_ref
):
    lin = jnp.sum(parts_ref[...].astype(F32), axis=0) + vec_ref[5:6, :]
    normal, scale = normalised(hidden_ref[...] + lin)
    gain = vec_ref[6:7, :]
    result_ref[...] = (normal * gain + vec_ref[7:8, :]).astype(BF16)
    grads = cotangent_ref[...].astype(F32)
    back = norm_back(grads, normal, scale, gain)
    low = back.astype(BF16)
    grad_ref[...] = back
    low_ref[...] = low
    sums_ref[...] = jnp.concatenate(
        [
            column_sum(low.astype(F32)),
            column_sum(grads * normal),
            column_sum(grads),
            jnp.zeros((5, back.shape[1]), F32),
        ]
    )


def second_norm(parts, hidden, cotangent, vectors):
    tokens, width = hidden.shape
    vmem = pl.BlockSpec(memory_space=pltpu.VMEM)
    return pl.pallas_call(
        second_norm_kernel,
        out_shape=(
            jax.ShapeDtypeStruct((tokens, width), BF16),
            jax.ShapeDtypeStruct((tokens, width), F32),
            jax.ShapeDtypeStruct((tokens, width), BF16),
            jax.ShapeDtypeStruct((8, width), F32),
        ),
        in_specs=[vmem] * 4,
        out_specs=(vmem,) * 4,
        compiler_params=pltpu.CompilerParams(vmem_limit_bytes=VMEM_BYTES),
        cost_estimate=pl.CostEstimate(
            flops=20000 * tokens * width, bytes_accessed=20 * tokens * width, transcendentals=0
        ),
        name="second_norm",
    )(parts, hidden, cotangent, vectors)


def ff_backward_kernel(
    grad_ref, slope_ref, gelu_ref, w_in_ref, w_out_ref, joined_ref, parts_ref, bias_ref, half_ref
):
    tokens, width = grad_ref.shape
    half = width // 2
    bias_ref[...] = jnp.zeros_like(bias_ref)

    def visit(tile, carry):
        at = pl.ds(pl.multiple_of(tile * FF_TILE, FF_TILE), FF_TILE)
        left, right = grad_ref[at, :half], grad_ref[at, half:]
        half_ref[0, at, :] = left
        half_ref[1, at, :] = right
        act_grad = nt(left, w_out_ref[0]) + nt(right, w_out_ref[1])
        for which, factor in ((0, slope_ref), (1, gelu_ref)):
            joined = (act_grad * factor[at, :].astype(F32)).astype(BF16)
            joined_ref[which, at, :] = joined
            bias_ref[which : which + 1, :] += column_sum(joined.astype(F32))
        parts_ref[at, :] = (
            nt(joined_ref[0, at, :], w_in_ref[0]) + nt(joined_ref[1, at, :], w_in_ref[1])
        ).astype(BF16)
        return carry

    lax.fori_loop(0, tokens // FF_TILE, visit, 0)


def ff_backward(grads, slope, gelu, w_in, w_out):
    tokens, width = grads.shape
    units = slope.shape[1]
    vmem = pl.BlockSpec(memory_space=pltpu.VMEM)
    return pl.pallas_call(
        ff_backward_kernel,
        out_shape=(
            jax.ShapeDtypeStruct((2, tokens, units), BF16),
            jax.ShapeDtypeStruct((tokens, width), BF16),
            jax.ShapeDtypeStruct((2, units), F32),
            jax.ShapeDtypeStruct((2, tokens, width // 2), BF16),
        ),
        in_specs=[vmem] * 5,
        out_specs=(vmem,) * 4,
        compiler_params=pltpu.CompilerParams(vmem_limit_bytes=VMEM_BYTES),
        cost_estimate=pl.CostEstimate(
            flops=32 * tokens * width * units,
            bytes_accessed=6 * width * units,
            transcendentals=0,
        ),
        name="ff_backward",
    )(grads, slope, gelu, w_in, w_out)


def first_back_kernel(
    parts_ref,
    second_ref,
    normal_ref,
    scale_ref,
    vec_ref,
    weight_ref,
    sums_ref,
    _,
    __,
    grad_ref,
    low_ref,
    out_ref,
    turned_ref,
):
    tokens, width = second_ref.shape
    half, count = width // 2, tokens // 2
    normal = normal_ref[...]
    grads = second_ref[...] + jnp.sum(parts_ref[...].astype(F32), axis=0)
    back = norm_back(grads, normal, scale_ref[...], vec_ref[3:4, :])
    low = back.astype(BF16)
    grad_ref[...] = back
    low_ref[0] = low[:, :half]
    low_ref[1] = low[:, half:]
    out_grad = nt(low[:, :half], weight_ref[0]) + nt(low[:, half:], weight_ref[1])
    for seq in range(2):
        for group in range(GROUPS):
            out_ref[seq * GROUPS + group] = out_grad[
                seq * count : (seq + 1) * count, group * GROUP_WIDTH : (group + 1) * GROUP_WIDTH
            ].astype(BF16)
    rows = jnp.concatenate(
        [
            column_sum(low.astype(F32)),
            column_sum(grads * normal),
            column_sum(grads),
            sums_ref[0:3, :],
            jnp.zeros((122, width), F32),
        ]
    )
    turned_ref[...] = rows.T.astype(BF16)


def first_back(parts, second_grad, normal, scale, vectors, weight, sums, *earlier):
    tokens, width = second_grad.shape
    vmem = pl.BlockSpec(memory_space=pltpu.VMEM)
    return pl.pallas_call(
        first_back_kernel,
        out_shape=(
            jax.ShapeDtypeStruct((tokens, width), F32),
            jax.ShapeDtypeStruct((2, tokens, width // 2), BF16),
            jax.ShapeDtypeStruct((2 * GROUPS, tokens // 2, GROUP_WIDTH), BF16),
            jax.ShapeDtypeStruct((width, 128), BF16),
        ),
        in_specs=[vmem] * 7 + [pl.BlockSpec(memory_space=pl.ANY)] * 2,
        out_specs=(vmem,) * 4,
        compiler_params=pltpu.CompilerParams(vmem_limit_bytes=VMEM_BYTES),
        cost_estimate=pl.CostEstimate(
            flops=64 * tokens * width * width, bytes_accessed=4 * width * width, transcendentals=0
        ),
        name="first_back",
    )(parts, second_grad, normal, scale, vectors, weight, sums, *earlier)


def swap_sum(keep, give, axis):
    return keep.astype(F32) + lax.ppermute(give.astype(BF16), axis, SWAP).astype(F32)


def gather_plane(block):
    return lax.all_gather(block, PLANE, axis=0, tiled=True)


def spread_plane(parts):
    return lax.all_to_all(parts.reshape(4, -1, parts.shape[1]), PLANE, 0, 0, tiled=True)


def after(array, earlier):
    first = earlier[(slice(0, 1),) * earlier.ndim].reshape((1,) * array.ndim)
    return array + (first.astype(F32) * 0.0).astype(array.dtype)


def hold_kernel(*refs):
    del refs


def hold(array, earlier):
    anywhere = pl.BlockSpec(memory_space=pl.ANY)
    return pl.pallas_call(
        hold_kernel,
        out_shape=jax.ShapeDtypeStruct(array.shape, array.dtype),
        in_specs=[anywhere] * 2,
        out_specs=anywhere,
        input_output_aliases={0: 0},
        name="hold",
    )(array, earlier)


def pick(parts, index):
    return lax.dynamic_index_in_dim(parts, index, 0, keepdims=False)


def two(own, other, index):
    return jnp.where(index == 0, jnp.stack([own, other]), jnp.stack([other, own]))


def body(
    tokens,
    positions,
    w_qkv,
    qv_bias,
    w_attn_out,
    attn_out_bias,
    norm1_gain,
    norm1_bias,
    w_in,
    in_bias,
    w_out,
    out_bias,
    norm2_gain,
    norm2_bias,
    cotangent,
):
    seq_count, row_count, width = tokens.shape
    outer = lax.axis_size("e")
    seq_size = 2 * outer * GROUPS
    devices = seq_size * 4
    shard = w_qkv.shape[0]
    ff_shard = w_out.shape[0]
    ring = 4 * outer
    group = lax.axis_index(("r", "x"))
    place = lax.axis_index(("y", "c"))
    units = 2 * ring * ff_shard
    y_at, c_at = lax.axis_index("y"), lax.axis_index("c")
    qkv_cols = 3 * GROUP_WIDTH

    with jax.named_scope("gather_qkv_weights"):
        own_pos = lax.dynamic_slice_in_dim(positions, place * row_count, row_count, 1)
        shorts = jnp.stack(
            [
                qv_bias[0],
                qv_bias[1],
                attn_out_bias,
                norm1_gain,
                norm1_bias,
                out_bias,
                norm2_gain,
                norm2_bias,
            ]
        )
        wide = -(-qkv_cols // 128) * 128
        longs = jnp.concatenate(
            [
                jnp.pad(own_pos >> 7, ((0, 0), (0, wide - 128 - row_count))).astype(BF16)[:, None],
                jnp.pad(own_pos & 127, ((0, 0), (0, wide - 128 - row_count))).astype(BF16)[:, None],
                jnp.broadcast_to(
                    jnp.pad(in_bias, (0, wide - 128 - 2 * ff_shard)), (2, 1, wide - 128)
                ),
                jnp.zeros((2, 5, wide - 128), BF16),
            ],
            axis=1,
        )
        smalls = jnp.concatenate(
            [jnp.broadcast_to(jnp.pad(shorts, ((0, 0), (0, 128 - shard))), (2, 8, 128)), longs],
            axis=2,
        )
        columns = (
            w_qkv.reshape(shard, 3, GROUPS, GROUP_WIDTH)
            .transpose(2, 0, 1, 3)
            .reshape(1, GROUPS, shard, qkv_cols)
        )
        columns = jnp.pad(columns, ((0, 0), (0, 0), (0, 0), (0, wide - qkv_cols)))
        parcel = jnp.concatenate(
            [
                jnp.broadcast_to(columns, (2, GROUPS, shard, wide)),
                jnp.broadcast_to(smalls[:, None], (2, GROUPS, 8, wide)),
            ],
            axis=2,
        ).reshape(8, shard + 8, wide)
        parcel = lax.all_to_all(parcel, SEQ_GROUP, 0, 0, tiled=True)

    with jax.named_scope("gather_tokens"):
        s_at, r_at, x_at = (lax.axis_index(name) for name in SEQ_GROUP)
        chunk = two(
            pick(tokens, s_at), lax.ppermute(pick(tokens, 1 - s_at), "s", SWAP), s_at
        )
        chunk = after(chunk, parcel)
        chunk = two(chunk, lax.ppermute(chunk, "r", SWAP), r_at)
        chunk = two(chunk, lax.ppermute(chunk, "x", SWAP), x_at)
        chunk = chunk.transpose(2, 1, 0, 3, 4).reshape(8 * row_count, width)

    with jax.named_scope("gather_qkv_weights"):
        sent = parcel
        parcel = two(parcel, lax.ppermute(parcel, "y", SWAP), y_at)
        parcel = two(parcel, lax.ppermute(parcel, "c", SWAP), c_at)
        parcels = parcel[None]
        if outer > 1:
            parcels = lax.all_gather(parcel, "e", axis=0, tiled=False)
        parcels = parcels.reshape(outer, 2, 2, 2, 2, 2, shard + 8, wide)
        order = (3, 0, 4, 5, 2, 1)
        qkv_slice = (
            parcels[..., :shard, :qkv_cols].transpose(*order, 6, 7).reshape(width, qkv_cols)
        )
        vectors = (
            parcels[..., shard:, :shard].transpose(6, *order, 7).reshape(8, width).astype(F32)
        )
        pos_parts = parcels[..., shard : shard + 2, 128 : 128 + row_count].astype(F32)
        chunk_pos = (pos_parts[..., 0, :] * 128.0 + pos_parts[..., 1, :]).reshape(
            outer, 2, 2, 8 * row_count
        )
        in_shift = lax.dynamic_index_in_dim(
            lax.dynamic_index_in_dim(
                parcels[..., shard + 2, 128 : 128 + 2 * ff_shard], y_at, 1, keepdims=False
            ),
            x_at,
            1,
            keepdims=False,
        )
        in_shift = (
            in_shift.transpose(1, 0, 2, 3, 4).reshape(2, units).astype(F32)
        )

    with jax.named_scope("gather_ff_weights"):
        half = width // 2
        in_cols = (
            w_in.reshape(shard, 2, ring, 4, 2 * ff_shard)
            .transpose(3, 1, 0, 2, 4)
            .reshape(4, 2, shard, units)
        )
        attn_cols = w_attn_out.reshape(shard, 2, half).transpose(1, 0, 2)
        in_parts = jnp.concatenate(
            [in_cols, jnp.broadcast_to(attn_cols, (4, 2, shard, half))], axis=3
        ).reshape(8, shard, units + half)
        in_parts = lax.all_to_all(after(in_parts, sent), ("x", "y", "c"), 0, 0, tiled=True)
        out_halves = w_out.reshape(ff_shard, 2, half).transpose(1, 0, 2)
        out_cols = two(
            pick(out_halves, c_at), lax.ppermute(pick(out_halves, 1 - c_at), "c", SWAP), c_at
        ).reshape(2 * ff_shard, half)
        packed = jnp.concatenate(
            [in_parts.reshape(8 * shard, units + half), out_cols], axis=1
        )
        packed = lax.all_gather(packed, RING, axis=0, tiled=True)
        core = c_at.reshape(1).astype(jnp.int32)

    with jax.named_scope("project"):
        qv_slice = lax.dynamic_slice_in_dim(vectors[:2], group * GROUP_WIDTH, GROUP_WIDTH, 1)
        column_bias = jnp.concatenate(
            [qv_slice[0], jnp.zeros((GROUP_WIDTH,), F32), qv_slice[1]]
        )
        turned_chunk = (
            chunk.reshape(8 * row_count, seq_size, 2, 2, shard)
            .transpose(0, 3, 2, 1, 4)
            .reshape(8 * row_count, width)
        )
        queries = (
            jnp.dot(chunk, qkv_slice[:, :GROUP_WIDTH], preferred_element_type=F32)
            + column_bias[:GROUP_WIDTH]
        ).astype(BF16)
        own_kv = (
            jnp.dot(chunk, qkv_slice[:, GROUP_WIDTH:], preferred_element_type=F32)
            + column_bias[GROUP_WIDTH:]
        ).astype(BF16)
    with jax.named_scope("gather_kv"):
        if outer > 1:
            own_kv = lax.all_gather(own_kv, "e", axis=0, tiled=True)
        y_kv = lax.ppermute(own_kv, "y", SWAP)
        key_values = [
            own_kv,
            lax.ppermute(own_kv, "c", SWAP),
            y_kv,
            lax.ppermute(y_kv, "c", SWAP),
        ]
    ordered_pos = jnp.stack(
        [
            lax.dynamic_index_in_dim(
                lax.dynamic_index_in_dim(chunk_pos, c_at ^ kc, 1, keepdims=False),
                y_at ^ ky,
                1,
                keepdims=False,
            )
            for ky in (0, 1)
            for kc in (0, 1)
        ]
    )
    query_pos = lax.dynamic_index_in_dim(ordered_pos[0], lax.axis_index("e"), 0, keepdims=True)
    key_pos = ordered_pos.reshape(4 * outer, 8 * row_count)
    head_ids = group * GROUP_HEADS + jnp.arange(GROUP_HEADS)
    slopes = 2.0 ** (-8.0 * (head_ids + 1).astype(F32) / HEADS) * LOG2E

    with jax.named_scope("attention"):
        near = 2 * outer
        state = attend(
            slopes, queries, query_pos, key_pos[:near], key_values[:2], None, last=False
        )
        attended, log_sums, attended_low = attend(
            slopes, queries, query_pos, key_pos[near:], key_values[2:], state, last=True
        )

    with jax.named_scope("return_attended"):
        returned = lax.all_to_all(
            attended_low.reshape(8, row_count, GROUP_WIDTH), SEQ_GROUP, 0, 0, tiled=True
        )
        mixed = (
            returned.reshape(2, GROUPS, row_count, GROUP_WIDTH)
            .transpose(0, 2, 1, 3)
            .reshape(2 * row_count, width)
        )
    with jax.named_scope("first_norm"):
        packed = hold(packed, mixed)
        attn_own = packed[:, units : units + half]
        attn_swap = lax.ppermute(attn_own, "c", SWAP)
        hidden_low, hidden, normal, scale, attn_full = first_norm(
            core,
            mixed,
            tokens.reshape(2 * row_count, width),
            vectors,
            attn_own,
            attn_swap,
            slice(None),
        )
        swapped = lax.ppermute(hold(packed, hidden_low), "c", SWAP)
    with jax.named_scope("gather_hidden"):
        hidden_group = gather_plane(hidden_low)
    with jax.named_scope("ff_forward"):
        activated_low, slope, gelu, ff_parts, in_slice, out_slice = ff_forward(
            core,
            hidden_group,
            in_shift,
            packed,
            swapped,
            slice(0, units),
            slice(units + half, units + width),
        )
    with jax.named_scope("sum_ff"):
        ff_parts = spread_plane(ff_parts)
    with jax.named_scope("second_norm"):
        result, second_grad, ff_grad, sums = second_norm(
            ff_parts, hidden, cotangent.reshape(2 * row_count, width), vectors
        )
    with jax.named_scope("gather_ff_grad"):
        ff_grads = gather_plane(ff_grad)
    with jax.named_scope("ff_backward"):
        joined_grad, hidden_parts, grad_in_shift, grad_halves = ff_backward(
            ff_grads, slope, gelu, in_slice, out_slice
        )
    with jax.named_scope("sum_hidden_grad"):
        hidden_parts = spread_plane(hidden_parts)
    with jax.named_scope("ff_weight_grads"):
        in_rows = swap_sum(
            tn(hidden_group, pick(joined_grad, c_at)),
            tn(hidden_group, pick(joined_grad, 1 - c_at)),
            "c",
        ).astype(BF16)
        out_rows = swap_sum(
            tn(activated_low, pick(grad_halves, c_at)),
            tn(activated_low, pick(grad_halves, 1 - c_at)),
            "c",
        ).astype(BF16)
        grad_in_rows = lax.psum_scatter(in_rows, RING, scatter_dimension=0, tiled=True)
        grad_out_rows = lax.psum_scatter(
            hold(out_rows, in_rows), RING, scatter_dimension=0, tiled=True
        ).reshape(2, ff_shard, half)
        grad_w_out = (
            two(
                pick(grad_out_rows, c_at),
                lax.ppermute(pick(grad_out_rows, 1 - c_at), "c", SWAP),
                c_at,
            )
            .transpose(1, 0, 2)
            .reshape(ff_shard, width)
            .astype(F32)
        )
        grad_in_rows = lax.all_to_all(
            grad_in_rows.reshape(8, shard, -1), ("x", "y", "c"), 0, 0, tiled=True
        )
        grad_w_in = (
            grad_in_rows.reshape(4, 2, shard, ring, 2 * ff_shard)
            .transpose(2, 1, 3, 0, 4)
            .reshape(shard, 2 * devices * ff_shard)
            .astype(F32)
        )
    with jax.named_scope("first_norm_back"):
        first_grad, attn_grad, out_grad, turned = first_back(
            hidden_parts,
            second_grad,
            normal,
            scale,
            vectors,
            attn_full,
            sums,
            in_rows,
            out_rows,
        )
    with jax.named_scope("send_out_grad"):
        out_grads = lax.all_to_all(
            out_grad,
            SEQ_GROUP,
            0,
            0,
            tiled=True,
        ).reshape(8 * row_count, GROUP_WIDTH)
    with jax.named_scope("attn_weight_grad"):
        give = jnp.concatenate(
            [tn(mixed, pick(attn_grad, 1 - c_at)).astype(BF16), turned], axis=1
        )
        keep = jnp.concatenate([tn(mixed, pick(attn_grad, c_at)), turned.astype(F32)], axis=1)
        attn_rows = swap_sum(keep, give, "c").astype(BF16)
        rows_out = lax.psum_scatter(attn_rows, RING, scatter_dimension=0, tiled=True)
        rows_out = rows_out.reshape(4, 2, shard, -1).transpose(1, 0, 2, 3)
        rows_out = two(
            pick(rows_out, c_at), lax.ppermute(pick(rows_out, 1 - c_at), "c", SWAP), c_at
        ).reshape(2, 2, 2, shard, -1)
        rows_out = swap_sum(
            lax.dynamic_index_in_dim(rows_out, y_at, 2, keepdims=False),
            lax.dynamic_index_in_dim(rows_out, 1 - y_at, 2, keepdims=False),
            "y",
        )
        rows_out = swap_sum(
            lax.dynamic_index_in_dim(rows_out, x_at, 1, keepdims=False),
            lax.dynamic_index_in_dim(rows_out, 1 - x_at, 1, keepdims=False),
            "x",
        )
        grad_w_attn = rows_out[..., :half].transpose(1, 0, 2).reshape(shard, width)
        vector_grads = rows_out[0, :, half : half + 8].T

    with jax.named_scope("attention_back"):
        state, y_part, cy_part = attend_back(
            slopes,
            queries,
            query_pos,
            key_pos[near:],
            out_grads,
            attended,
            log_sums,
            key_values[2:],
            None,
            last=False,
            earlier=attn_rows,
        )
        y_sum = swap_sum(y_part, cy_part, "c").astype(BF16)
        query_grads, own_part, c_part = attend_back(
            slopes,
            queries,
            query_pos,
            key_pos[:near],
            out_grads,
            attended,
            log_sums,
            key_values[:2],
            state,
            last=True,
            earlier=y_sum,
        )
    with jax.named_scope("sum_kv_grads"):
        kv_grads = swap_sum(swap_sum(own_part, c_part, "c"), y_sum, "y")
        if outer > 1:
            kv_grads = lax.psum_scatter(kv_grads, "e", scatter_dimension=0, tiled=True)
        qkv_grad = jnp.concatenate([query_grads, kv_grads.astype(BF16)], axis=1)

    with jax.named_scope("input_grad"):
        input_parts = nt(qkv_grad, qkv_slice).astype(BF16).reshape(8, row_count, width)
        input_parts = lax.all_to_all(input_parts, SEQ_GROUP, 0, 0, tiled=True)
        input_grad = first_grad.reshape(2, row_count, width) + jnp.sum(
            input_parts.reshape(2, GROUPS, row_count, width).astype(F32), axis=1
        )
    with jax.named_scope("qkv_weight_grad"):
        blocks = tn(turned_chunk, qkv_grad).reshape(2, 2, seq_size, shard, qkv_cols)
        column_sums = jnp.sum(qkv_grad.astype(F32), axis=0)
        rows_at = jnp.arange(8)[None, None, None, :, None]
        here = (jnp.arange(2)[:, None] == y_at) & (jnp.arange(2)[None, :] == x_at)
        shifts = jnp.pad(grad_in_shift.reshape(seq_size, 2 * ff_shard), ((0, 0), (0, qkv_cols - 2 * ff_shard)))
        smalls = jnp.where(
            rows_at == 0,
            column_sums[None, None, None, None, :],
            jnp.where(
                (rows_at == 1) & here[:, :, None, None, None], shifts[None, None, :, None, :], 0.0
            ),
        )
        bundle = jnp.concatenate([blocks, smalls], axis=3)
        bundle = swap_sum(pick(bundle, c_at), pick(bundle, 1 - c_at), "c")
        bundle = swap_sum(pick(bundle, y_at), pick(bundle, 1 - y_at), "y")
        shares = lax.all_to_all(bundle.astype(BF16), SEQ_AXIS, 0, 0, tiled=True).astype(F32)
        totals = jnp.sum(shares.reshape(2 * outer, GROUPS, shard + 8, qkv_cols), axis=0)
        grad_w_qkv = (
            totals[:, :shard]
            .reshape(GROUPS, shard, 3, GROUP_WIDTH)
            .transpose(1, 2, 0, 3)
            .reshape(shard, 3 * width)
        )
        sums = totals[:, shard].reshape(GROUPS, 3, GROUP_WIDTH).transpose(1, 0, 2).reshape(3, width)
        grad_qv = lax.dynamic_slice_in_dim(sums[0::2], lax.axis_index(EVERY) * shard, shard, 1)
        grad_in_bias = jnp.sum(totals[:, shard + 1, : 2 * ff_shard], axis=0)

    return (
        result.reshape(2, row_count, width).astype(BF16),
        input_grad,
        grad_w_qkv,
        grad_qv,
        grad_w_attn,
        vector_grads[0],
        vector_grads[1],
        vector_grads[2],
        grad_w_in,
        grad_in_bias,
        grad_w_out,
        vector_grads[3],
        vector_grads[4],
        vector_grads[5],
    )


def solution(mesh):
    seq_size = mesh.shape["seq"]
    split = Mesh(mesh.devices.reshape(2, seq_size // 8, 2, 2, 2, 2), EVERY)
    tokens_at = P(None, EVERY, None)
    rows_at = P(EVERY, None)
    vector_at = P(EVERY)
    return jax.shard_map(
        body,
        mesh=split,
        in_specs=(
            tokens_at,
            P(None, SEQ_AXIS),
            rows_at,
            P(None, EVERY),
            rows_at,
            vector_at,
            vector_at,
            vector_at,
            rows_at,
            vector_at,
            rows_at,
            vector_at,
            vector_at,
            vector_at,
            tokens_at,
        ),
        out_specs=(
            tokens_at,
            tokens_at,
            rows_at,
            P(None, EVERY),
            rows_at,
            vector_at,
            vector_at,
            vector_at,
            rows_at,
            vector_at,
            rows_at,
            vector_at,
            vector_at,
            vector_at,
        ),
        check_vma=False,
    )
```

```python
import functools

import jax
import jax.numpy as jnp
from jax import lax
from jax.experimental import pallas as pl
from jax.experimental.pallas import tpu as pltpu
from jax.sharding import Mesh
from jax.sharding import PartitionSpec as P

HEADS = 12
HEAD_DIM = 64
GROUPS = 4
GROUP_HEADS = HEADS // GROUPS
GROUP_WIDTH = GROUP_HEADS * HEAD_DIM
EPSILON = 1e-12
SCORE_SCALE = 0.125
LOG2E = 1.4426950408889634
LOWEST = -1e30
KEY_BLOCK = 512
FF_TILE = 256
SEQ_GROUP = ("s", "r", "x")
CHUNKS = ("e", "y", "c")
RING = ("s", "e", "r")
PLANE = ("x", "y")
SEQ_AXIS = ("s", "e", "r", "x")
EVERY = ("s", "e", "r", "x", "y", "c")
SWAP = ((0, 1), (1, 0))
BF16 = jnp.bfloat16
F32 = jnp.float32
VMEM_BYTES = 60 * 2**20


def nt(a, b):
    return lax.dot_general(a, b, (((1,), (1,)), ((), ())), preferred_element_type=F32)


def tn(a, b):
    return lax.dot_general(a, b, (((0,), (0,)), ((), ())), preferred_element_type=F32)


def nn(a, b):
    return lax.dot_general(a, b, (((1,), (0,)), ((), ())), preferred_element_type=F32)


def head_cols(head, base=0):
    return slice(base + head * HEAD_DIM, base + (head + 1) * HEAD_DIM)


def log2_scores(keys, queries, slope, key_pos, query_pos):
    products = nt(keys, queries)
    distances = jnp.abs(key_pos * slope - query_pos * slope)
    return products * (SCORE_SCALE * LOG2E) - distances


def column(row):
    return jnp.broadcast_to(row, (8, row.shape[1])).T[:, :1]


def key_blocks(kv_refs):
    start = 0
    for piece in kv_refs:
        yield piece, start
        start += piece.shape[0]


def turn_positions(pk_ref, column_ref):
    def turn(block, carry):
        at = pl.ds(pl.multiple_of(block * KEY_BLOCK, KEY_BLOCK), KEY_BLOCK)
        column_ref[at, :] = column(pk_ref[pl.ds(block, 1), :])
        return carry

    lax.fori_loop(0, pk_ref.shape[0], turn, 0)


def attend_kernel(deps, count, first, last, slopes_ref, q_ref, pq_ref, pk_ref, *refs):
    refs = refs[deps:]
    kv_refs, refs = refs[:count], refs[count:]
    if not first:
        (sum_in_ref, stat_in_ref), refs = refs[:2], refs[2:]
    sum_ref, stat_ref = refs[:2]
    column_ref = refs[-1]
    rows = q_ref.shape[0]
    query_pos = pq_ref[...]
    turn_positions(pk_ref, column_ref)
    for head in range(GROUP_HEADS):
        slope = slopes_ref[head]
        queries = q_ref[:, head_cols(head)]
        if first:
            carry = (
                jnp.full((1, rows), LOWEST, F32),
                jnp.zeros((1, rows), F32),
                jnp.zeros((HEAD_DIM, rows), F32),
            )
        else:
            carry = (
                stat_in_ref[head : head + 1, :],
                stat_in_ref[GROUP_HEADS + head : GROUP_HEADS + head + 1, :],
                sum_in_ref[head_cols(head), :],
            )
        for kv_ref, start in key_blocks(kv_refs):

            def visit(block, carry, kv_ref=kv_ref, start=start):
                top, total, summed = carry
                at = pl.ds(pl.multiple_of(block * KEY_BLOCK, KEY_BLOCK), KEY_BLOCK)
                pos_at = pl.ds(
                    pl.multiple_of(start + block * KEY_BLOCK, KEY_BLOCK), KEY_BLOCK
                )
                keys = kv_ref[at, head_cols(head)]
                values = kv_ref[at, head_cols(head, GROUP_WIDTH)]
                scores = log2_scores(keys, queries, slope, column_ref[pos_at, :], query_pos)
                new_top = jnp.maximum(top, jnp.max(scores, axis=0, keepdims=True))
                weights = jnp.exp2(scores - new_top)
                shrink = jnp.exp2(top - new_top)
                total = total * shrink + jnp.sum(weights, axis=0, keepdims=True)
                summed = summed * shrink + tn(values, weights.astype(BF16))
                return new_top, total, summed

            carry = lax.fori_loop(0, kv_ref.shape[0] // KEY_BLOCK, visit, carry)
        top, total, summed = carry
        if last:
            attended = summed / total
            sum_ref[head_cols(head), :] = attended
            refs[2][:, head_cols(head)] = attended.T.astype(BF16)
            stat_ref[head : head + 1, :] = top + jnp.log2(total)
        else:
            sum_ref[head_cols(head), :] = summed
            stat_ref[head : head + 1, :] = top
            stat_ref[GROUP_HEADS + head : GROUP_HEADS + head + 1, :] = total


def attend(slopes, queries, query_pos, key_pos, key_values, state, last, earlier):
    rows, length = queries.shape[0], key_pos.size
    vmem = pl.BlockSpec(memory_space=pltpu.VMEM)
    count = len(key_values)
    first = state is None
    state = () if first else state
    outs = [
        jax.ShapeDtypeStruct((GROUP_WIDTH, rows), F32),
        jax.ShapeDtypeStruct((GROUP_HEADS * (1 if last else 2), rows), F32),
    ]
    if last:
        outs.append(jax.ShapeDtypeStruct((rows, GROUP_WIDTH), BF16))
    return pl.pallas_call(
        functools.partial(attend_kernel, len(earlier), count, first, last),
        out_shape=tuple(outs),
        in_specs=[pl.BlockSpec(memory_space=pltpu.SMEM)]
        + [vmem] * 3
        + [pl.BlockSpec(memory_space=pl.ANY)] * len(earlier)
        + [vmem] * (count + len(state)),
        out_specs=(vmem,) * len(outs),
        scratch_shapes=[pltpu.VMEM((length, 1), F32)],
        compiler_params=pltpu.CompilerParams(vmem_limit_bytes=VMEM_BYTES),
        cost_estimate=pl.CostEstimate(
            flops=64 * rows * length * GROUP_WIDTH,
            bytes_accessed=rows * length,
            transcendentals=rows * length * GROUP_HEADS,
        ),
        name="attend",
    )(slopes, queries, query_pos, key_pos, *earlier, *key_values, *state)


def attend_back_kernel(
    deps, count, first, last, slopes_ref, q_ref, pq_ref, pk_ref, do_ref, out_ref, lse_ref, *refs
):
    refs = refs[deps:]
    kv_refs, refs = refs[:count], refs[count:]
    if not first:
        dq_in_ref, refs = refs[0], refs[1:]
    dq_ref, dkv_refs, column_ref = refs[0], refs[1 : count + 1], refs[-1]
    rows = q_ref.shape[0]
    query_pos = pq_ref[...]
    turn_positions(pk_ref, column_ref)
    for head in range(GROUP_HEADS):
        slope = slopes_ref[head]
        queries = q_ref[:, head_cols(head)]
        out_grads = do_ref[:, head_cols(head)]
        log_sum = lse_ref[head : head + 1, :]
        delta = jnp.sum(
            out_grads.astype(F32).T * out_ref[head_cols(head), :], axis=0, keepdims=True
        )
        if first:
            query_grads = jnp.zeros((HEAD_DIM, rows), F32)
        else:
            query_grads = dq_in_ref[head_cols(head), :]
        for (kv_ref, start), dkv_ref in zip(key_blocks(kv_refs), dkv_refs):

            def visit(block, query_grads, kv_ref=kv_ref, start=start, dkv_ref=dkv_ref):
                at = pl.ds(pl.multiple_of(block * KEY_BLOCK, KEY_BLOCK), KEY_BLOCK)
                pos_at = pl.ds(
                    pl.multiple_of(start + block * KEY_BLOCK, KEY_BLOCK), KEY_BLOCK
                )
                keys = kv_ref[at, head_cols(head)]
                values = kv_ref[at, head_cols(head, GROUP_WIDTH)]
                scores = log2_scores(keys, queries, slope, column_ref[pos_at, :], query_pos)
                probs = jnp.exp2(scores - log_sum)
                prob_grads = nt(values, out_grads)
                score_grads = (probs * (prob_grads - delta)).astype(BF16)
                dkv_ref[at, head_cols(head, GROUP_WIDTH)] = nn(
                    probs.astype(BF16), out_grads
                ).astype(BF16)
                dkv_ref[at, head_cols(head)] = (nn(score_grads, queries) * SCORE_SCALE).astype(
                    BF16
                )
                return query_grads + tn(keys, score_grads)

            query_grads = lax.fori_loop(0, kv_ref.shape[0] // KEY_BLOCK, visit, query_grads)
        if last:
            dq_ref[:, head_cols(head)] = (query_grads * SCORE_SCALE).T.astype(BF16)
        else:
            dq_ref[head_cols(head), :] = query_grads


def attend_back(
    slopes,
    queries,
    query_pos,
    key_pos,
    out_grads,
    attended,
    log_sums,
    key_values,
    state,
    last,
    earlier,
):
    rows, length = queries.shape[0], key_pos.size
    vmem = pl.BlockSpec(memory_space=pltpu.VMEM)
    count = len(key_values)
    first = state is None
    state = () if first else (state,)
    query_out = (
        jax.ShapeDtypeStruct((rows, GROUP_WIDTH), BF16)
        if last
        else jax.ShapeDtypeStruct((GROUP_WIDTH, rows), F32)
    )
    return pl.pallas_call(
        functools.partial(attend_back_kernel, len(earlier), count, first, last),
        out_shape=(query_out,)
        + tuple(jax.ShapeDtypeStruct(piece.shape, BF16) for piece in key_values),
        in_specs=[pl.BlockSpec(memory_space=pltpu.SMEM)]
        + [vmem] * 6
        + [pl.BlockSpec(memory_space=pl.ANY)] * len(earlier)
        + [vmem] * (count + len(state)),
        out_specs=(vmem,) * (1 + count),
        scratch_shapes=[pltpu.VMEM((length, 1), F32)],
        compiler_params=pltpu.CompilerParams(vmem_limit_bytes=VMEM_BYTES),
        cost_estimate=pl.CostEstimate(
            flops=84 * rows * length * GROUP_WIDTH,
            bytes_accessed=rows * length,
            transcendentals=rows * length * GROUP_HEADS,
        ),
        name="attend_back",
    )(
        slopes,
        queries,
        query_pos,
        key_pos,
        out_grads,
        attended,
        log_sums,
        *earlier,
        *key_values,
        *state,
    )


def assemble(core_ref, own_ref, swap_ref, columns, target, sems):
    core = core_ref[0]
    copies = []
    for which, (piece, half) in enumerate(((own_ref, core), (swap_ref, 1 - core))):
        copy = pltpu.make_async_copy(piece.at[:, columns], target.at[half], sems.at[which])
        copy.start()
        copies.append(copy)
    return copies


def first_norm_kernel(
    columns,
    core_ref,
    mixed_ref,
    rows_ref,
    vec_ref,
    own_ref,
    swap_ref,
    low_ref,
    hidden_ref,
    normal_ref,
    scale_ref,
    weight_ref,
    sems,
):
    for copy in assemble(core_ref, own_ref, swap_ref, columns, weight_ref, sems):
        copy.wait()
    mixed = mixed_ref[...]
    lin = jnp.concatenate([nn(mixed, weight_ref[0]), nn(mixed, weight_ref[1])], axis=1)
    total = rows_ref[...].astype(F32) + (lin + vec_ref[2:3, :])
    normal, scale = normalised(total)
    hidden = normal * vec_ref[3:4, :] + vec_ref[4:5, :]
    low_ref[...] = hidden.astype(BF16)
    hidden_ref[...] = hidden
    normal_ref[...] = normal
    scale_ref[...] = scale


def normalised(values):
    centred = values - jnp.mean(values, axis=1, keepdims=True)
    variance = jnp.mean(centred * centred, axis=1, keepdims=True)
    scale = lax.rsqrt(variance + EPSILON)
    return centred * scale, scale


def norm_back(grads, normal, scale, gain):
    scaled = grads * gain
    return (
        scaled
        - jnp.mean(scaled, axis=1, keepdims=True)
        - normal * jnp.mean(scaled * normal, axis=1, keepdims=True)
    ) * scale


def column_sum(values):
    return jnp.sum(values, axis=0, keepdims=True)


def first_norm(core, mixed, rows, vectors, own, swap, columns):
    tokens, width = mixed.shape
    vmem = pl.BlockSpec(memory_space=pltpu.VMEM)
    half = columns.stop - columns.start
    return pl.pallas_call(
        functools.partial(first_norm_kernel, columns),
        out_shape=(
            jax.ShapeDtypeStruct((tokens, width), BF16),
            jax.ShapeDtypeStruct((tokens, width), F32),
            jax.ShapeDtypeStruct((tokens, width), F32),
            jax.ShapeDtypeStruct((tokens, 1), F32),
            jax.ShapeDtypeStruct((2, width, half), BF16),
        ),
        in_specs=[pl.BlockSpec(memory_space=pltpu.SMEM)]
        + [vmem] * 3
        + [pl.BlockSpec(memory_space=pl.ANY)] * 2,
        out_specs=(vmem,) * 5,
        scratch_shapes=[pltpu.SemaphoreType.DMA((2,))],
        compiler_params=pltpu.CompilerParams(vmem_limit_bytes=VMEM_BYTES),
        cost_estimate=pl.CostEstimate(
            flops=64 * tokens * width * width, bytes_accessed=4 * width * width, transcendentals=0
        ),
        name="first_norm",
    )(core, mixed, rows, vectors, own, swap)


def ff_forward_kernel(
    in_columns,
    out_columns,
    core_ref,
    hidden_ref,
    bias_ref,
    own_ref,
    swap_ref,
    act_ref,
    slope_ref,
    gelu_ref,
    parts_ref,
    w_in_ref,
    w_out_ref,
    sems,
):
    in_copies = assemble(core_ref, own_ref, swap_ref, in_columns, w_in_ref, sems.at[0])
    out_copies = assemble(core_ref, own_ref, swap_ref, out_columns, w_out_ref, sems.at[1])
    for copy in in_copies:
        copy.wait()
    tokens = hidden_ref.shape[0]

    def expand(tile, carry):
        at = pl.ds(pl.multiple_of(tile * FF_TILE, FF_TILE), FF_TILE)
        rows = hidden_ref[at, :]
        gate = nn(rows, w_in_ref[0]) + bias_ref[0:1, :]
        up = nn(rows, w_in_ref[1]) + bias_ref[1:2, :]
        cdf = 0.5 * (1.0 + lax.erf(gate * (0.5**0.5)))
        density = jnp.exp(-0.5 * gate * gate) * 0.3989422804014327
        gelu = gate * cdf
        act_ref[at, :] = (gelu * up).astype(BF16)
        gelu_ref[at, :] = gelu.astype(BF16)
        slope_ref[at, :] = (up * (cdf + gate * density)).astype(BF16)
        return carry

    lax.fori_loop(0, tokens // FF_TILE, expand, 0)
    for copy in out_copies:
        copy.wait()

    def contract(tile, carry):
        at = pl.ds(pl.multiple_of(tile * FF_TILE, FF_TILE), FF_TILE)
        rows = act_ref[at, :]
        parts_ref[at, :] = jnp.concatenate(
            [nn(rows, w_out_ref[0]), nn(rows, w_out_ref[1])], axis=1
        ).astype(BF16)
        return carry

    lax.fori_loop(0, tokens // FF_TILE, contract, 0)


def ff_forward(core, hidden, bias, own, swap, in_columns, out_columns):
    tokens, width = hidden.shape
    units = bias.shape[1]
    vmem = pl.BlockSpec(memory_space=pltpu.VMEM)
    return pl.pallas_call(
        functools.partial(ff_forward_kernel, in_columns, out_columns),
        out_shape=(
            jax.ShapeDtypeStruct((tokens, units), BF16),
            jax.ShapeDtypeStruct((tokens, units), BF16),
            jax.ShapeDtypeStruct((tokens, units), BF16),
            jax.ShapeDtypeStruct((tokens, width), BF16),
            jax.ShapeDtypeStruct((2, width, units), BF16),
            jax.ShapeDtypeStruct((2, units, width // 2), BF16),
        ),
        in_specs=[pl.BlockSpec(memory_space=pltpu.SMEM)]
        + [vmem] * 2
        + [pl.BlockSpec(memory_space=pl.ANY)] * 2,
        out_specs=(vmem,) * 6,
        scratch_shapes=[pltpu.SemaphoreType.DMA((2, 2))],
        compiler_params=pltpu.CompilerParams(vmem_limit_bytes=VMEM_BYTES),
        cost_estimate=pl.CostEstimate(
            flops=32 * tokens * width * units,
            bytes_accessed=6 * width * units,
            transcendentals=2 * tokens * units,
        ),
        name="ff_forward",
    )(core, hidden, bias, own, swap)


def second_norm_kernel(
    parts_ref, hidden_ref, cotangent_ref, vec_ref, result_ref, grad_ref, low_ref, sums_ref
):
    lin = jnp.sum(parts_ref[...].astype(F32), axis=0) + vec_ref[5:6, :]
    normal, scale = normalised(hidden_ref[...] + lin)
    gain = vec_ref[6:7, :]
    result_ref[...] = (normal * gain + vec_ref[7:8, :]).astype(BF16)
    grads = cotangent_ref[...].astype(F32)
    back = norm_back(grads, normal, scale, gain)
    low = back.astype(BF16)
    grad_ref[...] = back
    low_ref[...] = low
    sums_ref[...] = jnp.concatenate(
        [
            column_sum(low.astype(F32)),
            column_sum(grads * normal),
            column_sum(grads),
            jnp.zeros((5, back.shape[1]), F32),
        ]
    )


def second_norm(parts, hidden, cotangent, vectors):
    tokens, width = hidden.shape
    vmem = pl.BlockSpec(memory_space=pltpu.VMEM)
    return pl.pallas_call(
        second_norm_kernel,
        out_shape=(
            jax.ShapeDtypeStruct((tokens, width), BF16),
            jax.ShapeDtypeStruct((tokens, width), F32),
            jax.ShapeDtypeStruct((tokens, width), BF16),
            jax.ShapeDtypeStruct((8, width), F32),
        ),
        in_specs=[vmem] * 4,
        out_specs=(vmem,) * 4,
        compiler_params=pltpu.CompilerParams(vmem_limit_bytes=VMEM_BYTES),
        cost_estimate=pl.CostEstimate(
            flops=20000 * tokens * width, bytes_accessed=20 * tokens * width, transcendentals=0
        ),
        name="second_norm",
    )(parts, hidden, cotangent, vectors)


def ff_backward_kernel(
    grad_ref, slope_ref, gelu_ref, w_in_ref, w_out_ref, joined_ref, parts_ref, bias_ref, half_ref
):
    tokens, width = grad_ref.shape
    half = width // 2
    bias_ref[...] = jnp.zeros_like(bias_ref)

    def visit(tile, carry):
        at = pl.ds(pl.multiple_of(tile * FF_TILE, FF_TILE), FF_TILE)
        left, right = grad_ref[at, :half], grad_ref[at, half:]
        half_ref[0, at, :] = left
        half_ref[1, at, :] = right
        act_grad = nt(left, w_out_ref[0]) + nt(right, w_out_ref[1])
        for which, factor in ((0, slope_ref), (1, gelu_ref)):
            joined = (act_grad * factor[at, :].astype(F32)).astype(BF16)
            joined_ref[which, at, :] = joined
            bias_ref[which : which + 1, :] += column_sum(joined.astype(F32))
        parts_ref[at, :] = (
            nt(joined_ref[0, at, :], w_in_ref[0]) + nt(joined_ref[1, at, :], w_in_ref[1])
        ).astype(BF16)
        return carry

    lax.fori_loop(0, tokens // FF_TILE, visit, 0)


def ff_backward(grads, slope, gelu, w_in, w_out):
    tokens, width = grads.shape
    units = slope.shape[1]
    vmem = pl.BlockSpec(memory_space=pltpu.VMEM)
    return pl.pallas_call(
        ff_backward_kernel,
        out_shape=(
            jax.ShapeDtypeStruct((2, tokens, units), BF16),
            jax.ShapeDtypeStruct((tokens, width), BF16),
            jax.ShapeDtypeStruct((2, units), F32),
            jax.ShapeDtypeStruct((2, tokens, width // 2), BF16),
        ),
        in_specs=[vmem] * 5,
        out_specs=(vmem,) * 4,
        compiler_params=pltpu.CompilerParams(vmem_limit_bytes=VMEM_BYTES),
        cost_estimate=pl.CostEstimate(
            flops=32 * tokens * width * units,
            bytes_accessed=6 * width * units,
            transcendentals=0,
        ),
        name="ff_backward",
    )(grads, slope, gelu, w_in, w_out)


def ff_grads_kernel(core_ref, act_ref, half_ref, hidden_ref, joined_ref, keep_ref, give_ref):
    core = core_ref[0]
    units = joined_ref.shape[2]
    hidden = hidden_ref[...]
    act = act_ref[...]
    give_ref[:, :units] = tn(hidden, joined_ref[1 - core]).astype(BF16)
    give_ref[:, units:] = tn(act, half_ref[1 - core]).astype(BF16)
    keep_ref[:, :units] = tn(hidden, joined_ref[core]).astype(BF16)
    keep_ref[:, units:] = tn(act, half_ref[core]).astype(BF16)


def ff_grads_of(core, act, halves, hidden, joined):
    width = hidden.shape[1]
    cols = joined.shape[2] + halves.shape[2]
    vmem = pl.BlockSpec(memory_space=pltpu.VMEM)
    return pl.pallas_call(
        ff_grads_kernel,
        out_shape=(jax.ShapeDtypeStruct((width, cols), BF16),) * 2,
        in_specs=[pl.BlockSpec(memory_space=pltpu.SMEM)] + [vmem] * 4,
        out_specs=(vmem,) * 2,
        compiler_params=pltpu.CompilerParams(vmem_limit_bytes=VMEM_BYTES),
        cost_estimate=pl.CostEstimate(flops=6 * 10**9, bytes_accessed=10**4, transcendentals=0),
        name="ff_grads",
    )(core, act, halves, hidden, joined)


def first_back_kernel(
    core_ref,
    parts_ref,
    second_ref,
    normal_ref,
    scale_ref,
    vec_ref,
    weight_ref,
    sums_ref,
    mixed_ref,
    _,
    grad_ref,
    out_ref,
    keep_ref,
    give_ref,
):
    tokens, width = second_ref.shape
    half, count = width // 2, tokens // 2
    normal = normal_ref[...]
    grads = second_ref[...] + jnp.sum(parts_ref[...].astype(F32), axis=0)
    back = norm_back(grads, normal, scale_ref[...], vec_ref[3:4, :])
    low = back.astype(BF16)
    grad_ref[...] = back
    out_grad = nt(low[:, :half], weight_ref[0]) + nt(low[:, half:], weight_ref[1])
    for seq in range(2):
        for group in range(GROUPS):
            out_ref[seq * GROUPS + group] = out_grad[
                seq * count : (seq + 1) * count, group * GROUP_WIDTH : (group + 1) * GROUP_WIDTH
            ].astype(BF16)
    rows = jnp.concatenate(
        [
            column_sum(low.astype(F32)),
            column_sum(grads * normal),
            column_sum(grads),
            sums_ref[0:3, :],
            jnp.zeros((122, width), F32),
        ]
    )
    turned = rows.T.astype(BF16)
    keep_ref[:, half:] = turned
    give_ref[:, half:] = turned
    left = tn(mixed_ref[...], low[:, :half]).astype(BF16)
    right = tn(mixed_ref[...], low[:, half:]).astype(BF16)
    own_left = core_ref[0] == 0
    keep_ref[:, :half] = jnp.where(own_left, left, right)
    give_ref[:, :half] = jnp.where(own_left, right, left)


def first_back(core, parts, second_grad, normal, scale, vectors, weight, sums, mixed, earlier):
    tokens, width = second_grad.shape
    vmem = pl.BlockSpec(memory_space=pltpu.VMEM)
    return pl.pallas_call(
        first_back_kernel,
        out_shape=(
            jax.ShapeDtypeStruct((tokens, width), F32),
            jax.ShapeDtypeStruct((2 * GROUPS, tokens // 2, GROUP_WIDTH), BF16),
            jax.ShapeDtypeStruct((width, width // 2 + 128), BF16),
            jax.ShapeDtypeStruct((width, width // 2 + 128), BF16),
        ),
        in_specs=[pl.BlockSpec(memory_space=pltpu.SMEM)]
        + [vmem] * 8
        + [pl.BlockSpec(memory_space=pl.ANY)],
        out_specs=(vmem,) * 4,
        compiler_params=pltpu.CompilerParams(vmem_limit_bytes=VMEM_BYTES),
        cost_estimate=pl.CostEstimate(
            flops=64 * tokens * width * width, bytes_accessed=4 * width * width, transcendentals=0
        ),
        name="first_back",
    )(core, parts, second_grad, normal, scale, vectors, weight, sums, mixed, earlier)


def finish_kernel(
    place_ref,
    dq_ref,
    own_ref,
    c_ref,
    y_ref,
    turned_ref,
    weight_ref,
    shift_ref,
    input_ref,
    keep_ref,
    give_ref,
):
    kv_grad = own_ref[...].astype(F32) + c_ref[...].astype(F32) + y_ref[...].astype(F32)
    grads = jnp.concatenate([dq_ref[...], kv_grad.astype(BF16)], axis=1)
    inputs = nt(grads, weight_ref[...]).astype(BF16)
    owners, count = input_ref.shape[0], input_ref.shape[1]
    for owner in range(owners):
        input_ref[owner] = inputs[owner * count : (owner + 1) * count]
    weights = tn(turned_ref[...], grads)
    cols = weights.shape[1]
    owners, shifts = shift_ref.shape
    shard = weights.shape[0] // (4 * owners)
    sums = column_sum(grads.astype(F32))
    for y_side in range(2):
        blocks = []
        for c_side in range(2):
            first = (y_side * 2 + c_side) * shard
            here = (place_ref[1] == c_side) & (place_ref[2] == y_side)
            shift = jnp.where(here, shift_ref[...], 0.0)
            blocks.append(
                jnp.concatenate(
                    [
                        *(
                            weights[at : at + shard]
                            for at in range(first, weights.shape[0], 4 * shard)
                        ),
                        jnp.concatenate([shift, jnp.zeros((owners, cols - shifts), F32)], axis=1),
                        jnp.broadcast_to(sums, (8, cols)),
                    ]
                ).astype(BF16)
            )
        own_first = place_ref[0] == 0
        keep_ref[y_side] = jnp.where(own_first, blocks[0], blocks[1])
        give_ref[y_side] = jnp.where(own_first, blocks[1], blocks[0])


def finish(place, query_grads, own, from_c, from_y, turned, weight, shifts):
    tokens, width = turned.shape
    cols = weight.shape[1]
    rows = width // 4 + shifts.shape[0] + 8
    vmem = pl.BlockSpec(memory_space=pltpu.VMEM)
    return pl.pallas_call(
        finish_kernel,
        out_shape=(
            jax.ShapeDtypeStruct((8, tokens // 8, width), BF16),
            jax.ShapeDtypeStruct((2, rows, cols), BF16),
            jax.ShapeDtypeStruct((2, rows, cols), BF16),
        ),
        in_specs=[pl.BlockSpec(memory_space=pltpu.SMEM)] + [vmem] * 7,
        out_specs=(vmem,) * 3,
        compiler_params=pltpu.CompilerParams(vmem_limit_bytes=VMEM_BYTES),
        cost_estimate=pl.CostEstimate(
            flops=16 * tokens * width * cols, bytes_accessed=4 * tokens * width, transcendentals=0
        ),
        name="finish",
    )(place, query_grads, own, from_c, from_y, turned, weight, shifts)


def swap_sum(keep, give, axis):
    return keep.astype(F32) + lax.ppermute(give.astype(BF16), axis, SWAP).astype(F32)


def gather_plane(block):
    return lax.all_gather(block, PLANE, axis=0, tiled=True)


def spread_plane(parts):
    return lax.all_to_all(parts.reshape(4, -1, parts.shape[1]), PLANE, 0, 0, tiled=True)


def after(array, earlier):
    first = earlier[(slice(0, 1),) * earlier.ndim].reshape((1,) * array.ndim)
    return array + (first.astype(F32) * 0.0).astype(array.dtype)


def hold_kernel(*refs):
    del refs


def hold(array, earlier):
    anywhere = pl.BlockSpec(memory_space=pl.ANY)
    return pl.pallas_call(
        hold_kernel,
        out_shape=jax.ShapeDtypeStruct(array.shape, array.dtype),
        in_specs=[anywhere] * 2,
        out_specs=anywhere,
        input_output_aliases={0: 0},
        name="hold",
    )(array, earlier)


def pick_at(parts, index, axis):
    return lax.dynamic_index_in_dim(parts, index, axis, keepdims=False)


def plane_hop(parts, name):
    index = lax.axis_index(name)
    return two(
        pick_at(parts, index, 2),
        lax.ppermute(pick_at(parts, 1 - index, 2), name, SWAP),
        index,
    )


def pick(parts, index):
    return lax.dynamic_index_in_dim(parts, index, 0, keepdims=False)


def two(own, other, index):
    return jnp.where(index == 0, jnp.stack([own, other]), jnp.stack([other, own]))


def body(
    tokens,
    positions,
    w_qkv,
    qv_bias,
    w_attn_out,
    attn_out_bias,
    norm1_gain,
    norm1_bias,
    w_in,
    in_bias,
    w_out,
    out_bias,
    norm2_gain,
    norm2_bias,
    cotangent,
):
    seq_count, row_count, width = tokens.shape
    outer = lax.axis_size("e")
    seq_size = 2 * outer * GROUPS
    devices = seq_size * 4
    shard = w_qkv.shape[0]
    ff_shard = w_out.shape[0]
    ring = 4 * outer
    group = lax.axis_index(("r", "x"))
    place = lax.axis_index(("y", "c"))
    units = 2 * ring * ff_shard
    y_at, c_at = lax.axis_index("y"), lax.axis_index("c")
    qkv_cols = 3 * GROUP_WIDTH

    half = width // 2

    with jax.named_scope("gather_ff_weights"):
        in_cols = (
            w_in.reshape(shard, 2, ring, 4, 2 * ff_shard)
            .transpose(3, 1, 0, 2, 4)
            .reshape(4, 2, shard, units)
        )
        attn_cols = w_attn_out.reshape(shard, 2, half).transpose(1, 0, 2)
        in_parts = jnp.concatenate(
            [in_cols, jnp.broadcast_to(attn_cols, (4, 2, shard, half))], axis=3
        ).reshape(8, shard, units + half)
        in_parts = lax.all_to_all(
            in_parts, ("x", "y", "c"), 0, 0, tiled=True
        ).reshape(8 * shard, units + half)

    with jax.named_scope("gather_qkv_weights"):
        own_pos = lax.dynamic_slice_in_dim(positions, place * row_count, row_count, 1)
        shorts = jnp.stack(
            [
                qv_bias[0],
                qv_bias[1],
                attn_out_bias,
                norm1_gain,
                norm1_bias,
                out_bias,
                norm2_gain,
                norm2_bias,
            ]
        )
        spare = 64
        wide = qkv_cols + spare
        high = max(shard, 16)
        shift_rows = -(-2 * ff_shard // spare)
        smalls = jnp.concatenate(
            [
                jnp.broadcast_to(jnp.pad(shorts, ((0, 0), (0, spare - shard))), (2, 8, spare)),
                (own_pos >> 7).astype(BF16)[:, None],
                (own_pos & 127).astype(BF16)[:, None],
                jnp.broadcast_to(
                    jnp.pad(in_bias, (0, shift_rows * spare - 2 * ff_shard)).reshape(
                        shift_rows, spare
                    ),
                    (2, shift_rows, spare),
                ),
                jnp.zeros((2, high - 10 - shift_rows, spare), BF16),
            ],
            axis=1,
        )
        columns = (
            w_qkv.reshape(shard, 3, GROUPS, GROUP_WIDTH)
            .transpose(2, 0, 1, 3)
            .reshape(1, GROUPS, shard, qkv_cols)
        )
        columns = jnp.pad(columns, ((0, 0), (0, 0), (0, high - shard), (0, 0)))
        parcel = jnp.concatenate(
            [
                jnp.broadcast_to(columns, (2, GROUPS, high, qkv_cols)),
                jnp.broadcast_to(smalls[:, None], (2, GROUPS, high, spare)),
            ],
            axis=3,
        ).reshape(8, high, wide)
        parcel = lax.all_to_all(after(parcel, in_parts), SEQ_GROUP, 0, 0, tiled=True)

    with jax.named_scope("gather_tokens"):
        s_at, r_at, x_at = (lax.axis_index(name) for name in SEQ_GROUP)
        chunk = two(
            pick(tokens, s_at), lax.ppermute(pick(tokens, 1 - s_at), "s", SWAP), s_at
        )
        chunk = two(chunk, lax.ppermute(chunk, "r", SWAP), r_at)
        parcel = hold(parcel, chunk)
        chunk = two(chunk, lax.ppermute(chunk, "x", SWAP), x_at)
        chunk = chunk.transpose(2, 1, 0, 3, 4).reshape(8 * row_count, width)

    with jax.named_scope("gather_qkv_weights"):
        parcels = lax.all_gather(parcel, CHUNKS, axis=0, tiled=False)
        parcels = parcels.reshape(outer, 2, 2, 2, 2, 2, high, wide)
        order = (3, 0, 4, 5, 1, 2)
        qkv_slice = (
            parcels[..., :shard, :qkv_cols].transpose(*order, 6, 7).reshape(width, qkv_cols)
        )
        smalls = parcels[..., qkv_cols:]
        vectors = (
            smalls[..., :8, :shard].transpose(6, *order, 7).reshape(8, width).astype(F32)
        )
        pos_parts = smalls[..., 8:10, :row_count].astype(F32)
        chunk_pos = (pos_parts[..., 0, :] * 128.0 + pos_parts[..., 1, :]).reshape(
            outer, 2, 2, 8 * row_count
        )
        in_shift = pick_at(
            pick_at(smalls[..., 10 : 10 + shift_rows, :], x_at, 1), y_at, 1
        )
        in_shift = (
            in_shift.transpose(1, 0, 2, 3, 4, 5)
            .reshape(seq_size, shift_rows * spare)[:, : 2 * ff_shard]
            .reshape(2, units)
            .astype(F32)
        )

    with jax.named_scope("gather_ff_weights"):
        out_halves = w_out.reshape(ff_shard, 2, half).transpose(1, 0, 2)
        out_cols = two(
            pick(out_halves, c_at), lax.ppermute(pick(out_halves, 1 - c_at), "c", SWAP), c_at
        ).reshape(2 * ff_shard, half)
        packed = jnp.concatenate([in_parts, out_cols], axis=1)
        packed = lax.all_gather(packed, RING, axis=0, tiled=True)
        core = c_at.reshape(1).astype(jnp.int32)

    with jax.named_scope("project"):
        qv_slice = lax.dynamic_slice_in_dim(vectors[:2], group * GROUP_WIDTH, GROUP_WIDTH, 1)
        column_bias = jnp.concatenate(
            [qv_slice[0], jnp.zeros((GROUP_WIDTH,), F32), qv_slice[1]]
        )
        queries = (
            jnp.dot(chunk, qkv_slice[:, :GROUP_WIDTH], preferred_element_type=F32)
            + column_bias[:GROUP_WIDTH]
        ).astype(BF16)
        own_kv = (
            jnp.dot(chunk, qkv_slice[:, GROUP_WIDTH:], preferred_element_type=F32)
            + column_bias[GROUP_WIDTH:]
        ).astype(BF16)
    with jax.named_scope("gather_kv"):
        if outer > 1:
            own_kv = lax.all_gather(own_kv, "e", axis=0, tiled=True)
        y_kv = lax.ppermute(own_kv, "y", SWAP)
        key_values = [
            own_kv,
            lax.ppermute(own_kv, "c", SWAP),
            y_kv,
            lax.ppermute(y_kv, "c", SWAP),
        ]
    ordered_pos = jnp.stack(
        [
            lax.dynamic_index_in_dim(
                lax.dynamic_index_in_dim(chunk_pos, y_at ^ ky, 1, keepdims=False),
                c_at ^ kc,
                1,
                keepdims=False,
            )
            for ky in (0, 1)
            for kc in (0, 1)
        ]
    )
    query_pos = lax.dynamic_index_in_dim(ordered_pos[0], lax.axis_index("e"), 0, keepdims=True)
    key_pos = ordered_pos.reshape(4 * outer, 8 * row_count)
    head_ids = group * GROUP_HEADS + jnp.arange(GROUP_HEADS)
    slopes = 2.0 ** (-8.0 * (head_ids + 1).astype(F32) / HEADS) * LOG2E

    with jax.named_scope("attention"):
        span = outer
        parts = ((0, 2), (2, 3), (3, 4))
        state = None
        for number, (first, last) in enumerate(parts):
            state = attend(
                slopes,
                queries,
                query_pos,
                key_pos[first * span : last * span],
                key_values[first:last],
                state,
                last=last == 4,
                earlier=(vectors, in_shift) if number == 1 else (),
            )
        attended, log_sums, attended_low = state

    with jax.named_scope("return_attended"):
        returned = lax.all_to_all(
            attended_low.reshape(8, row_count, GROUP_WIDTH), SEQ_GROUP, 0, 0, tiled=True
        )
        mixed = (
            returned.reshape(2, GROUPS, row_count, GROUP_WIDTH)
            .transpose(0, 2, 1, 3)
            .reshape(2 * row_count, width)
        )
    with jax.named_scope("first_norm"):
        packed = hold(packed, mixed)
        attn_own = packed[:, units : units + half]
        attn_swap = lax.ppermute(attn_own, "c", SWAP)
        hidden_low, hidden, normal, scale, attn_full = first_norm(
            core,
            mixed,
            tokens.reshape(2 * row_count, width),
            vectors,
            attn_own,
            attn_swap,
            slice(0, half),
        )
        packed = hold(packed, hidden_low)
        swapped = lax.ppermute(packed, "c", SWAP)
    with jax.named_scope("gather_hidden"):
        hidden_group = gather_plane(hidden_low)
    with jax.named_scope("ff_forward"):
        activated_low, slope, gelu, ff_parts, in_slice, out_slice = ff_forward(
            core,
            hidden_group,
            in_shift,
            packed,
            swapped,
            slice(0, units),
            slice(units + half, units + width),
        )
    with jax.named_scope("sum_ff"):
        ff_parts = spread_plane(ff_parts)
    with jax.named_scope("second_norm"):
        result, second_grad, ff_grad, sums = second_norm(
            ff_parts, hidden, cotangent.reshape(2 * row_count, width), vectors
        )
    with jax.named_scope("gather_ff_grad"):
        ff_grads = gather_plane(ff_grad)
    with jax.named_scope("ff_backward"):
        joined_grad, hidden_parts, grad_in_shift, grad_halves = ff_backward(
            ff_grads, slope, gelu, in_slice, out_slice
        )
    with jax.named_scope("sum_hidden_grad"):
        hidden_parts = spread_plane(hidden_parts)
    with jax.named_scope("ff_weight_grads"):
        keep, give = ff_grads_of(core, activated_low, grad_halves, hidden_group, joined_grad)
        ff_keep, ff_give = keep, give
    with jax.named_scope("first_norm_back"):
        first_grad, out_grad, keep, give = first_back(
            core,
            hidden_parts,
            second_grad,
            normal,
            scale,
            vectors,
            attn_full,
            sums,
            mixed,
            ff_keep,
        )
    with jax.named_scope("send_out_grad"):
        out_grads = lax.all_to_all(out_grad, SEQ_GROUP, 0, 0, tiled=True).reshape(
            8 * row_count, GROUP_WIDTH
        )
    with jax.named_scope("attn_weight_grad"):
        rows = jnp.concatenate(
            [swap_sum(keep, give, "c"), swap_sum(ff_keep, ff_give, "c")], axis=1
        ).astype(BF16)
        rows = hold(rows, out_grads)
        row_sums = lax.psum_scatter(rows, RING, scatter_dimension=0, tiled=True)

    with jax.named_scope("attention_back"):
        state, c_part, y_part, cy_part = attend_back(
            slopes,
            queries,
            query_pos,
            key_pos[span:],
            out_grads,
            attended,
            log_sums,
            key_values[1:],
            None,
            last=False,
            earlier=(rows,),
        )
        y_sum = swap_sum(y_part, cy_part, "c").astype(BF16)
        query_grads, own_part = attend_back(
            slopes,
            queries,
            query_pos,
            key_pos[:span],
            out_grads,
            attended,
            log_sums,
            key_values[:1],
            state,
            last=True,
            earlier=(y_sum,),
        )
    with jax.named_scope("sum_kv_grads"):
        from_c = lax.ppermute(c_part, "c", SWAP)
        from_y = lax.ppermute(y_sum, "y", SWAP)
        if outer > 1:
            total = own_part.astype(F32) + from_c.astype(F32) + from_y.astype(F32)
            own_part = lax.psum_scatter(
                total, "e", scatter_dimension=0, tiled=True
            ).astype(BF16)
            from_c = from_y = jnp.zeros_like(own_part)

    with jax.named_scope("finish"):
        input_parts, keep, give = finish(
            jnp.stack([c_at, y_at, x_at]).astype(jnp.int32),
            query_grads,
            own_part,
            from_c,
            from_y,
            chunk,
            qkv_slice,
            grad_in_shift.reshape(seq_size, 2 * ff_shard),
        )
    with jax.named_scope("input_grad"):
        input_parts = lax.all_to_all(input_parts, SEQ_GROUP, 0, 0, tiled=True)
        input_grad = first_grad.reshape(2, row_count, width) + jnp.sum(
            input_parts.reshape(2, GROUPS, row_count, width).astype(F32), axis=1
        )
    with jax.named_scope("qkv_weight_grad"):
        bundle = swap_sum(keep, give, "c").astype(BF16)
        bundle = swap_sum(pick(bundle, y_at), pick(bundle, 1 - y_at), "y").astype(BF16)
        ends = width // 4 + seq_size
        shares = jnp.concatenate(
            [
                bundle[: width // 4].reshape(seq_size, shard, qkv_cols),
                jnp.broadcast_to(bundle[ends : ends + 1], (seq_size, 1, qkv_cols)),
                bundle[width // 4 : ends][:, None],
                jnp.zeros((seq_size, 6, qkv_cols), BF16),
            ],
            axis=1,
        )
    with jax.named_scope("ff_weight_grads"):
        row_sums = hold(row_sums, bundle)
        own_cols = half + 128 + units
        split = plane_hop(row_sums[:, :own_cols].reshape(2, 2, 2, shard, own_cols), "c")
    with jax.named_scope("qkv_weight_grad"):
        shares = lax.all_to_all(
            hold(hold(shares, input_parts), split), SEQ_AXIS, 0, 0, tiled=True
        )
    with jax.named_scope("ff_weight_grads"):
        exchanged = plane_hop(plane_hop(split, "y"), "x").reshape(4, 2, shard, own_cols)
        out_sums = row_sums[:, own_cols:].reshape(2, ff_shard, half)
        grad_w_out = (
            two(
                pick(out_sums, c_at),
                lax.ppermute(pick(out_sums, 1 - c_at), "c", SWAP),
                c_at,
            )
            .transpose(1, 0, 2)
            .reshape(ff_shard, width)
            .astype(F32)
        )
        grad_w_in = (
            exchanged[..., half + 128 :]
            .reshape(4, 2, shard, ring, 2 * ff_shard)
            .transpose(2, 1, 3, 0, 4)
            .reshape(shard, 2 * devices * ff_shard)
            .astype(F32)
        )
        grad_w_attn = (
            jnp.sum(exchanged[..., :half].astype(F32), axis=0)
            .transpose(1, 0, 2)
            .reshape(shard, width)
        )
        vector_grads = jnp.sum(exchanged[:, 0, :, half : half + 8].astype(F32), axis=0).T
    with jax.named_scope("qkv_weight_grad"):
        shares = hold(shares, exchanged).astype(F32)
        totals = jnp.sum(shares.reshape(2 * outer, GROUPS, shard + 8, qkv_cols), axis=0)
        grad_w_qkv = (
            totals[:, :shard]
            .reshape(GROUPS, shard, 3, GROUP_WIDTH)
            .transpose(1, 2, 0, 3)
            .reshape(shard, 3 * width)
        )
        sums = totals[:, shard].reshape(GROUPS, 3, GROUP_WIDTH).transpose(1, 0, 2).reshape(3, width)
        grad_qv = lax.dynamic_slice_in_dim(sums[0::2], lax.axis_index(EVERY) * shard, shard, 1)
        grad_in_bias = jnp.sum(totals[:, shard + 1, : 2 * ff_shard], axis=0)

    return (
        result.reshape(2, row_count, width).astype(BF16),
        input_grad,
        grad_w_qkv,
        grad_qv,
        grad_w_attn,
        vector_grads[0],
        vector_grads[1],
        vector_grads[2],
        grad_w_in,
        grad_in_bias,
        grad_w_out,
        vector_grads[3],
        vector_grads[4],
        vector_grads[5],
    )


def solution(mesh):
    seq_size = mesh.shape["seq"]
    split = Mesh(mesh.devices.reshape(2, seq_size // 8, 2, 2, 2, 2), EVERY)
    tokens_at = P(None, EVERY, None)
    rows_at = P(EVERY, None)
    vector_at = P(EVERY)
    return jax.shard_map(
        body,
        mesh=split,
        in_specs=(
            tokens_at,
            P(None, SEQ_AXIS),
            rows_at,
            P(None, EVERY),
            rows_at,
            vector_at,
            vector_at,
            vector_at,
            rows_at,
            vector_at,
            rows_at,
            vector_at,
            vector_at,
            vector_at,
            tokens_at,
        ),
        out_specs=(
            tokens_at,
            tokens_at,
            rows_at,
            P(None, EVERY),
            rows_at,
            vector_at,
            vector_at,
            vector_at,
            rows_at,
            vector_at,
            rows_at,
            vector_at,
            vector_at,
            vector_at,
        ),
        check_vma=False,
    )
```

```python
import functools

import jax
import jax.numpy as jnp
from jax import lax
from jax.experimental import pallas as pl
from jax.experimental.pallas import tpu as pltpu
from jax.sharding import Mesh
from jax.sharding import PartitionSpec as P

HEADS = 12
HEAD_DIM = 64
GROUPS = 4
GROUP_HEADS = HEADS // GROUPS
GROUP_WIDTH = GROUP_HEADS * HEAD_DIM
EPSILON = 1e-12
SCORE_SCALE = 0.125
LOG2E = 1.4426950408889634
LOWEST = -1e30
GRAD_TILE = 256
KEY_BLOCK = 512
FF_TILE = 256
SEQ_GROUP = ("s", "r", "x")
CHUNKS = ("e", "y", "c")
RING = ("s", "e", "r")
PLANE = ("x", "y")
SEQ_AXIS = ("s", "e", "r", "x")
EVERY = ("s", "e", "r", "x", "y", "c")
SWAP = ((0, 1), (1, 0))
BF16 = jnp.bfloat16
F32 = jnp.float32
VMEM_BYTES = 60 * 2**20


def nt(a, b):
    return lax.dot_general(a, b, (((1,), (1,)), ((), ())), preferred_element_type=F32)


def tn(a, b):
    return lax.dot_general(a, b, (((0,), (0,)), ((), ())), preferred_element_type=F32)


def nn(a, b):
    return lax.dot_general(a, b, (((1,), (0,)), ((), ())), preferred_element_type=F32)


def head_cols(head, base=0):
    return slice(base + head * HEAD_DIM, base + (head + 1) * HEAD_DIM)


def log2_scores(keys, queries, slope, key_pos, query_pos):
    products = nt(keys, queries)
    distances = jnp.abs(key_pos * slope - query_pos * slope)
    return products * (SCORE_SCALE * LOG2E) - distances


def column(row):
    return jnp.broadcast_to(row, (8, row.shape[1])).T[:, :1]


def key_blocks(kv_refs):
    start = 0
    for piece in kv_refs:
        yield piece, start
        start += piece.shape[0]


def turn_positions(pk_ref, column_ref):
    length = pk_ref.shape[1]

    def turn(row, carry):
        at = pl.ds(pl.multiple_of(row * length, length), length)
        column_ref[at, :] = column(pk_ref[pl.ds(row, 1), :])
        return carry

    lax.fori_loop(0, pk_ref.shape[0], turn, 0)


def attend_kernel(deps, count, first, last, slopes_ref, q_ref, pq_ref, pk_ref, *refs):
    refs = refs[deps:]
    kv_refs, refs = refs[:count], refs[count:]
    if not first:
        (sum_in_ref, stat_in_ref), refs = refs[:2], refs[2:]
    sum_ref, stat_ref = refs[:2]
    column_ref = refs[-1]
    rows = q_ref.shape[0]
    query_pos = pq_ref[...]
    turn_positions(pk_ref, column_ref)
    for head in range(GROUP_HEADS):
        slope = slopes_ref[head]
        queries = q_ref[:, head_cols(head)]
        if first:
            carry = (
                jnp.full((1, rows), LOWEST, F32),
                jnp.zeros((1, rows), F32),
                jnp.zeros((HEAD_DIM, rows), F32),
            )
        else:
            carry = (
                stat_in_ref[head : head + 1, :],
                stat_in_ref[GROUP_HEADS + head : GROUP_HEADS + head + 1, :],
                sum_in_ref[head_cols(head), :],
            )
        for kv_ref, start in key_blocks(kv_refs):

            def visit(block, carry, kv_ref=kv_ref, start=start):
                top, total, summed = carry
                at = pl.ds(pl.multiple_of(block * KEY_BLOCK, KEY_BLOCK), KEY_BLOCK)
                pos_at = pl.ds(
                    pl.multiple_of(start + block * KEY_BLOCK, KEY_BLOCK), KEY_BLOCK
                )
                keys = kv_ref[at, head_cols(head)]
                values = kv_ref[at, head_cols(head, GROUP_WIDTH)]
                scores = log2_scores(keys, queries, slope, column_ref[pos_at, :], query_pos)
                new_top = jnp.maximum(top, jnp.max(scores, axis=0, keepdims=True))
                weights = jnp.exp2(scores - new_top)
                shrink = jnp.exp2(top - new_top)
                total = total * shrink + jnp.sum(weights, axis=0, keepdims=True)
                summed = summed * shrink + tn(values, weights.astype(BF16))
                return new_top, total, summed

            carry = lax.fori_loop(0, kv_ref.shape[0] // KEY_BLOCK, visit, carry)
        top, total, summed = carry
        if last:
            attended = summed / total
            sum_ref[head_cols(head), :] = attended
            refs[2][:, head_cols(head)] = attended.T.astype(BF16)
            stat_ref[head : head + 1, :] = top + jnp.log2(total)
        else:
            sum_ref[head_cols(head), :] = summed
            stat_ref[head : head + 1, :] = top
            stat_ref[GROUP_HEADS + head : GROUP_HEADS + head + 1, :] = total


def attend(slopes, queries, query_pos, key_pos, key_values, state, last, earlier):
    rows, length = queries.shape[0], key_pos.size
    vmem = pl.BlockSpec(memory_space=pltpu.VMEM)
    count = len(key_values)
    first = state is None
    state = () if first else state
    outs = [
        jax.ShapeDtypeStruct((GROUP_WIDTH, rows), F32),
        jax.ShapeDtypeStruct((GROUP_HEADS * (1 if last else 2), rows), F32),
    ]
    if last:
        outs.append(jax.ShapeDtypeStruct((rows, GROUP_WIDTH), BF16))
    return pl.pallas_call(
        functools.partial(attend_kernel, len(earlier), count, first, last),
        out_shape=tuple(outs),
        in_specs=[pl.BlockSpec(memory_space=pltpu.SMEM)]
        + [vmem] * 3
        + [pl.BlockSpec(memory_space=pl.ANY)] * len(earlier)
        + [vmem] * (count + len(state)),
        out_specs=(vmem,) * len(outs),
        scratch_shapes=[pltpu.VMEM((length, 1), F32)],
        compiler_params=pltpu.CompilerParams(vmem_limit_bytes=VMEM_BYTES),
        cost_estimate=pl.CostEstimate(
            flops=64 * rows * length * GROUP_WIDTH,
            bytes_accessed=rows * length,
            transcendentals=rows * length * GROUP_HEADS,
        ),
        name="attend",
    )(slopes, queries, query_pos, key_pos, *earlier, *key_values, *state)


def attend_back_kernel(
    deps, count, first, last, slopes_ref, q_ref, pq_ref, pk_ref, do_ref, out_ref, lse_ref, *refs
):
    refs = refs[deps:]
    kv_refs, refs = refs[:count], refs[count:]
    if not first:
        dq_in_ref, refs = refs[0], refs[1:]
    dq_ref, dkv_refs, column_ref = refs[0], refs[1 : count + 1], refs[-1]
    rows = q_ref.shape[0]
    query_pos = pq_ref[...]
    turn_positions(pk_ref, column_ref)
    for head in range(GROUP_HEADS):
        slope = slopes_ref[head]
        queries = q_ref[:, head_cols(head)]
        out_grads = do_ref[:, head_cols(head)]
        log_sum = lse_ref[head : head + 1, :]
        delta = jnp.sum(
            out_grads.astype(F32).T * out_ref[head_cols(head), :], axis=0, keepdims=True
        )
        if first:
            query_grads = jnp.zeros((HEAD_DIM, rows), F32)
        else:
            query_grads = dq_in_ref[head_cols(head), :]
        for (kv_ref, start), dkv_ref in zip(key_blocks(kv_refs), dkv_refs):

            def visit(block, query_grads, kv_ref=kv_ref, start=start, dkv_ref=dkv_ref):
                at = pl.ds(pl.multiple_of(block * KEY_BLOCK, KEY_BLOCK), KEY_BLOCK)
                pos_at = pl.ds(
                    pl.multiple_of(start + block * KEY_BLOCK, KEY_BLOCK), KEY_BLOCK
                )
                keys = kv_ref[at, head_cols(head)]
                values = kv_ref[at, head_cols(head, GROUP_WIDTH)]
                scores = log2_scores(keys, queries, slope, column_ref[pos_at, :], query_pos)
                probs = jnp.exp2(scores - log_sum)
                prob_grads = nt(values, out_grads)
                score_grads = (probs * (prob_grads - delta)).astype(BF16)
                dkv_ref[at, head_cols(head, GROUP_WIDTH)] = nn(
                    probs.astype(BF16), out_grads
                ).astype(BF16)
                dkv_ref[at, head_cols(head)] = (nn(score_grads, queries) * SCORE_SCALE).astype(
                    BF16
                )
                return query_grads + tn(keys, score_grads)

            query_grads = lax.fori_loop(0, kv_ref.shape[0] // KEY_BLOCK, visit, query_grads)
        if last:
            dq_ref[:, head_cols(head)] = (query_grads * SCORE_SCALE).T.astype(BF16)
        else:
            dq_ref[head_cols(head), :] = query_grads


def attend_back(
    slopes,
    queries,
    query_pos,
    key_pos,
    out_grads,
    attended,
    log_sums,
    key_values,
    state,
    last,
    earlier,
):
    rows, length = queries.shape[0], key_pos.size
    vmem = pl.BlockSpec(memory_space=pltpu.VMEM)
    count = len(key_values)
    first = state is None
    state = () if first else (state,)
    query_out = (
        jax.ShapeDtypeStruct((rows, GROUP_WIDTH), BF16)
        if last
        else jax.ShapeDtypeStruct((GROUP_WIDTH, rows), F32)
    )
    return pl.pallas_call(
        functools.partial(attend_back_kernel, len(earlier), count, first, last),
        out_shape=(query_out,)
        + tuple(jax.ShapeDtypeStruct(piece.shape, BF16) for piece in key_values),
        in_specs=[pl.BlockSpec(memory_space=pltpu.SMEM)]
        + [vmem] * 6
        + [pl.BlockSpec(memory_space=pl.ANY)] * len(earlier)
        + [vmem] * (count + len(state)),
        out_specs=(vmem,) * (1 + count),
        scratch_shapes=[pltpu.VMEM((length, 1), F32)],
        compiler_params=pltpu.CompilerParams(vmem_limit_bytes=VMEM_BYTES),
        cost_estimate=pl.CostEstimate(
            flops=84 * rows * length * GROUP_WIDTH,
            bytes_accessed=rows * length,
            transcendentals=rows * length * GROUP_HEADS,
        ),
        name="attend_back",
    )(
        slopes,
        queries,
        query_pos,
        key_pos,
        out_grads,
        attended,
        log_sums,
        *earlier,
        *key_values,
        *state,
    )


def assemble(core_ref, own_ref, swap_ref, columns, target, sems):
    core = core_ref[0]
    copies = []
    for which, (piece, half) in enumerate(((own_ref, core), (swap_ref, 1 - core))):
        copy = pltpu.make_async_copy(piece.at[:, columns], target.at[half], sems.at[which])
        copy.start()
        copies.append(copy)
    return copies


def merged(parts_ref):
    return jnp.concatenate(
        [
            jnp.concatenate(
                [parts_ref[seq * GROUPS + group] for group in range(GROUPS)], axis=1
            )
            for seq in range(2)
        ]
    )


def first_norm_kernel(
    columns,
    core_ref,
    mixed_ref,
    rows_ref,
    vec_ref,
    own_ref,
    swap_ref,
    low_ref,
    hidden_ref,
    normal_ref,
    scale_ref,
    weight_ref,
    sems,
):
    for copy in assemble(core_ref, own_ref, swap_ref, columns, weight_ref, sems):
        copy.wait()
    mixed = merged(mixed_ref)
    lin = jnp.concatenate([nn(mixed, weight_ref[0]), nn(mixed, weight_ref[1])], axis=1)
    total = rows_ref[...].astype(F32) + (lin + vec_ref[2:3, :])
    normal, scale = normalised(total)
    hidden = normal * vec_ref[3:4, :] + vec_ref[4:5, :]
    low_ref[...] = hidden.astype(BF16)
    hidden_ref[...] = hidden
    normal_ref[...] = normal
    scale_ref[...] = scale


def normalised(values):
    centred = values - jnp.mean(values, axis=1, keepdims=True)
    variance = jnp.mean(centred * centred, axis=1, keepdims=True)
    scale = lax.rsqrt(variance + EPSILON)
    return centred * scale, scale


def norm_back(grads, normal, scale, gain):
    scaled = grads * gain
    return (
        scaled
        - jnp.mean(scaled, axis=1, keepdims=True)
        - normal * jnp.mean(scaled * normal, axis=1, keepdims=True)
    ) * scale


def column_sum(values):
    return jnp.sum(values, axis=0, keepdims=True)


def first_norm(core, mixed, rows, vectors, own, swap, columns):
    tokens, width = rows.shape
    vmem = pl.BlockSpec(memory_space=pltpu.VMEM)
    half = columns.stop - columns.start
    return pl.pallas_call(
        functools.partial(first_norm_kernel, columns),
        out_shape=(
            jax.ShapeDtypeStruct((tokens, width), BF16),
            jax.ShapeDtypeStruct((tokens, width), F32),
            jax.ShapeDtypeStruct((tokens, width), F32),
            jax.ShapeDtypeStruct((tokens, 1), F32),
            jax.ShapeDtypeStruct((2, width, half), BF16),
        ),
        in_specs=[pl.BlockSpec(memory_space=pltpu.SMEM)]
        + [vmem] * 3
        + [pl.BlockSpec(memory_space=pl.ANY)] * 2,
        out_specs=(vmem,) * 5,
        scratch_shapes=[pltpu.SemaphoreType.DMA((2,))],
        compiler_params=pltpu.CompilerParams(vmem_limit_bytes=VMEM_BYTES),
        cost_estimate=pl.CostEstimate(
            flops=64 * tokens * width * width, bytes_accessed=4 * width * width, transcendentals=0
        ),
        name="first_norm",
    )(core, mixed, rows, vectors, own, swap)


def ff_forward_kernel(
    in_columns,
    out_columns,
    core_ref,
    hidden_ref,
    bias_ref,
    own_ref,
    swap_ref,
    act_ref,
    slope_ref,
    gelu_ref,
    parts_ref,
    w_in_ref,
    w_out_ref,
    sems,
):
    in_copies = assemble(core_ref, own_ref, swap_ref, in_columns, w_in_ref, sems.at[0])
    out_copies = assemble(core_ref, own_ref, swap_ref, out_columns, w_out_ref, sems.at[1])
    for copy in in_copies:
        copy.wait()
    tokens = hidden_ref.shape[0]

    def expand(tile, carry):
        at = pl.ds(pl.multiple_of(tile * FF_TILE, FF_TILE), FF_TILE)
        rows = hidden_ref[at, :]
        gate = nn(rows, w_in_ref[0]) + bias_ref[0:1, :]
        up = nn(rows, w_in_ref[1]) + bias_ref[1:2, :]
        cdf = 0.5 * (1.0 + lax.erf(gate * (0.5**0.5)))
        density = jnp.exp(-0.5 * gate * gate) * 0.3989422804014327
        gelu = gate * cdf
        act_ref[at, :] = (gelu * up).astype(BF16)
        gelu_ref[at, :] = gelu.astype(BF16)
        slope_ref[at, :] = (up * (cdf + gate * density)).astype(BF16)
        return carry

    lax.fori_loop(0, tokens // FF_TILE, expand, 0)
    for copy in out_copies:
        copy.wait()

    def contract(tile, carry):
        at = pl.ds(pl.multiple_of(tile * FF_TILE, FF_TILE), FF_TILE)
        rows = act_ref[at, :]
        parts_ref[at, :] = jnp.concatenate(
            [nn(rows, w_out_ref[0]), nn(rows, w_out_ref[1])], axis=1
        ).astype(BF16)
        return carry

    lax.fori_loop(0, tokens // FF_TILE, contract, 0)


def ff_forward(core, hidden, bias, own, swap, in_columns, out_columns):
    tokens, width = hidden.shape
    units = bias.shape[1]
    vmem = pl.BlockSpec(memory_space=pltpu.VMEM)
    return pl.pallas_call(
        functools.partial(ff_forward_kernel, in_columns, out_columns),
        out_shape=(
            jax.ShapeDtypeStruct((tokens, units), BF16),
            jax.ShapeDtypeStruct((tokens, units), BF16),
            jax.ShapeDtypeStruct((tokens, units), BF16),
            jax.ShapeDtypeStruct((tokens, width), BF16),
            jax.ShapeDtypeStruct((2, width, units), BF16),
            jax.ShapeDtypeStruct((2, units, width // 2), BF16),
        ),
        in_specs=[pl.BlockSpec(memory_space=pltpu.SMEM)]
        + [vmem] * 2
        + [pl.BlockSpec(memory_space=pl.ANY)] * 2,
        out_specs=(vmem,) * 6,
        scratch_shapes=[pltpu.SemaphoreType.DMA((2, 2))],
        compiler_params=pltpu.CompilerParams(vmem_limit_bytes=VMEM_BYTES),
        cost_estimate=pl.CostEstimate(
            flops=32 * tokens * width * units,
            bytes_accessed=6 * width * units,
            transcendentals=2 * tokens * units,
        ),
        name="ff_forward",
    )(core, hidden, bias, own, swap)


def second_norm_kernel(
    parts_ref, hidden_ref, cotangent_ref, vec_ref, result_ref, grad_ref, low_ref, sums_ref
):
    lin = jnp.sum(parts_ref[...].astype(F32), axis=0) + vec_ref[5:6, :]
    normal, scale = normalised(hidden_ref[...] + lin)
    gain = vec_ref[6:7, :]
    result_ref[...] = (normal * gain + vec_ref[7:8, :]).astype(BF16)
    grads = cotangent_ref[...].astype(F32)
    back = norm_back(grads, normal, scale, gain)
    low = back.astype(BF16)
    grad_ref[...] = back
    low_ref[...] = low
    sums_ref[...] = jnp.concatenate(
        [
            column_sum(low.astype(F32)),
            column_sum(grads * normal),
            column_sum(grads),
            jnp.zeros((5, back.shape[1]), F32),
        ]
    )


def second_norm(parts, hidden, cotangent, vectors):
    tokens, width = hidden.shape
    vmem = pl.BlockSpec(memory_space=pltpu.VMEM)
    return pl.pallas_call(
        second_norm_kernel,
        out_shape=(
            jax.ShapeDtypeStruct((tokens, width), BF16),
            jax.ShapeDtypeStruct((tokens, width), F32),
            jax.ShapeDtypeStruct((tokens, width), BF16),
            jax.ShapeDtypeStruct((8, width), F32),
        ),
        in_specs=[vmem] * 4,
        out_specs=(vmem,) * 4,
        compiler_params=pltpu.CompilerParams(vmem_limit_bytes=VMEM_BYTES),
        cost_estimate=pl.CostEstimate(
            flops=20000 * tokens * width, bytes_accessed=20 * tokens * width, transcendentals=0
        ),
        name="second_norm",
    )(parts, hidden, cotangent, vectors)


def ff_backward_kernel(
    grad_ref, slope_ref, gelu_ref, w_in_ref, w_out_ref, joined_ref, parts_ref, bias_ref, half_ref
):
    tokens, width = grad_ref.shape
    half = width // 2
    bias_ref[...] = jnp.zeros_like(bias_ref)

    def visit(tile, carry):
        at = pl.ds(pl.multiple_of(tile * FF_TILE, FF_TILE), FF_TILE)
        left, right = grad_ref[at, :half], grad_ref[at, half:]
        half_ref[0, at, :] = left
        half_ref[1, at, :] = right
        act_grad = nt(left, w_out_ref[0]) + nt(right, w_out_ref[1])
        for which, factor in ((0, slope_ref), (1, gelu_ref)):
            joined = (act_grad * factor[at, :].astype(F32)).astype(BF16)
            joined_ref[which, at, :] = joined
            bias_ref[which : which + 1, :] += column_sum(joined.astype(F32))
        parts_ref[at, :] = (
            nt(joined_ref[0, at, :], w_in_ref[0]) + nt(joined_ref[1, at, :], w_in_ref[1])
        ).astype(BF16)
        return carry

    lax.fori_loop(0, tokens // FF_TILE, visit, 0)


def ff_backward(grads, slope, gelu, w_in, w_out):
    tokens, width = grads.shape
    units = slope.shape[1]
    vmem = pl.BlockSpec(memory_space=pltpu.VMEM)
    return pl.pallas_call(
        ff_backward_kernel,
        out_shape=(
            jax.ShapeDtypeStruct((2, tokens, units), BF16),
            jax.ShapeDtypeStruct((tokens, width), BF16),
            jax.ShapeDtypeStruct((2, units), F32),
            jax.ShapeDtypeStruct((2, tokens, width // 2), BF16),
        ),
        in_specs=[vmem] * 5,
        out_specs=(vmem,) * 4,
        compiler_params=pltpu.CompilerParams(vmem_limit_bytes=VMEM_BYTES),
        cost_estimate=pl.CostEstimate(
            flops=32 * tokens * width * units,
            bytes_accessed=6 * width * units,
            transcendentals=0,
        ),
        name="ff_backward",
    )(grads, slope, gelu, w_in, w_out)


def ff_grads_kernel(core_ref, act_ref, half_ref, hidden_ref, joined_ref, keep_ref, give_ref):
    core = core_ref[0]
    units = joined_ref.shape[2]

    def visit(tile, carry):
        at = pl.ds(pl.multiple_of(tile * GRAD_TILE, GRAD_TILE), GRAD_TILE)
        hidden = hidden_ref[:, at]
        act = act_ref[:, at]
        give_ref[at, :units] = tn(hidden, joined_ref[1 - core]).astype(BF16)
        give_ref[at, units:] = tn(act, half_ref[1 - core]).astype(BF16)
        keep_ref[at, :units] = tn(hidden, joined_ref[core]).astype(BF16)
        keep_ref[at, units:] = tn(act, half_ref[core]).astype(BF16)
        return carry

    lax.fori_loop(0, hidden_ref.shape[1] // GRAD_TILE, visit, 0)


def ff_grads_of(core, act, halves, hidden, joined):
    width = hidden.shape[1]
    cols = joined.shape[2] + halves.shape[2]
    vmem = pl.BlockSpec(memory_space=pltpu.VMEM)
    return pl.pallas_call(
        ff_grads_kernel,
        out_shape=(jax.ShapeDtypeStruct((width, cols), BF16),) * 2,
        in_specs=[pl.BlockSpec(memory_space=pltpu.SMEM)] + [vmem] * 4,
        out_specs=(vmem,) * 2,
        compiler_params=pltpu.CompilerParams(vmem_limit_bytes=VMEM_BYTES),
        cost_estimate=pl.CostEstimate(flops=6 * 10**9, bytes_accessed=10**4, transcendentals=0),
        name="ff_grads",
    )(core, act, halves, hidden, joined)


def first_back_kernel(
    core_ref,
    parts_ref,
    second_ref,
    normal_ref,
    scale_ref,
    vec_ref,
    weight_ref,
    sums_ref,
    mixed_ref,
    _,
    grad_ref,
    out_ref,
    keep_ref,
    give_ref,
):
    tokens, width = second_ref.shape
    half, count = width // 2, tokens // 2
    normal = normal_ref[...]
    grads = second_ref[...] + jnp.sum(parts_ref[...].astype(F32), axis=0)
    back = norm_back(grads, normal, scale_ref[...], vec_ref[3:4, :])
    low = back.astype(BF16)
    grad_ref[...] = back
    out_grad = nt(low[:, :half], weight_ref[0]) + nt(low[:, half:], weight_ref[1])
    for seq in range(2):
        for group in range(GROUPS):
            out_ref[seq * GROUPS + group] = out_grad[
                seq * count : (seq + 1) * count, group * GROUP_WIDTH : (group + 1) * GROUP_WIDTH
            ].astype(BF16)
    rows = jnp.concatenate(
        [
            column_sum(low.astype(F32)),
            column_sum(grads * normal),
            column_sum(grads),
            sums_ref[0:3, :],
            jnp.zeros((122, width), F32),
        ]
    )
    turned = rows.T.astype(BF16)
    keep_ref[:, half:] = turned
    give_ref[:, half:] = turned
    mixed = merged(mixed_ref)
    left = tn(mixed, low[:, :half]).astype(BF16)
    right = tn(mixed, low[:, half:]).astype(BF16)
    own_left = core_ref[0] == 0
    keep_ref[:, :half] = jnp.where(own_left, left, right)
    give_ref[:, :half] = jnp.where(own_left, right, left)


def first_back(core, parts, second_grad, normal, scale, vectors, weight, sums, mixed, earlier):
    tokens, width = second_grad.shape
    vmem = pl.BlockSpec(memory_space=pltpu.VMEM)
    return pl.pallas_call(
        first_back_kernel,
        out_shape=(
            jax.ShapeDtypeStruct((tokens, width), F32),
            jax.ShapeDtypeStruct((2 * GROUPS, tokens // 2, GROUP_WIDTH), BF16),
            jax.ShapeDtypeStruct((width, width // 2 + 128), BF16),
            jax.ShapeDtypeStruct((width, width // 2 + 128), BF16),
        ),
        in_specs=[pl.BlockSpec(memory_space=pltpu.SMEM)]
        + [vmem] * 8
        + [pl.BlockSpec(memory_space=pl.ANY)],
        out_specs=(vmem,) * 4,
        compiler_params=pltpu.CompilerParams(vmem_limit_bytes=VMEM_BYTES),
        cost_estimate=pl.CostEstimate(
            flops=64 * tokens * width * width, bytes_accessed=4 * width * width, transcendentals=0
        ),
        name="first_back",
    )(core, parts, second_grad, normal, scale, vectors, weight, sums, mixed, earlier)


def input_back_kernel(
    place_ref, dq_ref, own_ref, c_ref, y_ref, weight_ref, keep_ref, give_ref, grad_ref
):
    kv_grad = own_ref[...].astype(F32) + c_ref[...].astype(F32) + y_ref[...].astype(F32)
    grads = jnp.concatenate([dq_ref[...], kv_grad.astype(BF16)], axis=1)
    grad_ref[...] = grads
    inputs = nt(grads, weight_ref[...]).astype(BF16)
    pairs, count = keep_ref.shape[0], keep_ref.shape[1]
    own_first = place_ref[2] == 0
    for pair in range(pairs):
        first = inputs[2 * pair * count : (2 * pair + 1) * count]
        second = inputs[(2 * pair + 1) * count : (2 * pair + 2) * count]
        keep_ref[pair] = jnp.where(own_first, first, second)
        give_ref[pair] = jnp.where(own_first, second, first)


def input_back(place, query_grads, own, from_c, from_y, weight):
    tokens = query_grads.shape[0]
    width, cols = weight.shape
    vmem = pl.BlockSpec(memory_space=pltpu.VMEM)
    return pl.pallas_call(
        input_back_kernel,
        out_shape=(
            jax.ShapeDtypeStruct((4, tokens // 8, width), BF16),
            jax.ShapeDtypeStruct((4, tokens // 8, width), BF16),
            jax.ShapeDtypeStruct((tokens, cols), BF16),
        ),
        in_specs=[pl.BlockSpec(memory_space=pltpu.SMEM)] + [vmem] * 5,
        out_specs=(vmem,) * 3,
        compiler_params=pltpu.CompilerParams(vmem_limit_bytes=VMEM_BYTES),
        cost_estimate=pl.CostEstimate(
            flops=10 * tokens * width * cols, bytes_accessed=4 * tokens * width, transcendentals=0
        ),
        name="input_back",
    )(place, query_grads, own, from_c, from_y, weight)


def qkv_weight_kernel(place_ref, chunk_ref, grad_ref, shift_ref, keep_ref, give_ref):
    grads = grad_ref[...]
    weights = tn(chunk_ref[...], grads)
    cols = weights.shape[1]
    owners, shifts = shift_ref.shape
    shard = weights.shape[0] // (4 * owners)
    sums = column_sum(grads.astype(F32))
    for y_side in range(2):
        blocks = []
        for c_side in range(2):
            first = (y_side * 2 + c_side) * shard
            here = (place_ref[1] == c_side) & (place_ref[2] == y_side)
            shift = jnp.where(here, shift_ref[...], 0.0)
            blocks.append(
                jnp.concatenate(
                    [
                        *(
                            weights[at : at + shard]
                            for at in range(first, weights.shape[0], 4 * shard)
                        ),
                        jnp.concatenate([shift, jnp.zeros((owners, cols - shifts), F32)], axis=1),
                        jnp.broadcast_to(sums, (8, cols)),
                    ]
                ).astype(BF16)
            )
        own_first = place_ref[0] == 0
        keep_ref[y_side] = jnp.where(own_first, blocks[0], blocks[1])
        give_ref[y_side] = jnp.where(own_first, blocks[1], blocks[0])


def qkv_weight(place, chunk, grads, shifts):
    tokens, width = chunk.shape
    cols = grads.shape[1]
    rows = width // 4 + shifts.shape[0] + 8
    vmem = pl.BlockSpec(memory_space=pltpu.VMEM)
    return pl.pallas_call(
        qkv_weight_kernel,
        out_shape=(jax.ShapeDtypeStruct((2, rows, cols), BF16),) * 2,
        in_specs=[pl.BlockSpec(memory_space=pltpu.SMEM)] + [vmem] * 3,
        out_specs=(vmem,) * 2,
        compiler_params=pltpu.CompilerParams(vmem_limit_bytes=VMEM_BYTES),
        cost_estimate=pl.CostEstimate(
            flops=14 * tokens * width * cols, bytes_accessed=4 * tokens * width, transcendentals=0
        ),
        name="qkv_weight",
    )(place, chunk, grads, shifts)


def unpack_kernel(half, ring, parts_ref, in_ref, attn_ref, vec_ref):
    start = half + 128
    units = parts_ref.shape[3] - start
    piece = units // ring
    for side in range(2):
        for place in range(ring):
            at = start + place * piece
            to = (side * ring + place) * 4 * piece
            in_ref[:, to : to + 4 * piece] = jnp.concatenate(
                [parts_ref[plane, side, :, at : at + piece].astype(F32) for plane in range(4)],
                axis=1,
            )
        attn_ref[:, side * half : (side + 1) * half] = sum(
            parts_ref[plane, side, :, :half].astype(F32) for plane in range(4)
        )
    vectors = sum(parts_ref[plane, 0, :, half:start].astype(F32) for plane in range(4))
    vec_ref[...] = vectors.T[:8]


def unpack(parts, half, ring):
    shard, cols = parts.shape[2:]
    units = cols - half - 128
    vmem = pl.BlockSpec(memory_space=pltpu.VMEM)
    return pl.pallas_call(
        functools.partial(unpack_kernel, half, ring),
        out_shape=(
            jax.ShapeDtypeStruct((shard, 8 * units), F32),
            jax.ShapeDtypeStruct((shard, 2 * half), F32),
            jax.ShapeDtypeStruct((8, shard), F32),
        ),
        in_specs=[vmem],
        out_specs=(vmem,) * 3,
        compiler_params=pltpu.CompilerParams(vmem_limit_bytes=VMEM_BYTES),
        name="unpack",
    )(parts)


def swap_sum(keep, give, axis):
    return keep.astype(F32) + lax.ppermute(give.astype(BF16), axis, SWAP).astype(F32)


def gather_plane(block):
    return lax.all_gather(block, PLANE, axis=0, tiled=True)


def spread_plane(parts):
    return lax.all_to_all(parts.reshape(4, -1, parts.shape[1]), PLANE, 0, 0, tiled=True)


def after(array, earlier):
    first = earlier[(slice(0, 1),) * earlier.ndim].reshape((1,) * array.ndim)
    return array + (first.astype(F32) * 0.0).astype(array.dtype)


def hold_kernel(*refs):
    del refs


def hold(array, earlier, cost=1):
    anywhere = pl.BlockSpec(memory_space=pl.ANY)
    return pl.pallas_call(
        hold_kernel,
        out_shape=jax.ShapeDtypeStruct(array.shape, array.dtype),
        in_specs=[anywhere] * 2,
        out_specs=anywhere,
        input_output_aliases={0: 0},
        cost_estimate=pl.CostEstimate(flops=cost, bytes_accessed=1, transcendentals=0),
        name="hold",
    )(array, earlier)


def pick_at(parts, index, axis):
    return lax.dynamic_index_in_dim(parts, index, axis, keepdims=False)


def pick(parts, index):
    return lax.dynamic_index_in_dim(parts, index, 0, keepdims=False)


def two(own, other, index):
    return jnp.where(index == 0, jnp.stack([own, other]), jnp.stack([other, own]))


def body(
    tokens,
    positions,
    w_qkv,
    qv_bias,
    w_attn_out,
    attn_out_bias,
    norm1_gain,
    norm1_bias,
    w_in,
    in_bias,
    w_out,
    out_bias,
    norm2_gain,
    norm2_bias,
    cotangent,
):
    seq_count, row_count, width = tokens.shape
    outer = lax.axis_size("e")
    seq_size = 2 * outer * GROUPS
    devices = seq_size * 4
    shard = w_qkv.shape[0]
    ff_shard = w_out.shape[0]
    ring = 4 * outer
    group = lax.axis_index(("r", "x"))
    place = lax.axis_index(("y", "c"))
    units = 2 * ring * ff_shard
    y_at, c_at = lax.axis_index("y"), lax.axis_index("c")
    qkv_cols = 3 * GROUP_WIDTH

    half = width // 2

    with jax.named_scope("gather_ff_weights"):
        in_cols = (
            w_in.reshape(shard, 2, ring, 4, 2 * ff_shard)
            .transpose(3, 1, 0, 2, 4)
            .reshape(4, 2, shard, units)
        )
        attn_cols = w_attn_out.reshape(shard, 2, half).transpose(1, 0, 2)
        in_parts = jnp.concatenate(
            [in_cols, jnp.broadcast_to(attn_cols, (4, 2, shard, half))], axis=3
        ).reshape(8, shard, units + half)
        in_parts = lax.all_to_all(
            in_parts, ("x", "y", "c"), 0, 0, tiled=True
        ).reshape(8 * shard, units + half)
        out_halves = w_out.reshape(ff_shard, 2, half).transpose(1, 0, 2)
        out_cols = two(
            pick(out_halves, c_at), lax.ppermute(pick(out_halves, 1 - c_at), "c", SWAP), c_at
        ).reshape(2 * ff_shard, half)
        packed = jnp.concatenate([in_parts, out_cols], axis=1)

    with jax.named_scope("gather_qkv_weights"):
        own_pos = lax.dynamic_slice_in_dim(positions, place * row_count, row_count, 1)
        shorts = jnp.stack(
            [
                qv_bias[0],
                qv_bias[1],
                attn_out_bias,
                norm1_gain,
                norm1_bias,
                out_bias,
                norm2_gain,
                norm2_bias,
            ]
        )
        spare = 64
        wide = qkv_cols + spare
        high = max(shard, 16)
        shift_rows = -(-2 * ff_shard // spare)
        smalls = jnp.concatenate(
            [
                jnp.broadcast_to(jnp.pad(shorts, ((0, 0), (0, spare - shard))), (2, 8, spare)),
                (own_pos >> 7).astype(BF16)[:, None],
                (own_pos & 127).astype(BF16)[:, None],
                jnp.broadcast_to(
                    jnp.pad(in_bias, (0, shift_rows * spare - 2 * ff_shard)).reshape(
                        shift_rows, spare
                    ),
                    (2, shift_rows, spare),
                ),
                jnp.zeros((2, high - 10 - shift_rows, spare), BF16),
            ],
            axis=1,
        )
        columns = (
            w_qkv.reshape(shard, 3, GROUPS, GROUP_WIDTH)
            .transpose(2, 0, 1, 3)
            .reshape(1, GROUPS, shard, qkv_cols)
        )
        columns = jnp.pad(columns, ((0, 0), (0, 0), (0, high - shard), (0, 0)))
        parcel = jnp.concatenate(
            [
                jnp.broadcast_to(columns, (2, GROUPS, high, qkv_cols)),
                jnp.broadcast_to(smalls[:, None], (2, GROUPS, high, spare)),
            ],
            axis=3,
        ).reshape(8, high, wide)
        parcel = lax.all_to_all(after(parcel, in_parts), SEQ_GROUP, 0, 0, tiled=True)

    with jax.named_scope("gather_tokens"):
        s_at, r_at, x_at = (lax.axis_index(name) for name in SEQ_GROUP)
        chunk = two(
            pick(tokens, s_at), lax.ppermute(pick(tokens, 1 - s_at), "s", SWAP), s_at
        )
        chunk = two(chunk, lax.ppermute(chunk, "r", SWAP), r_at)
        chunk = hold(chunk, packed)
        chunk = two(chunk, lax.ppermute(chunk, "x", SWAP), x_at)
        chunk = chunk.transpose(2, 1, 0, 3, 4).reshape(8 * row_count, width)

    with jax.named_scope("gather_qkv_weights"):
        parcels = lax.all_gather(hold(parcel, chunk), CHUNKS, axis=0, tiled=False)
        parcels = parcels.reshape(outer, 2, 2, 2, 2, 2, high, wide)
        order = (3, 0, 4, 5, 1, 2)
        qkv_slice = (
            parcels[..., :shard, :qkv_cols].transpose(*order, 6, 7).reshape(width, qkv_cols)
        )
        smalls = parcels[..., qkv_cols:]
        vectors = (
            smalls[..., :8, :shard].transpose(6, *order, 7).reshape(8, width).astype(F32)
        )
        pos_parts = smalls[..., 8:10, :row_count].astype(F32)
        chunk_pos = (pos_parts[..., 0, :] * 128.0 + pos_parts[..., 1, :]).reshape(
            outer, 2, 2, 8 * row_count
        )
        in_shift = pick_at(
            pick_at(smalls[..., 10 : 10 + shift_rows, :], x_at, 1), y_at, 1
        )
        in_shift = (
            in_shift.transpose(1, 0, 2, 3, 4, 5)
            .reshape(seq_size, shift_rows * spare)[:, : 2 * ff_shard]
            .reshape(2, units)
            .astype(F32)
        )

    with jax.named_scope("gather_ff_weights"):
        packed = lax.all_gather(packed, RING, axis=0, tiled=True)
        core = c_at.reshape(1).astype(jnp.int32)

    with jax.named_scope("project"):
        qv_slice = lax.dynamic_slice_in_dim(vectors[:2], group * GROUP_WIDTH, GROUP_WIDTH, 1)
        column_bias = jnp.concatenate(
            [qv_slice[0], jnp.zeros((GROUP_WIDTH,), F32), qv_slice[1]]
        )
        queries = (
            jnp.dot(chunk, qkv_slice[:, :GROUP_WIDTH], preferred_element_type=F32)
            + column_bias[:GROUP_WIDTH]
        ).astype(BF16)
        own_kv = (
            jnp.dot(chunk, qkv_slice[:, GROUP_WIDTH:], preferred_element_type=F32)
            + column_bias[GROUP_WIDTH:]
        ).astype(BF16)
    with jax.named_scope("gather_kv"):
        if outer > 1:
            own_kv = lax.all_gather(own_kv, "e", axis=0, tiled=True)
        y_kv = lax.ppermute(own_kv, "y", SWAP)
        key_values = [own_kv, lax.ppermute(own_kv, "c", SWAP)]
    ordered_pos = jnp.stack(
        [
            lax.dynamic_index_in_dim(
                lax.dynamic_index_in_dim(chunk_pos, y_at ^ ky, 1, keepdims=False),
                c_at ^ kc,
                1,
                keepdims=False,
            )
            for ky in (0, 1)
            for kc in (0, 1)
        ]
    )
    query_pos = lax.dynamic_index_in_dim(ordered_pos[0], lax.axis_index("e"), 0, keepdims=True)
    key_pos = ordered_pos.reshape(4 * outer, 8 * row_count)
    head_ids = group * GROUP_HEADS + jnp.arange(GROUP_HEADS)
    slopes = 2.0 ** (-8.0 * (head_ids + 1).astype(F32) / HEADS) * LOG2E

    with jax.named_scope("attention"):
        span = outer
        parts = ((0, 2), (2, 3), (3, 4))
        state = None
        for number, (first, last) in enumerate(parts):
            state = attend(
                slopes,
                queries,
                query_pos,
                key_pos[first * span : last * span],
                key_values[first:last],
                state,
                last=last == 4,
                earlier=(vectors, in_shift) if number == 1 else (),
            )
            if number == 0:
                y_kv = hold(y_kv, state[0])
                key_values += [y_kv, lax.ppermute(y_kv, "c", SWAP)]
        attended, log_sums, attended_low = state

    with jax.named_scope("return_attended"):
        returned = lax.all_to_all(
            attended_low.reshape(8, row_count, GROUP_WIDTH), SEQ_GROUP, 0, 0, tiled=True
        )
    with jax.named_scope("first_norm"):
        packed = hold(packed, returned)
        attn_own = packed[:, units : units + half]
        attn_swap = lax.ppermute(attn_own, "c", SWAP)
        hidden_low, hidden, normal, scale, attn_full = first_norm(
            core,
            returned,
            tokens.reshape(2 * row_count, width),
            vectors,
            attn_own,
            attn_swap,
            slice(0, half),
        )
        packed = hold(packed, hidden_low)
        swapped = lax.ppermute(packed, "c", SWAP)
    with jax.named_scope("gather_hidden"):
        hidden_group = gather_plane(hidden_low)
    with jax.named_scope("ff_forward"):
        activated_low, slope, gelu, ff_parts, in_slice, out_slice = ff_forward(
            core,
            hidden_group,
            in_shift,
            packed,
            swapped,
            slice(0, units),
            slice(units + half, units + width),
        )
    with jax.named_scope("sum_ff"):
        ff_parts = spread_plane(ff_parts)
    with jax.named_scope("second_norm"):
        result, second_grad, ff_grad, sums = second_norm(
            ff_parts, hidden, cotangent.reshape(2 * row_count, width), vectors
        )
    with jax.named_scope("gather_ff_grad"):
        ff_grads = gather_plane(ff_grad)
    with jax.named_scope("ff_backward"):
        joined_grad, hidden_parts, grad_in_shift, grad_halves = ff_backward(
            ff_grads, slope, gelu, in_slice, out_slice
        )
    with jax.named_scope("sum_hidden_grad"):
        hidden_parts = spread_plane(hidden_parts)
    with jax.named_scope("ff_weight_grads"):
        keep, give = ff_grads_of(core, activated_low, grad_halves, hidden_group, joined_grad)
        ff_keep, ff_give = keep, give
    with jax.named_scope("first_norm_back"):
        first_grad, out_grad, keep, give = first_back(
            core,
            hidden_parts,
            second_grad,
            normal,
            scale,
            vectors,
            attn_full,
            sums,
            returned,
            ff_keep,
        )
    with jax.named_scope("send_out_grad"):
        out_grads = lax.all_to_all(out_grad, SEQ_GROUP, 0, 0, tiled=True).reshape(
            8 * row_count, GROUP_WIDTH
        )
    with jax.named_scope("attn_weight_grad"):
        rows = jnp.concatenate(
            [swap_sum(keep, give, "c"), swap_sum(ff_keep, ff_give, "c")], axis=1
        ).astype(BF16)
        rows = hold(rows, out_grads)
        row_sums = lax.psum_scatter(rows, RING, scatter_dimension=0, tiled=True)

    with jax.named_scope("attention_back"):
        state, c_part, y_part, cy_part = attend_back(
            slopes,
            queries,
            query_pos,
            key_pos[span:],
            out_grads,
            attended,
            log_sums,
            key_values[1:],
            None,
            last=False,
            earlier=(rows,),
        )
        y_sum = swap_sum(y_part, cy_part, "c").astype(BF16)
        query_grads, own_part = attend_back(
            slopes,
            queries,
            query_pos,
            key_pos[:span],
            out_grads,
            attended,
            log_sums,
            key_values[:1],
            state,
            last=True,
            earlier=(y_sum,),
        )
    with jax.named_scope("sum_kv_grads"):
        from_c = lax.ppermute(c_part, "c", SWAP)
        from_y = lax.ppermute(y_sum, "y", SWAP)
        if outer > 1:
            total = own_part.astype(F32) + from_c.astype(F32) + from_y.astype(F32)
            own_part = lax.psum_scatter(
                total, "e", scatter_dimension=0, tiled=True
            ).astype(BF16)
            from_c = from_y = jnp.zeros_like(own_part)

    with jax.named_scope("input_back"):
        spot = jnp.stack([c_at, y_at, x_at]).astype(jnp.int32)
        input_keep, input_give, qkv_grad = input_back(
            spot, query_grads, own_part, from_c, from_y, qkv_slice
        )
    with jax.named_scope("qkv_weight_grad"):
        keep, give = qkv_weight(
            spot,
            chunk,
            qkv_grad,
            grad_in_shift.reshape(seq_size, 2 * ff_shard),
        )
        bundle = swap_sum(keep, give, "c").astype(BF16)
        from_x = lax.ppermute(input_give, "x", SWAP)
        parts = (hold(input_keep, bundle).astype(F32) + from_x.astype(F32)).reshape(
            2, 2, row_count, width
        )
        bundle = swap_sum(pick(bundle, y_at), pick(bundle, 1 - y_at), "y").astype(BF16)
        ends = width // 4 + seq_size
        shares = jnp.concatenate(
            [
                bundle[: width // 4].reshape(seq_size, shard, qkv_cols),
                jnp.broadcast_to(bundle[ends : ends + 1], (seq_size, 1, qkv_cols)),
                bundle[width // 4 : ends][:, None],
                jnp.zeros((seq_size, 6, qkv_cols), BF16),
            ],
            axis=1,
        )
    with jax.named_scope("input_grad"):
        from_r = lax.ppermute(pick_at(parts, 1 - r_at, 1).astype(BF16), "r", SWAP)
        parts = hold(pick_at(parts, r_at, 1), shares) + from_r.astype(F32)
        input_grad = first_grad.reshape(2, row_count, width) + two(
            pick(parts, s_at),
            lax.ppermute(pick(parts, 1 - s_at).astype(BF16), "s", SWAP).astype(F32),
            s_at,
        )
    with jax.named_scope("qkv_weight_grad"):
        shares = lax.all_to_all(shares, SEQ_AXIS, 0, 0, tiled=True)
    with jax.named_scope("ff_weight_grads"):
        own_cols = half + 128 + units
        row_sums = hold(row_sums, shares)
        exchanged = lax.all_to_all(
            row_sums[:, :own_cols].reshape(8, shard, own_cols), ("x", "y", "c"), 0, 0, tiled=True
        ).reshape(4, 2, shard, own_cols)
        out_sums = row_sums[:, own_cols:].reshape(2, ff_shard, half)
        grad_w_out = (
            two(
                pick(out_sums, c_at),
                lax.ppermute(pick(out_sums, 1 - c_at), "c", SWAP),
                c_at,
            )
            .transpose(1, 0, 2)
            .reshape(ff_shard, width)
            .astype(F32)
        )
        if outer == 1:
            grad_w_in, grad_w_attn, vector_grads = unpack(exchanged, half, ring)
        else:
            grad_w_in = (
                exchanged[..., half + 128 :]
                .reshape(4, 2, shard, ring, 2 * ff_shard)
                .transpose(2, 1, 3, 0, 4)
                .reshape(shard, 2 * devices * ff_shard)
                .astype(F32)
            )
            grad_w_attn = (
                jnp.sum(exchanged[..., :half].astype(F32), axis=0)
                .transpose(1, 0, 2)
                .reshape(shard, width)
            )
            vector_grads = jnp.sum(exchanged[:, 0, :, half : half + 8].astype(F32), axis=0).T
    with jax.named_scope("qkv_weight_grad"):
        shares = shares.astype(F32)
        totals = jnp.sum(shares.reshape(2 * outer, GROUPS, shard + 8, qkv_cols), axis=0)
        grad_w_qkv = (
            totals[:, :shard]
            .reshape(GROUPS, shard, 3, GROUP_WIDTH)
            .transpose(1, 2, 0, 3)
            .reshape(shard, 3 * width)
        )
        sums = totals[:, shard].reshape(GROUPS, 3, GROUP_WIDTH).transpose(1, 0, 2).reshape(3, width)
        grad_qv = lax.dynamic_slice_in_dim(sums[0::2], lax.axis_index(EVERY) * shard, shard, 1)
        grad_in_bias = jnp.sum(totals[:, shard + 1, : 2 * ff_shard], axis=0)

    return (
        result.reshape(2, row_count, width).astype(BF16),
        input_grad,
        grad_w_qkv,
        grad_qv,
        grad_w_attn,
        vector_grads[0],
        vector_grads[1],
        vector_grads[2],
        grad_w_in,
        grad_in_bias,
        grad_w_out,
        vector_grads[3],
        vector_grads[4],
        vector_grads[5],
    )


def solution(mesh):
    seq_size = mesh.shape["seq"]
    split = Mesh(mesh.devices.reshape(2, seq_size // 8, 2, 2, 2, 2), EVERY)
    tokens_at = P(None, EVERY, None)
    rows_at = P(EVERY, None)
    vector_at = P(EVERY)
    return jax.shard_map(
        body,
        mesh=split,
        in_specs=(
            tokens_at,
            P(None, SEQ_AXIS),
            rows_at,
            P(None, EVERY),
            rows_at,
            vector_at,
            vector_at,
            vector_at,
            rows_at,
            vector_at,
            rows_at,
            vector_at,
            vector_at,
            vector_at,
            tokens_at,
        ),
        out_specs=(
            tokens_at,
            tokens_at,
            rows_at,
            P(None, EVERY),
            rows_at,
            vector_at,
            vector_at,
            vector_at,
            rows_at,
            vector_at,
            rows_at,
            vector_at,
            vector_at,
            vector_at,
        ),
        check_vma=False,
    )
```

```python
import functools

import jax
import jax.numpy as jnp
from jax import lax
from jax.experimental import pallas as pl
from jax.experimental.pallas import tpu as pltpu
from jax.sharding import Mesh
from jax.sharding import PartitionSpec as P

HEADS = 12
HEAD_DIM = 64
GROUPS = 4
GROUP_HEADS = HEADS // GROUPS
GROUP_WIDTH = GROUP_HEADS * HEAD_DIM
EPSILON = 1e-12
SCORE_SCALE = 0.125
LOG2E = 1.4426950408889634
LOWEST = -1e30
GRAD_TILE = 256
KEY_BLOCK = 512
FF_TILE = 256
SEQ_GROUP = ("s", "r", "x")
CHUNKS = ("e", "y", "c")
RING = ("s", "e", "r")
PLANE = ("x", "y")
SEQ_AXIS = ("s", "e", "r", "x")
EVERY = ("s", "e", "r", "x", "y", "c")
SWAP = ((0, 1), (1, 0))
BF16 = jnp.bfloat16
F32 = jnp.float32
VMEM_BYTES = 60 * 2**20


def nt(a, b):
    return lax.dot_general(a, b, (((1,), (1,)), ((), ())), preferred_element_type=F32)


def tn(a, b):
    return lax.dot_general(a, b, (((0,), (0,)), ((), ())), preferred_element_type=F32)


def nn(a, b):
    return lax.dot_general(a, b, (((1,), (0,)), ((), ())), preferred_element_type=F32)


def head_cols(head, base=0):
    return slice(base + head * HEAD_DIM, base + (head + 1) * HEAD_DIM)


def log2_scores(keys, queries, slope, key_pos, query_pos):
    products = nt(keys, queries)
    distances = jnp.abs(key_pos * slope - query_pos * slope)
    return products * (SCORE_SCALE * LOG2E) - distances


def column(row):
    return jnp.broadcast_to(row, (8, row.shape[1])).T[:, :1]


def key_blocks(kv_refs):
    start = 0
    for piece in kv_refs:
        yield piece, start
        start += piece.shape[0]


def turn_positions(pk_ref, column_ref):
    length = pk_ref.shape[1]

    def turn(row, carry):
        at = pl.ds(pl.multiple_of(row * length, length), length)
        column_ref[at, :] = column(pk_ref[pl.ds(row, 1), :])
        return carry

    lax.fori_loop(0, pk_ref.shape[0], turn, 0)


def attend_kernel(deps, count, first, last, slopes_ref, q_ref, pq_ref, pk_ref, *refs):
    refs = refs[deps:]
    kv_refs, refs = refs[:count], refs[count:]
    if not first:
        (sum_in_ref, stat_in_ref), refs = refs[:2], refs[2:]
    sum_ref, stat_ref = refs[:2]
    column_ref = refs[-1]
    rows = q_ref.shape[0]
    query_pos = pq_ref[...]
    turn_positions(pk_ref, column_ref)
    for head in range(GROUP_HEADS):
        slope = slopes_ref[head]
        queries = q_ref[:, head_cols(head)]
        if first:
            carry = (
                jnp.full((1, rows), LOWEST, F32),
                jnp.zeros((1, rows), F32),
                jnp.zeros((HEAD_DIM, rows), F32),
            )
        else:
            carry = (
                stat_in_ref[head : head + 1, :],
                stat_in_ref[GROUP_HEADS + head : GROUP_HEADS + head + 1, :],
                sum_in_ref[head_cols(head), :],
            )
        for kv_ref, start in key_blocks(kv_refs):

            def visit(block, carry, kv_ref=kv_ref, start=start):
                top, total, summed = carry
                at = pl.ds(pl.multiple_of(block * KEY_BLOCK, KEY_BLOCK), KEY_BLOCK)
                pos_at = pl.ds(
                    pl.multiple_of(start + block * KEY_BLOCK, KEY_BLOCK), KEY_BLOCK
                )
                keys = kv_ref[at, head_cols(head)]
                values = kv_ref[at, head_cols(head, GROUP_WIDTH)]
                scores = log2_scores(keys, queries, slope, column_ref[pos_at, :], query_pos)
                new_top = jnp.maximum(top, jnp.max(scores, axis=0, keepdims=True))
                weights = jnp.exp2(scores - new_top)
                shrink = jnp.exp2(top - new_top)
                total = total * shrink + jnp.sum(weights, axis=0, keepdims=True)
                summed = summed * shrink + tn(values, weights.astype(BF16))
                return new_top, total, summed

            carry = lax.fori_loop(0, kv_ref.shape[0] // KEY_BLOCK, visit, carry)
        top, total, summed = carry
        if last:
            attended = summed / total
            sum_ref[head_cols(head), :] = attended
            refs[2][:, head_cols(head)] = attended.T.astype(BF16)
            stat_ref[head : head + 1, :] = top + jnp.log2(total)
        else:
            sum_ref[head_cols(head), :] = summed
            stat_ref[head : head + 1, :] = top
            stat_ref[GROUP_HEADS + head : GROUP_HEADS + head + 1, :] = total


def attend(slopes, queries, query_pos, key_pos, key_values, state, last, earlier):
    rows, length = queries.shape[0], key_pos.size
    vmem = pl.BlockSpec(memory_space=pltpu.VMEM)
    count = len(key_values)
    first = state is None
    state = () if first else state
    outs = [
        jax.ShapeDtypeStruct((GROUP_WIDTH, rows), F32),
        jax.ShapeDtypeStruct((GROUP_HEADS * (1 if last else 2), rows), F32),
    ]
    if last:
        outs.append(jax.ShapeDtypeStruct((rows, GROUP_WIDTH), BF16))
    return pl.pallas_call(
        functools.partial(attend_kernel, len(earlier), count, first, last),
        out_shape=tuple(outs),
        in_specs=[pl.BlockSpec(memory_space=pltpu.SMEM)]
        + [vmem] * 3
        + [pl.BlockSpec(memory_space=pl.ANY)] * len(earlier)
        + [vmem] * (count + len(state)),
        out_specs=(vmem,) * len(outs),
        scratch_shapes=[pltpu.VMEM((length, 1), F32)],
        compiler_params=pltpu.CompilerParams(vmem_limit_bytes=VMEM_BYTES),
        cost_estimate=pl.CostEstimate(
            flops=64 * rows * length * GROUP_WIDTH,
            bytes_accessed=rows * length,
            transcendentals=rows * length * GROUP_HEADS,
        ),
        name="attend",
    )(slopes, queries, query_pos, key_pos, *earlier, *key_values, *state)


def attend_back_kernel(
    deps, count, first, last, slopes_ref, q_ref, pq_ref, pk_ref, do_ref, out_ref, lse_ref, *refs
):
    refs = refs[deps:]
    kv_refs, refs = refs[:count], refs[count:]
    if not first:
        dq_in_ref, refs = refs[0], refs[1:]
    dq_ref, dkv_refs, column_ref = refs[0], refs[1 : count + 1], refs[-1]
    rows = q_ref.shape[0]
    query_pos = pq_ref[...]
    turn_positions(pk_ref, column_ref)
    for head in range(GROUP_HEADS):
        slope = slopes_ref[head]
        queries = q_ref[:, head_cols(head)]
        out_grads = do_ref[:, head_cols(head)]
        log_sum = lse_ref[head : head + 1, :]
        delta = jnp.sum(
            out_grads.astype(F32).T * out_ref[head_cols(head), :], axis=0, keepdims=True
        )
        if first:
            query_grads = jnp.zeros((HEAD_DIM, rows), F32)
        else:
            query_grads = dq_in_ref[head_cols(head), :]
        for (kv_ref, start), dkv_ref in zip(key_blocks(kv_refs), dkv_refs):

            def visit(block, query_grads, kv_ref=kv_ref, start=start, dkv_ref=dkv_ref):
                at = pl.ds(pl.multiple_of(block * KEY_BLOCK, KEY_BLOCK), KEY_BLOCK)
                pos_at = pl.ds(
                    pl.multiple_of(start + block * KEY_BLOCK, KEY_BLOCK), KEY_BLOCK
                )
                keys = kv_ref[at, head_cols(head)]
                values = kv_ref[at, head_cols(head, GROUP_WIDTH)]
                scores = log2_scores(keys, queries, slope, column_ref[pos_at, :], query_pos)
                probs = jnp.exp2(scores - log_sum)
                prob_grads = nt(values, out_grads)
                score_grads = (probs * (prob_grads - delta)).astype(BF16)
                dkv_ref[at, head_cols(head, GROUP_WIDTH)] = nn(
                    probs.astype(BF16), out_grads
                ).astype(BF16)
                dkv_ref[at, head_cols(head)] = (nn(score_grads, queries) * SCORE_SCALE).astype(
                    BF16
                )
                return query_grads + tn(keys, score_grads)

            query_grads = lax.fori_loop(0, kv_ref.shape[0] // KEY_BLOCK, visit, query_grads)
        if last:
            dq_ref[:, head_cols(head)] = (query_grads * SCORE_SCALE).T.astype(BF16)
        else:
            dq_ref[head_cols(head), :] = query_grads


def attend_back(
    slopes,
    queries,
    query_pos,
    key_pos,
    out_grads,
    attended,
    log_sums,
    key_values,
    state,
    last,
    earlier,
):
    rows, length = queries.shape[0], key_pos.size
    vmem = pl.BlockSpec(memory_space=pltpu.VMEM)
    count = len(key_values)
    first = state is None
    state = () if first else (state,)
    query_out = (
        jax.ShapeDtypeStruct((rows, GROUP_WIDTH), BF16)
        if last
        else jax.ShapeDtypeStruct((GROUP_WIDTH, rows), F32)
    )
    return pl.pallas_call(
        functools.partial(attend_back_kernel, len(earlier), count, first, last),
        out_shape=(query_out,)
        + tuple(jax.ShapeDtypeStruct(piece.shape, BF16) for piece in key_values),
        in_specs=[pl.BlockSpec(memory_space=pltpu.SMEM)]
        + [vmem] * 6
        + [pl.BlockSpec(memory_space=pl.ANY)] * len(earlier)
        + [vmem] * (count + len(state)),
        out_specs=(vmem,) * (1 + count),
        scratch_shapes=[pltpu.VMEM((length, 1), F32)],
        compiler_params=pltpu.CompilerParams(vmem_limit_bytes=VMEM_BYTES),
        cost_estimate=pl.CostEstimate(
            flops=84 * rows * length * GROUP_WIDTH,
            bytes_accessed=rows * length,
            transcendentals=rows * length * GROUP_HEADS,
        ),
        name="attend_back",
    )(
        slopes,
        queries,
        query_pos,
        key_pos,
        out_grads,
        attended,
        log_sums,
        *earlier,
        *key_values,
        *state,
    )


def assemble(core_ref, own_ref, swap_ref, columns, target, sems):
    core = core_ref[0]
    copies = []
    for which, (piece, half) in enumerate(((own_ref, core), (swap_ref, 1 - core))):
        copy = pltpu.make_async_copy(piece.at[:, columns], target.at[half], sems.at[which])
        copy.start()
        copies.append(copy)
    return copies


def merged(parts_ref):
    return jnp.concatenate(
        [
            jnp.concatenate(
                [parts_ref[seq * GROUPS + group] for group in range(GROUPS)], axis=1
            )
            for seq in range(2)
        ]
    )


def first_norm_kernel(
    columns,
    core_ref,
    mixed_ref,
    rows_ref,
    vec_ref,
    own_ref,
    swap_ref,
    low_ref,
    hidden_ref,
    normal_ref,
    scale_ref,
    weight_ref,
    sems,
):
    for copy in assemble(core_ref, own_ref, swap_ref, columns, weight_ref, sems):
        copy.wait()
    mixed = merged(mixed_ref)
    lin = jnp.concatenate([nn(mixed, weight_ref[0]), nn(mixed, weight_ref[1])], axis=1)
    total = rows_ref[...].astype(F32) + (lin + vec_ref[2:3, :])
    normal, scale = normalised(total)
    hidden = normal * vec_ref[3:4, :] + vec_ref[4:5, :]
    low_ref[...] = hidden.astype(BF16)
    hidden_ref[...] = hidden
    normal_ref[...] = normal
    scale_ref[...] = scale


def normalised(values):
    centred = values - jnp.mean(values, axis=1, keepdims=True)
    variance = jnp.mean(centred * centred, axis=1, keepdims=True)
    scale = lax.rsqrt(variance + EPSILON)
    return centred * scale, scale


def norm_back(grads, normal, scale, gain):
    scaled = grads * gain
    return (
        scaled
        - jnp.mean(scaled, axis=1, keepdims=True)
        - normal * jnp.mean(scaled * normal, axis=1, keepdims=True)
    ) * scale


def column_sum(values):
    return jnp.sum(values, axis=0, keepdims=True)


def first_norm(core, mixed, rows, vectors, own, swap, columns):
    tokens, width = rows.shape
    vmem = pl.BlockSpec(memory_space=pltpu.VMEM)
    half = columns.stop - columns.start
    return pl.pallas_call(
        functools.partial(first_norm_kernel, columns),
        out_shape=(
            jax.ShapeDtypeStruct((tokens, width), BF16),
            jax.ShapeDtypeStruct((tokens, width), F32),
            jax.ShapeDtypeStruct((tokens, width), F32),
            jax.ShapeDtypeStruct((tokens, 1), F32),
            jax.ShapeDtypeStruct((2, width, half), BF16),
        ),
        in_specs=[pl.BlockSpec(memory_space=pltpu.SMEM)]
        + [vmem] * 3
        + [pl.BlockSpec(memory_space=pl.ANY)] * 2,
        out_specs=(vmem,) * 5,
        scratch_shapes=[pltpu.SemaphoreType.DMA((2,))],
        compiler_params=pltpu.CompilerParams(vmem_limit_bytes=VMEM_BYTES),
        cost_estimate=pl.CostEstimate(
            flops=64 * tokens * width * width, bytes_accessed=4 * width * width, transcendentals=0
        ),
        name="first_norm",
    )(core, mixed, rows, vectors, own, swap)


def ff_forward_kernel(
    in_columns,
    out_columns,
    core_ref,
    hidden_ref,
    bias_ref,
    own_ref,
    swap_ref,
    act_ref,
    slope_ref,
    gelu_ref,
    parts_ref,
    w_in_ref,
    w_out_ref,
    sems,
):
    in_copies = assemble(core_ref, own_ref, swap_ref, in_columns, w_in_ref, sems.at[0])
    out_copies = assemble(core_ref, own_ref, swap_ref, out_columns, w_out_ref, sems.at[1])
    for copy in in_copies:
        copy.wait()
    tokens = hidden_ref.shape[0]

    def expand(tile, carry):
        at = pl.ds(pl.multiple_of(tile * FF_TILE, FF_TILE), FF_TILE)
        rows = hidden_ref[at, :]
        gate = nn(rows, w_in_ref[0]) + bias_ref[0:1, :]
        up = nn(rows, w_in_ref[1]) + bias_ref[1:2, :]
        cdf = 0.5 * (1.0 + lax.erf(gate * (0.5**0.5)))
        density = jnp.exp(-0.5 * gate * gate) * 0.3989422804014327
        gelu = gate * cdf
        act_ref[at, :] = (gelu * up).astype(BF16)
        gelu_ref[at, :] = gelu.astype(BF16)
        slope_ref[at, :] = (up * (cdf + gate * density)).astype(BF16)
        return carry

    lax.fori_loop(0, tokens // FF_TILE, expand, 0)
    for copy in out_copies:
        copy.wait()

    def contract(tile, carry):
        at = pl.ds(pl.multiple_of(tile * FF_TILE, FF_TILE), FF_TILE)
        rows = act_ref[at, :]
        parts_ref[at, :] = jnp.concatenate(
            [nn(rows, w_out_ref[0]), nn(rows, w_out_ref[1])], axis=1
        ).astype(BF16)
        return carry

    lax.fori_loop(0, tokens // FF_TILE, contract, 0)


def ff_forward(core, hidden, bias, own, swap, in_columns, out_columns):
    tokens, width = hidden.shape
    units = bias.shape[1]
    vmem = pl.BlockSpec(memory_space=pltpu.VMEM)
    return pl.pallas_call(
        functools.partial(ff_forward_kernel, in_columns, out_columns),
        out_shape=(
            jax.ShapeDtypeStruct((tokens, units), BF16),
            jax.ShapeDtypeStruct((tokens, units), BF16),
            jax.ShapeDtypeStruct((tokens, units), BF16),
            jax.ShapeDtypeStruct((tokens, width), BF16),
            jax.ShapeDtypeStruct((2, width, units), BF16),
            jax.ShapeDtypeStruct((2, units, width // 2), BF16),
        ),
        in_specs=[pl.BlockSpec(memory_space=pltpu.SMEM)]
        + [vmem] * 2
        + [pl.BlockSpec(memory_space=pl.ANY)] * 2,
        out_specs=(vmem,) * 6,
        scratch_shapes=[pltpu.SemaphoreType.DMA((2, 2))],
        compiler_params=pltpu.CompilerParams(vmem_limit_bytes=VMEM_BYTES),
        cost_estimate=pl.CostEstimate(
            flops=32 * tokens * width * units,
            bytes_accessed=6 * width * units,
            transcendentals=2 * tokens * units,
        ),
        name="ff_forward",
    )(core, hidden, bias, own, swap)


def second_norm_kernel(
    parts_ref, hidden_ref, cotangent_ref, vec_ref, result_ref, grad_ref, low_ref, sums_ref
):
    lin = jnp.sum(parts_ref[...].astype(F32), axis=0) + vec_ref[5:6, :]
    normal, scale = normalised(hidden_ref[...] + lin)
    gain = vec_ref[6:7, :]
    result_ref[...] = (normal * gain + vec_ref[7:8, :]).astype(BF16)
    grads = cotangent_ref[...].astype(F32)
    back = norm_back(grads, normal, scale, gain)
    low = back.astype(BF16)
    grad_ref[...] = back
    low_ref[...] = low
    sums_ref[...] = jnp.concatenate(
        [
            column_sum(low.astype(F32)),
            column_sum(grads * normal),
            column_sum(grads),
            jnp.zeros((5, back.shape[1]), F32),
        ]
    )


def second_norm(parts, hidden, cotangent, vectors):
    tokens, width = hidden.shape
    vmem = pl.BlockSpec(memory_space=pltpu.VMEM)
    return pl.pallas_call(
        second_norm_kernel,
        out_shape=(
            jax.ShapeDtypeStruct((tokens, width), BF16),
            jax.ShapeDtypeStruct((tokens, width), F32),
            jax.ShapeDtypeStruct((tokens, width), BF16),
            jax.ShapeDtypeStruct((8, width), F32),
        ),
        in_specs=[vmem] * 4,
        out_specs=(vmem,) * 4,
        compiler_params=pltpu.CompilerParams(vmem_limit_bytes=VMEM_BYTES),
        cost_estimate=pl.CostEstimate(
            flops=20000 * tokens * width, bytes_accessed=20 * tokens * width, transcendentals=0
        ),
        name="second_norm",
    )(parts, hidden, cotangent, vectors)


def ff_backward_kernel(
    grad_ref, slope_ref, gelu_ref, w_in_ref, w_out_ref, joined_ref, parts_ref, bias_ref, half_ref
):
    tokens, width = grad_ref.shape
    half = width // 2
    bias_ref[...] = jnp.zeros_like(bias_ref)

    def visit(tile, carry):
        at = pl.ds(pl.multiple_of(tile * FF_TILE, FF_TILE), FF_TILE)
        left, right = grad_ref[at, :half], grad_ref[at, half:]
        half_ref[0, at, :] = left
        half_ref[1, at, :] = right
        act_grad = nt(left, w_out_ref[0]) + nt(right, w_out_ref[1])
        for which, factor in ((0, slope_ref), (1, gelu_ref)):
            joined = (act_grad * factor[at, :].astype(F32)).astype(BF16)
            joined_ref[which, at, :] = joined
            bias_ref[which : which + 1, :] += column_sum(joined.astype(F32))
        parts_ref[at, :] = (
            nt(joined_ref[0, at, :], w_in_ref[0]) + nt(joined_ref[1, at, :], w_in_ref[1])
        ).astype(BF16)
        return carry

    lax.fori_loop(0, tokens // FF_TILE, visit, 0)


def ff_backward(grads, slope, gelu, w_in, w_out):
    tokens, width = grads.shape
    units = slope.shape[1]
    vmem = pl.BlockSpec(memory_space=pltpu.VMEM)
    return pl.pallas_call(
        ff_backward_kernel,
        out_shape=(
            jax.ShapeDtypeStruct((2, tokens, units), BF16),
            jax.ShapeDtypeStruct((tokens, width), BF16),
            jax.ShapeDtypeStruct((2, units), F32),
            jax.ShapeDtypeStruct((2, tokens, width // 2), BF16),
        ),
        in_specs=[vmem] * 5,
        out_specs=(vmem,) * 4,
        compiler_params=pltpu.CompilerParams(vmem_limit_bytes=VMEM_BYTES),
        cost_estimate=pl.CostEstimate(
            flops=32 * tokens * width * units,
            bytes_accessed=6 * width * units,
            transcendentals=0,
        ),
        name="ff_backward",
    )(grads, slope, gelu, w_in, w_out)


def ff_grads_kernel(core_ref, act_ref, half_ref, hidden_ref, joined_ref, keep_ref, give_ref):
    core = core_ref[0]
    units = joined_ref.shape[2]

    def visit(tile, carry):
        at = pl.ds(pl.multiple_of(tile * GRAD_TILE, GRAD_TILE), GRAD_TILE)
        hidden = hidden_ref[:, at]
        act = act_ref[:, at]
        give_ref[at, :units] = tn(hidden, joined_ref[1 - core]).astype(BF16)
        give_ref[at, units:] = tn(act, half_ref[1 - core]).astype(BF16)
        keep_ref[at, :units] = tn(hidden, joined_ref[core]).astype(BF16)
        keep_ref[at, units:] = tn(act, half_ref[core]).astype(BF16)
        return carry

    lax.fori_loop(0, hidden_ref.shape[1] // GRAD_TILE, visit, 0)


def ff_grads_of(core, act, halves, hidden, joined):
    width = hidden.shape[1]
    cols = joined.shape[2] + halves.shape[2]
    vmem = pl.BlockSpec(memory_space=pltpu.VMEM)
    return pl.pallas_call(
        ff_grads_kernel,
        out_shape=(jax.ShapeDtypeStruct((width, cols), BF16),) * 2,
        in_specs=[pl.BlockSpec(memory_space=pltpu.SMEM)] + [vmem] * 4,
        out_specs=(vmem,) * 2,
        compiler_params=pltpu.CompilerParams(vmem_limit_bytes=VMEM_BYTES),
        cost_estimate=pl.CostEstimate(flops=6 * 10**9, bytes_accessed=10**4, transcendentals=0),
        name="ff_grads",
    )(core, act, halves, hidden, joined)


def first_back_kernel(
    core_ref,
    parts_ref,
    second_ref,
    normal_ref,
    scale_ref,
    vec_ref,
    weight_ref,
    sums_ref,
    mixed_ref,
    _,
    grad_ref,
    out_ref,
    keep_ref,
    give_ref,
):
    tokens, width = second_ref.shape
    half, count = width // 2, tokens // 2
    normal = normal_ref[...]
    grads = second_ref[...] + jnp.sum(parts_ref[...].astype(F32), axis=0)
    back = norm_back(grads, normal, scale_ref[...], vec_ref[3:4, :])
    low = back.astype(BF16)
    grad_ref[...] = back
    out_grad = nt(low[:, :half], weight_ref[0]) + nt(low[:, half:], weight_ref[1])
    for seq in range(2):
        for group in range(GROUPS):
            out_ref[seq * GROUPS + group] = out_grad[
                seq * count : (seq + 1) * count, group * GROUP_WIDTH : (group + 1) * GROUP_WIDTH
            ].astype(BF16)
    rows = jnp.concatenate(
        [
            column_sum(low.astype(F32)),
            column_sum(grads * normal),
            column_sum(grads),
            sums_ref[0:3, :],
            jnp.zeros((122, width), F32),
        ]
    )
    turned = rows.T.astype(BF16)
    keep_ref[:, half:] = turned
    give_ref[:, half:] = turned
    mixed = merged(mixed_ref)
    left = tn(mixed, low[:, :half]).astype(BF16)
    right = tn(mixed, low[:, half:]).astype(BF16)
    own_left = core_ref[0] == 0
    keep_ref[:, :half] = jnp.where(own_left, left, right)
    give_ref[:, :half] = jnp.where(own_left, right, left)


def first_back(core, parts, second_grad, normal, scale, vectors, weight, sums, mixed, earlier):
    tokens, width = second_grad.shape
    vmem = pl.BlockSpec(memory_space=pltpu.VMEM)
    return pl.pallas_call(
        first_back_kernel,
        out_shape=(
            jax.ShapeDtypeStruct((tokens, width), F32),
            jax.ShapeDtypeStruct((2 * GROUPS, tokens // 2, GROUP_WIDTH), BF16),
            jax.ShapeDtypeStruct((width, width // 2 + 128), BF16),
            jax.ShapeDtypeStruct((width, width // 2 + 128), BF16),
        ),
        in_specs=[pl.BlockSpec(memory_space=pltpu.SMEM)]
        + [vmem] * 8
        + [pl.BlockSpec(memory_space=pl.ANY)],
        out_specs=(vmem,) * 4,
        compiler_params=pltpu.CompilerParams(vmem_limit_bytes=VMEM_BYTES),
        cost_estimate=pl.CostEstimate(
            flops=64 * tokens * width * width, bytes_accessed=4 * width * width, transcendentals=0
        ),
        name="first_back",
    )(core, parts, second_grad, normal, scale, vectors, weight, sums, mixed, earlier)


def input_back_kernel(
    place_ref, dq_ref, own_ref, c_ref, y_ref, weight_ref, keep_ref, give_ref, grad_ref
):
    kv_grad = own_ref[...].astype(F32) + c_ref[...].astype(F32) + y_ref[...].astype(F32)
    grads = jnp.concatenate([dq_ref[...], kv_grad.astype(BF16)], axis=1)
    grad_ref[...] = grads
    inputs = nt(grads, weight_ref[...]).astype(BF16)
    pairs, count = keep_ref.shape[0], keep_ref.shape[1]
    own_first = place_ref[2] == 0
    for pair in range(pairs):
        first = inputs[2 * pair * count : (2 * pair + 1) * count]
        second = inputs[(2 * pair + 1) * count : (2 * pair + 2) * count]
        keep_ref[pair] = jnp.where(own_first, first, second)
        give_ref[pair] = jnp.where(own_first, second, first)


def input_back(place, query_grads, own, from_c, from_y, weight):
    tokens = query_grads.shape[0]
    width, cols = weight.shape
    vmem = pl.BlockSpec(memory_space=pltpu.VMEM)
    return pl.pallas_call(
        input_back_kernel,
        out_shape=(
            jax.ShapeDtypeStruct((4, tokens // 8, width), BF16),
            jax.ShapeDtypeStruct((4, tokens // 8, width), BF16),
            jax.ShapeDtypeStruct((tokens, cols), BF16),
        ),
        in_specs=[pl.BlockSpec(memory_space=pltpu.SMEM)] + [vmem] * 5,
        out_specs=(vmem,) * 3,
        compiler_params=pltpu.CompilerParams(vmem_limit_bytes=VMEM_BYTES),
        cost_estimate=pl.CostEstimate(
            flops=10 * tokens * width * cols, bytes_accessed=4 * tokens * width, transcendentals=0
        ),
        name="input_back",
    )(place, query_grads, own, from_c, from_y, weight)


def qkv_weight_kernel(place_ref, chunk_ref, grad_ref, shift_ref, keep_ref, give_ref):
    grads = grad_ref[...]
    weights = tn(chunk_ref[...], grads)
    cols = weights.shape[1]
    owners, shifts = shift_ref.shape
    shard = weights.shape[0] // (4 * owners)
    sums = column_sum(grads.astype(F32))
    for y_side in range(2):
        blocks = []
        for c_side in range(2):
            first = (y_side * 2 + c_side) * shard
            here = (place_ref[1] == c_side) & (place_ref[2] == y_side)
            shift = jnp.where(here, shift_ref[...], 0.0)
            blocks.append(
                jnp.concatenate(
                    [
                        *(
                            weights[at : at + shard]
                            for at in range(first, weights.shape[0], 4 * shard)
                        ),
                        jnp.concatenate([shift, jnp.zeros((owners, cols - shifts), F32)], axis=1),
                        jnp.broadcast_to(sums, (8, cols)),
                    ]
                ).astype(BF16)
            )
        own_first = place_ref[0] == 0
        keep_ref[y_side] = jnp.where(own_first, blocks[0], blocks[1])
        give_ref[y_side] = jnp.where(own_first, blocks[1], blocks[0])


def qkv_weight(place, chunk, grads, shifts):
    tokens, width = chunk.shape
    cols = grads.shape[1]
    rows = width // 4 + shifts.shape[0] + 8
    vmem = pl.BlockSpec(memory_space=pltpu.VMEM)
    return pl.pallas_call(
        qkv_weight_kernel,
        out_shape=(jax.ShapeDtypeStruct((2, rows, cols), BF16),) * 2,
        in_specs=[pl.BlockSpec(memory_space=pltpu.SMEM)] + [vmem] * 3,
        out_specs=(vmem,) * 2,
        compiler_params=pltpu.CompilerParams(vmem_limit_bytes=VMEM_BYTES),
        cost_estimate=pl.CostEstimate(
            flops=14 * tokens * width * cols, bytes_accessed=4 * tokens * width, transcendentals=0
        ),
        name="qkv_weight",
    )(place, chunk, grads, shifts)


def share_kernel(shard, shifts, first_ref, parts_ref, weight_ref, sums_ref, shift_ref):
    totals = [
        parts_ref[group].astype(F32) + parts_ref[GROUPS + group].astype(F32)
        for group in range(GROUPS)
    ]

    def part(number, rows):
        cols = slice(number * GROUP_WIDTH, (number + 1) * GROUP_WIDTH)
        return jnp.concatenate([total[rows, cols] for total in totals], axis=1)

    width = GROUPS * GROUP_WIDTH
    for number in range(3):
        weight_ref[:, number * width : (number + 1) * width] = part(number, slice(0, shard))
    sums = jnp.concatenate(
        [
            part(0, slice(shard, shard + 1)),
            part(2, slice(shard, shard + 1)),
            jnp.zeros((6, width), F32),
        ]
    )
    sums_ref[...] = pltpu.roll(sums, width - first_ref[0], 1)[:2, :shard]
    shift_ref[...] = sum(total[shard + 1 : shard + 2, :shifts] for total in totals)


def share(first, parts, shard, shifts):
    width = GROUPS * GROUP_WIDTH
    vmem = pl.BlockSpec(memory_space=pltpu.VMEM)
    return pl.pallas_call(
        functools.partial(share_kernel, shard, shifts),
        out_shape=(
            jax.ShapeDtypeStruct((shard, 3 * width), F32),
            jax.ShapeDtypeStruct((2, shard), F32),
            jax.ShapeDtypeStruct((1, shifts), F32),
        ),
        in_specs=[pl.BlockSpec(memory_space=pltpu.SMEM), vmem],
        out_specs=(vmem,) * 3,
        compiler_params=pltpu.CompilerParams(vmem_limit_bytes=VMEM_BYTES),
        cost_estimate=pl.CostEstimate(flops=10**10, bytes_accessed=10**6, transcendentals=0),
        name="share",
    )(first, parts)


def unpack_kernel(
    half,
    ring,
    core_ref,
    parts_ref,
    keep_ref,
    come_ref,
    _,
    __,
    in_ref,
    attn_ref,
    vec_ref,
    out_ref,
):
    keep, come = keep_ref[...].astype(F32), come_ref[...].astype(F32)
    own_first = core_ref[0] == 0
    out_ref[:, :half] = jnp.where(own_first, keep, come)
    out_ref[:, half:] = jnp.where(own_first, come, keep)
    start = half + 128
    units = parts_ref.shape[3] - start
    piece = units // ring
    for side in range(2):
        for place in range(ring):
            at = start + place * piece
            to = (side * ring + place) * 4 * piece
            in_ref[:, to : to + 4 * piece] = jnp.concatenate(
                [parts_ref[plane, side, :, at : at + piece].astype(F32) for plane in range(4)],
                axis=1,
            )
        attn_ref[:, side * half : (side + 1) * half] = sum(
            parts_ref[plane, side, :, :half].astype(F32) for plane in range(4)
        )
    vectors = sum(parts_ref[plane, 0, :, half:start].astype(F32) for plane in range(4))
    vec_ref[...] = vectors.T[:8]


def unpack(core, parts, keep, come, half, ring, *earlier):
    shard, cols = parts.shape[2:]
    units = cols - half - 128
    vmem = pl.BlockSpec(memory_space=pltpu.VMEM)
    return pl.pallas_call(
        functools.partial(unpack_kernel, half, ring),
        out_shape=(
            jax.ShapeDtypeStruct((shard, 8 * units), F32),
            jax.ShapeDtypeStruct((shard, 2 * half), F32),
            jax.ShapeDtypeStruct((8, shard), F32),
            jax.ShapeDtypeStruct((keep.shape[0], 2 * half), F32),
        ),
        in_specs=[pl.BlockSpec(memory_space=pltpu.SMEM)]
        + [vmem] * 3
        + [pl.BlockSpec(memory_space=pl.ANY)] * 2,
        out_specs=(vmem,) * 4,
        compiler_params=pltpu.CompilerParams(vmem_limit_bytes=VMEM_BYTES),
        name="unpack",
    )(core, parts, keep, come, *earlier)


def swap_sum(keep, give, axis):
    return keep.astype(F32) + lax.ppermute(give.astype(BF16), axis, SWAP).astype(F32)


def gather_plane(block):
    return lax.all_gather(block, PLANE, axis=0, tiled=True)


def spread_plane(parts):
    return lax.all_to_all(parts.reshape(4, -1, parts.shape[1]), PLANE, 0, 0, tiled=True)


def after(array, earlier):
    first = earlier[(slice(0, 1),) * earlier.ndim].reshape((1,) * array.ndim)
    return array + (first.astype(F32) * 0.0).astype(array.dtype)


def hold_kernel(*refs):
    del refs


def hold(array, earlier, cost=1):
    anywhere = pl.BlockSpec(memory_space=pl.ANY)
    return pl.pallas_call(
        hold_kernel,
        out_shape=jax.ShapeDtypeStruct(array.shape, array.dtype),
        in_specs=[anywhere] * 2,
        out_specs=anywhere,
        input_output_aliases={0: 0},
        cost_estimate=pl.CostEstimate(flops=cost, bytes_accessed=1, transcendentals=0),
        name="hold",
    )(array, earlier)


def pick_at(parts, index, axis):
    return lax.dynamic_index_in_dim(parts, index, axis, keepdims=False)


def pick(parts, index):
    return lax.dynamic_index_in_dim(parts, index, 0, keepdims=False)


def two(own, other, index):
    return jnp.where(index == 0, jnp.stack([own, other]), jnp.stack([other, own]))


def body(
    tokens,
    positions,
    w_qkv,
    qv_bias,
    w_attn_out,
    attn_out_bias,
    norm1_gain,
    norm1_bias,
    w_in,
    in_bias,
    w_out,
    out_bias,
    norm2_gain,
    norm2_bias,
    cotangent,
):
    seq_count, row_count, width = tokens.shape
    outer = lax.axis_size("e")
    seq_size = 2 * outer * GROUPS
    devices = seq_size * 4
    shard = w_qkv.shape[0]
    ff_shard = w_out.shape[0]
    ring = 4 * outer
    group = lax.axis_index(("r", "x"))
    place = lax.axis_index(("y", "c"))
    units = 2 * ring * ff_shard
    y_at, c_at = lax.axis_index("y"), lax.axis_index("c")
    qkv_cols = 3 * GROUP_WIDTH

    half = width // 2

    with jax.named_scope("gather_ff_weights"):
        in_cols = (
            w_in.reshape(shard, 2, ring, 4, 2 * ff_shard)
            .transpose(3, 1, 0, 2, 4)
            .reshape(4, 2, shard, units)
        )
        attn_cols = w_attn_out.reshape(shard, 2, half).transpose(1, 0, 2)
        in_parts = jnp.concatenate(
            [in_cols, jnp.broadcast_to(attn_cols, (4, 2, shard, half))], axis=3
        ).reshape(8, shard, units + half)
        in_parts = lax.all_to_all(
            in_parts, ("x", "y", "c"), 0, 0, tiled=True
        ).reshape(8 * shard, units + half)
        out_halves = w_out.reshape(ff_shard, 2, half).transpose(1, 0, 2)
        out_cols = two(
            pick(out_halves, c_at), lax.ppermute(pick(out_halves, 1 - c_at), "c", SWAP), c_at
        ).reshape(2 * ff_shard, half)
        packed = jnp.concatenate([in_parts, out_cols], axis=1)

    with jax.named_scope("gather_qkv_weights"):
        own_pos = lax.dynamic_slice_in_dim(positions, place * row_count, row_count, 1)
        shorts = jnp.stack(
            [
                qv_bias[0],
                qv_bias[1],
                attn_out_bias,
                norm1_gain,
                norm1_bias,
                out_bias,
                norm2_gain,
                norm2_bias,
            ]
        )
        spare = 64
        wide = qkv_cols + spare
        high = max(shard, 16)
        shift_rows = -(-2 * ff_shard // spare)
        smalls = jnp.concatenate(
            [
                jnp.broadcast_to(jnp.pad(shorts, ((0, 0), (0, spare - shard))), (2, 8, spare)),
                (own_pos >> 7).astype(BF16)[:, None],
                (own_pos & 127).astype(BF16)[:, None],
                jnp.broadcast_to(
                    jnp.pad(in_bias, (0, shift_rows * spare - 2 * ff_shard)).reshape(
                        shift_rows, spare
                    ),
                    (2, shift_rows, spare),
                ),
                jnp.zeros((2, high - 10 - shift_rows, spare), BF16),
            ],
            axis=1,
        )
        columns = (
            w_qkv.reshape(shard, 3, GROUPS, GROUP_WIDTH)
            .transpose(2, 0, 1, 3)
            .reshape(1, GROUPS, shard, qkv_cols)
        )
        columns = jnp.pad(columns, ((0, 0), (0, 0), (0, high - shard), (0, 0)))
        parcel = jnp.concatenate(
            [
                jnp.broadcast_to(columns, (2, GROUPS, high, qkv_cols)),
                jnp.broadcast_to(smalls[:, None], (2, GROUPS, high, spare)),
            ],
            axis=3,
        ).reshape(8, high, wide)
        parcel = lax.all_to_all(after(parcel, in_parts), SEQ_GROUP, 0, 0, tiled=True)

    with jax.named_scope("gather_tokens"):
        s_at, r_at, x_at = (lax.axis_index(name) for name in SEQ_GROUP)
        chunk = two(
            pick(tokens, s_at), lax.ppermute(pick(tokens, 1 - s_at), "s", SWAP), s_at
        )
        chunk = two(chunk, lax.ppermute(chunk, "r", SWAP), r_at)
        chunk = hold(chunk, packed)
        chunk = two(chunk, lax.ppermute(chunk, "x", SWAP), x_at)
        chunk = chunk.transpose(2, 1, 0, 3, 4).reshape(8 * row_count, width)

    with jax.named_scope("gather_qkv_weights"):
        parcels = lax.all_gather(hold(parcel, chunk), CHUNKS, axis=0, tiled=False)
        parcels = parcels.reshape(outer, 2, 2, 2, 2, 2, high, wide)
        order = (3, 0, 4, 5, 1, 2)
        qkv_slice = (
            parcels[..., :shard, :qkv_cols].transpose(*order, 6, 7).reshape(width, qkv_cols)
        )
        smalls = parcels[..., qkv_cols:]
        vectors = (
            smalls[..., :8, :shard].transpose(6, *order, 7).reshape(8, width).astype(F32)
        )
        pos_parts = smalls[..., 8:10, :row_count].astype(F32)
        chunk_pos = (pos_parts[..., 0, :] * 128.0 + pos_parts[..., 1, :]).reshape(
            outer, 2, 2, 8 * row_count
        )
        in_shift = pick_at(
            pick_at(smalls[..., 10 : 10 + shift_rows, :], x_at, 1), y_at, 1
        )
        in_shift = (
            in_shift.transpose(1, 0, 2, 3, 4, 5)
            .reshape(seq_size, shift_rows * spare)[:, : 2 * ff_shard]
            .reshape(2, units)
            .astype(F32)
        )

    with jax.named_scope("gather_ff_weights"):
        packed = lax.all_gather(packed, RING, axis=0, tiled=True)
        core = c_at.reshape(1).astype(jnp.int32)

    with jax.named_scope("project"):
        qv_slice = lax.dynamic_slice_in_dim(vectors[:2], group * GROUP_WIDTH, GROUP_WIDTH, 1)
        column_bias = jnp.concatenate(
            [qv_slice[0], jnp.zeros((GROUP_WIDTH,), F32), qv_slice[1]]
        )
        queries = (
            jnp.dot(chunk, qkv_slice[:, :GROUP_WIDTH], preferred_element_type=F32)
            + column_bias[:GROUP_WIDTH]
        ).astype(BF16)
        own_kv = (
            jnp.dot(chunk, qkv_slice[:, GROUP_WIDTH:], preferred_element_type=F32)
            + column_bias[GROUP_WIDTH:]
        ).astype(BF16)
    with jax.named_scope("gather_kv"):
        if outer > 1:
            own_kv = lax.all_gather(own_kv, "e", axis=0, tiled=True)
        y_kv = lax.ppermute(own_kv, "y", SWAP)
        key_values = [own_kv, lax.ppermute(own_kv, "c", SWAP)]
    ordered_pos = jnp.stack(
        [
            lax.dynamic_index_in_dim(
                lax.dynamic_index_in_dim(chunk_pos, y_at ^ ky, 1, keepdims=False),
                c_at ^ kc,
                1,
                keepdims=False,
            )
            for ky in (0, 1)
            for kc in (0, 1)
        ]
    )
    query_pos = lax.dynamic_index_in_dim(ordered_pos[0], lax.axis_index("e"), 0, keepdims=True)
    key_pos = ordered_pos.reshape(4 * outer, 8 * row_count)
    head_ids = group * GROUP_HEADS + jnp.arange(GROUP_HEADS)
    slopes = 2.0 ** (-8.0 * (head_ids + 1).astype(F32) / HEADS) * LOG2E

    with jax.named_scope("attention"):
        span = outer
        parts = ((0, 2), (2, 3), (3, 4))
        state = None
        for number, (first, last) in enumerate(parts):
            state = attend(
                slopes,
                queries,
                query_pos,
                key_pos[first * span : last * span],
                key_values[first:last],
                state,
                last=last == 4,
                earlier=(vectors, in_shift) if number == 1 else (),
            )
            if number == 0:
                y_kv = hold(y_kv, state[0])
                key_values += [y_kv, lax.ppermute(y_kv, "c", SWAP)]
        attended, log_sums, attended_low = state

    with jax.named_scope("return_attended"):
        returned = lax.all_to_all(
            attended_low.reshape(8, row_count, GROUP_WIDTH), SEQ_GROUP, 0, 0, tiled=True
        )
    with jax.named_scope("first_norm"):
        packed = hold(packed, returned)
        attn_own = packed[:, units : units + half]
        attn_swap = lax.ppermute(attn_own, "c", SWAP)
        hidden_low, hidden, normal, scale, attn_full = first_norm(
            core,
            returned,
            tokens.reshape(2 * row_count, width),
            vectors,
            attn_own,
            attn_swap,
            slice(0, half),
        )
        packed = hold(packed, hidden_low)
        swapped = lax.ppermute(packed, "c", SWAP)
    with jax.named_scope("gather_hidden"):
        hidden_group = gather_plane(hidden_low)
    with jax.named_scope("ff_forward"):
        activated_low, slope, gelu, ff_parts, in_slice, out_slice = ff_forward(
            core,
            hidden_group,
            in_shift,
            packed,
            swapped,
            slice(0, units),
            slice(units + half, units + width),
        )
    with jax.named_scope("sum_ff"):
        ff_parts = spread_plane(ff_parts)
    with jax.named_scope("second_norm"):
        result, second_grad, ff_grad, sums = second_norm(
            ff_parts, hidden, cotangent.reshape(2 * row_count, width), vectors
        )
    with jax.named_scope("gather_ff_grad"):
        ff_grads = gather_plane(ff_grad)
    with jax.named_scope("ff_backward"):
        joined_grad, hidden_parts, grad_in_shift, grad_halves = ff_backward(
            ff_grads, slope, gelu, in_slice, out_slice
        )
    with jax.named_scope("sum_hidden_grad"):
        hidden_parts = spread_plane(hidden_parts)
    with jax.named_scope("ff_weight_grads"):
        keep, give = ff_grads_of(core, activated_low, grad_halves, hidden_group, joined_grad)
        ff_keep, ff_give = keep, give
    with jax.named_scope("first_norm_back"):
        first_grad, out_grad, keep, give = first_back(
            core,
            hidden_parts,
            second_grad,
            normal,
            scale,
            vectors,
            attn_full,
            sums,
            returned,
            ff_keep,
        )
    with jax.named_scope("send_out_grad"):
        out_grads = lax.all_to_all(out_grad, SEQ_GROUP, 0, 0, tiled=True).reshape(
            8 * row_count, GROUP_WIDTH
        )
    with jax.named_scope("attn_weight_grad"):
        rows = jnp.concatenate(
            [swap_sum(keep, give, "c"), swap_sum(ff_keep, ff_give, "c")], axis=1
        ).astype(BF16)
        rows = hold(rows, out_grads)
        row_sums = lax.psum_scatter(rows, RING, scatter_dimension=0, tiled=True)

    with jax.named_scope("attention_back"):
        state, c_part, y_part, cy_part = attend_back(
            slopes,
            queries,
            query_pos,
            key_pos[span:],
            out_grads,
            attended,
            log_sums,
            key_values[1:],
            None,
            last=False,
            earlier=(rows,),
        )
        y_sum = swap_sum(y_part, cy_part, "c").astype(BF16)
        query_grads, own_part = attend_back(
            slopes,
            queries,
            query_pos,
            key_pos[:span],
            out_grads,
            attended,
            log_sums,
            key_values[:1],
            state,
            last=True,
            earlier=(y_sum,),
        )
    with jax.named_scope("sum_kv_grads"):
        from_c = lax.ppermute(c_part, "c", SWAP)
        from_y = lax.ppermute(y_sum, "y", SWAP)
        if outer > 1:
            total = own_part.astype(F32) + from_c.astype(F32) + from_y.astype(F32)
            own_part = lax.psum_scatter(
                total, "e", scatter_dimension=0, tiled=True
            ).astype(BF16)
            from_c = from_y = jnp.zeros_like(own_part)

    with jax.named_scope("input_back"):
        spot = jnp.stack([c_at, y_at, x_at]).astype(jnp.int32)
        input_keep, input_give, qkv_grad = input_back(
            spot, query_grads, own_part, from_c, from_y, qkv_slice
        )
    with jax.named_scope("qkv_weight_grad"):
        keep, give = qkv_weight(
            spot,
            chunk,
            qkv_grad,
            grad_in_shift.reshape(seq_size, 2 * ff_shard),
        )
        bundle = swap_sum(keep, give, "c").astype(BF16)
        from_x = lax.ppermute(input_give, "x", SWAP)
        parts = (hold(input_keep, bundle).astype(F32) + from_x.astype(F32)).reshape(
            2, 2, row_count, width
        )
        bundle = swap_sum(pick(bundle, y_at), pick(bundle, 1 - y_at), "y").astype(BF16)
        ends = width // 4 + seq_size
        shares = jnp.concatenate(
            [
                bundle[: width // 4].reshape(seq_size, shard, qkv_cols),
                jnp.broadcast_to(bundle[ends : ends + 1], (seq_size, 1, qkv_cols)),
                bundle[width // 4 : ends][:, None],
                jnp.zeros((seq_size, 6, qkv_cols), BF16),
            ],
            axis=1,
        )
    with jax.named_scope("input_grad"):
        from_r = lax.ppermute(
            hold(pick_at(parts, 1 - r_at, 1).astype(BF16), row_sums), "r", SWAP
        )
        parts = hold(pick_at(parts, r_at, 1), shares) + from_r.astype(F32)
    with jax.named_scope("qkv_weight_grad"):
        shares = lax.all_to_all(shares, SEQ_AXIS, 0, 0, tiled=True)
        from_s = lax.ppermute(
            hold(pick(parts, 1 - s_at).astype(BF16), shares), "s", SWAP
        )
    with jax.named_scope("ff_weight_grads"):
        own_cols = half + 128 + units
        row_sums = hold(row_sums, shares)
        plane_rows = row_sums[:, :own_cols].reshape(8, shard, own_cols)
    with jax.named_scope("qkv_weight_grad"):
        first_col = lax.axis_index(EVERY) * shard
        if outer == 1:
            grad_w_qkv, grad_qv, grad_in_bias = share(
                first_col.reshape(1).astype(jnp.int32), hold(shares, plane_rows), shard, 2 * ff_shard
            )
            grad_in_bias = grad_in_bias[0]
        else:
            totals = jnp.sum(
                shares.astype(F32).reshape(2 * outer, GROUPS, shard + 8, qkv_cols), axis=0
            )
            grad_w_qkv = (
                totals[:, :shard]
                .reshape(GROUPS, shard, 3, GROUP_WIDTH)
                .transpose(1, 2, 0, 3)
                .reshape(shard, 3 * width)
            )
            sums = (
                totals[:, shard].reshape(GROUPS, 3, GROUP_WIDTH).transpose(1, 0, 2).reshape(3, width)
            )
            grad_qv = lax.dynamic_slice_in_dim(sums[0::2], first_col, shard, 1)
            grad_in_bias = jnp.sum(totals[:, shard + 1, : 2 * ff_shard], axis=0)
    with jax.named_scope("input_grad"):
        input_grad = first_grad.reshape(2, row_count, width) + two(
            pick(parts, s_at), from_s.astype(F32), s_at
        )
    with jax.named_scope("ff_weight_grads"):
        exchanged = lax.all_to_all(
            plane_rows, ("x", "y", "c"), 0, 0, tiled=True
        ).reshape(4, 2, shard, own_cols)
        out_sums = row_sums[:, own_cols:].reshape(2, ff_shard, half)
        out_come = lax.ppermute(pick(out_sums, 1 - c_at), "c", SWAP)
        out_keep = pick(out_sums, c_at)
        if outer == 1:
            grad_w_in, grad_w_attn, vector_grads, grad_w_out = unpack(
                core, exchanged, out_keep, out_come, half, ring, grad_w_qkv, input_grad
            )
        else:
            grad_w_in = (
                exchanged[..., half + 128 :]
                .reshape(4, 2, shard, ring, 2 * ff_shard)
                .transpose(2, 1, 3, 0, 4)
                .reshape(shard, 2 * devices * ff_shard)
                .astype(F32)
            )
            grad_w_attn = (
                jnp.sum(exchanged[..., :half].astype(F32), axis=0)
                .transpose(1, 0, 2)
                .reshape(shard, width)
            )
            vector_grads = jnp.sum(exchanged[:, 0, :, half : half + 8].astype(F32), axis=0).T
            grad_w_out = (
                two(out_keep, out_come, c_at)
                .transpose(1, 0, 2)
                .reshape(ff_shard, width)
                .astype(F32)
            )
    return (
        result.reshape(2, row_count, width).astype(BF16),
        input_grad,
        grad_w_qkv,
        grad_qv,
        grad_w_attn,
        vector_grads[0],
        vector_grads[1],
        vector_grads[2],
        grad_w_in,
        grad_in_bias,
        grad_w_out,
        vector_grads[3],
        vector_grads[4],
        vector_grads[5],
    )


def solution(mesh):
    seq_size = mesh.shape["seq"]
    split = Mesh(mesh.devices.reshape(2, seq_size // 8, 2, 2, 2, 2), EVERY)
    tokens_at = P(None, EVERY, None)
    rows_at = P(EVERY, None)
    vector_at = P(EVERY)
    return jax.shard_map(
        body,
        mesh=split,
        in_specs=(
            tokens_at,
            P(None, SEQ_AXIS),
            rows_at,
            P(None, EVERY),
            rows_at,
            vector_at,
            vector_at,
            vector_at,
            rows_at,
            vector_at,
            rows_at,
            vector_at,
            vector_at,
            vector_at,
            tokens_at,
        ),
        out_specs=(
            tokens_at,
            tokens_at,
            rows_at,
            P(None, EVERY),
            rows_at,
            vector_at,
            vector_at,
            vector_at,
            rows_at,
            vector_at,
            rows_at,
            vector_at,
            vector_at,
            vector_at,
        ),
        check_vma=False,
    )
```

```python
import functools

import jax
import jax.numpy as jnp
from jax import lax
from jax.experimental import pallas as pl
from jax.experimental.pallas import tpu as pltpu
from jax.sharding import Mesh
from jax.sharding import PartitionSpec as P

HEADS = 12
HEAD_DIM = 64
GROUPS = 4
GROUP_HEADS = HEADS // GROUPS
GROUP_WIDTH = GROUP_HEADS * HEAD_DIM
EPSILON = 1e-12
SCORE_SCALE = 0.125
LOG2E = 1.4426950408889634
LOWEST = -1e30
GRAD_TILE = 256
KEY_BLOCK = 512
FF_TILE = 256
SEQ_GROUP = ("s", "r", "x")
CHUNKS = ("e", "y", "c")
RING = ("s", "e", "r")
PLANE = ("x", "y")
SEQ_AXIS = ("s", "e", "r", "x")
EVERY = ("s", "e", "r", "x", "y", "c")
SWAP = ((0, 1), (1, 0))
BF16 = jnp.bfloat16
F32 = jnp.float32
VMEM_BYTES = 60 * 2**20


def nt(a, b):
    return lax.dot_general(a, b, (((1,), (1,)), ((), ())), preferred_element_type=F32)


def tn(a, b):
    return lax.dot_general(a, b, (((0,), (0,)), ((), ())), preferred_element_type=F32)


def nn(a, b):
    return lax.dot_general(a, b, (((1,), (0,)), ((), ())), preferred_element_type=F32)


def head_cols(head, base=0):
    return slice(base + head * HEAD_DIM, base + (head + 1) * HEAD_DIM)


def log2_scores(keys, queries, slope, key_pos, query_pos):
    products = nt(keys, queries)
    distances = jnp.abs(key_pos * slope - query_pos * slope)
    return products * (SCORE_SCALE * LOG2E) - distances


def column(row):
    return jnp.broadcast_to(row, (8, row.shape[1])).T[:, :1]


def key_blocks(kv_refs):
    start = 0
    for piece in kv_refs:
        yield piece, start
        start += piece.shape[0]


def turn_positions(pk_ref, column_ref):
    length = pk_ref.shape[1]

    def turn(row, carry):
        at = pl.ds(pl.multiple_of(row * length, length), length)
        column_ref[at, :] = column(pk_ref[pl.ds(row, 1), :])
        return carry

    lax.fori_loop(0, pk_ref.shape[0], turn, 0)


def attend_kernel(deps, count, first, last, slopes_ref, q_ref, pq_ref, pk_ref, *refs):
    refs = refs[deps:]
    kv_refs, refs = refs[:count], refs[count:]
    if not first:
        (sum_in_ref, stat_in_ref), refs = refs[:2], refs[2:]
    sum_ref, stat_ref = refs[:2]
    column_ref = refs[-1]
    rows = q_ref.shape[0]
    query_pos = pq_ref[...]
    turn_positions(pk_ref, column_ref)
    for head in range(GROUP_HEADS):
        slope = slopes_ref[head]
        queries = q_ref[:, head_cols(head)]
        if first:
            carry = (
                jnp.full((1, rows), LOWEST, F32),
                jnp.zeros((1, rows), F32),
                jnp.zeros((HEAD_DIM, rows), F32),
            )
        else:
            carry = (
                stat_in_ref[head : head + 1, :],
                stat_in_ref[GROUP_HEADS + head : GROUP_HEADS + head + 1, :],
                sum_in_ref[head_cols(head), :],
            )
        for kv_ref, start in key_blocks(kv_refs):

            def visit(block, carry, kv_ref=kv_ref, start=start):
                top, total, summed = carry
                at = pl.ds(pl.multiple_of(block * KEY_BLOCK, KEY_BLOCK), KEY_BLOCK)
                pos_at = pl.ds(
                    pl.multiple_of(start + block * KEY_BLOCK, KEY_BLOCK), KEY_BLOCK
                )
                keys = kv_ref[at, head_cols(head)]
                values = kv_ref[at, head_cols(head, GROUP_WIDTH)]
                scores = log2_scores(keys, queries, slope, column_ref[pos_at, :], query_pos)
                new_top = jnp.maximum(top, jnp.max(scores, axis=0, keepdims=True))
                weights = jnp.exp2(scores - new_top)
                shrink = jnp.exp2(top - new_top)
                total = total * shrink + jnp.sum(weights, axis=0, keepdims=True)
                summed = summed * shrink + tn(values, weights.astype(BF16))
                return new_top, total, summed

            carry = lax.fori_loop(0, kv_ref.shape[0] // KEY_BLOCK, visit, carry)
        top, total, summed = carry
        if last:
            attended = summed / total
            sum_ref[head_cols(head), :] = attended
            refs[2][:, head_cols(head)] = attended.T.astype(BF16)
            stat_ref[head : head + 1, :] = top + jnp.log2(total)
        else:
            sum_ref[head_cols(head), :] = summed
            stat_ref[head : head + 1, :] = top
            stat_ref[GROUP_HEADS + head : GROUP_HEADS + head + 1, :] = total


def attend(slopes, queries, query_pos, key_pos, key_values, state, last, earlier):
    rows, length = queries.shape[0], key_pos.size
    vmem = pl.BlockSpec(memory_space=pltpu.VMEM)
    count = len(key_values)
    first = state is None
    state = () if first else state
    outs = [
        jax.ShapeDtypeStruct((GROUP_WIDTH, rows), F32),
        jax.ShapeDtypeStruct((GROUP_HEADS * (1 if last else 2), rows), F32),
    ]
    if last:
        outs.append(jax.ShapeDtypeStruct((rows, GROUP_WIDTH), BF16))
    return pl.pallas_call(
        functools.partial(attend_kernel, len(earlier), count, first, last),
        out_shape=tuple(outs),
        in_specs=[pl.BlockSpec(memory_space=pltpu.SMEM)]
        + [vmem] * 3
        + [pl.BlockSpec(memory_space=pl.ANY)] * len(earlier)
        + [vmem] * (count + len(state)),
        out_specs=(vmem,) * len(outs),
        scratch_shapes=[pltpu.VMEM((length, 1), F32)],
        compiler_params=pltpu.CompilerParams(vmem_limit_bytes=VMEM_BYTES),
        cost_estimate=pl.CostEstimate(
            flops=64 * rows * length * GROUP_WIDTH,
            bytes_accessed=rows * length,
            transcendentals=rows * length * GROUP_HEADS,
        ),
        name="attend",
    )(slopes, queries, query_pos, key_pos, *earlier, *key_values, *state)


def attend_back_kernel(
    deps, count, first, last, slopes_ref, q_ref, pq_ref, pk_ref, do_ref, out_ref, lse_ref, *refs
):
    refs = refs[deps:]
    kv_refs, refs = refs[:count], refs[count:]
    if not first:
        dq_in_ref, refs = refs[0], refs[1:]
    dq_ref, dkv_refs, column_ref = refs[0], refs[1 : count + 1], refs[-1]
    rows = q_ref.shape[0]
    query_pos = pq_ref[...]
    turn_positions(pk_ref, column_ref)
    for head in range(GROUP_HEADS):
        slope = slopes_ref[head]
        queries = q_ref[:, head_cols(head)]
        out_grads = do_ref[:, head_cols(head)]
        log_sum = lse_ref[head : head + 1, :]
        delta = jnp.sum(
            out_grads.astype(F32).T * out_ref[head_cols(head), :], axis=0, keepdims=True
        )
        if first:
            query_grads = jnp.zeros((HEAD_DIM, rows), F32)
        else:
            query_grads = dq_in_ref[head_cols(head), :]
        for (kv_ref, start), dkv_ref in zip(key_blocks(kv_refs), dkv_refs):

            def visit(block, query_grads, kv_ref=kv_ref, start=start, dkv_ref=dkv_ref):
                at = pl.ds(pl.multiple_of(block * KEY_BLOCK, KEY_BLOCK), KEY_BLOCK)
                pos_at = pl.ds(
                    pl.multiple_of(start + block * KEY_BLOCK, KEY_BLOCK), KEY_BLOCK
                )
                keys = kv_ref[at, head_cols(head)]
                values = kv_ref[at, head_cols(head, GROUP_WIDTH)]
                scores = log2_scores(keys, queries, slope, column_ref[pos_at, :], query_pos)
                probs = jnp.exp2(scores - log_sum)
                prob_grads = nt(values, out_grads)
                score_grads = (probs * (prob_grads - delta)).astype(BF16)
                dkv_ref[at, head_cols(head, GROUP_WIDTH)] = nn(
                    probs.astype(BF16), out_grads
                ).astype(BF16)
                dkv_ref[at, head_cols(head)] = (nn(score_grads, queries) * SCORE_SCALE).astype(
                    BF16
                )
                return query_grads + tn(keys, score_grads)

            query_grads = lax.fori_loop(0, kv_ref.shape[0] // KEY_BLOCK, visit, query_grads)
        if last:
            dq_ref[:, head_cols(head)] = (query_grads * SCORE_SCALE).T.astype(BF16)
        else:
            dq_ref[head_cols(head), :] = query_grads


def attend_back(
    slopes,
    queries,
    query_pos,
    key_pos,
    out_grads,
    attended,
    log_sums,
    key_values,
    state,
    last,
    earlier,
):
    rows, length = queries.shape[0], key_pos.size
    vmem = pl.BlockSpec(memory_space=pltpu.VMEM)
    count = len(key_values)
    first = state is None
    state = () if first else (state,)
    query_out = (
        jax.ShapeDtypeStruct((rows, GROUP_WIDTH), BF16)
        if last
        else jax.ShapeDtypeStruct((GROUP_WIDTH, rows), F32)
    )
    return pl.pallas_call(
        functools.partial(attend_back_kernel, len(earlier), count, first, last),
        out_shape=(query_out,)
        + tuple(jax.ShapeDtypeStruct(piece.shape, BF16) for piece in key_values),
        in_specs=[pl.BlockSpec(memory_space=pltpu.SMEM)]
        + [vmem] * 6
        + [pl.BlockSpec(memory_space=pl.ANY)] * len(earlier)
        + [vmem] * (count + len(state)),
        out_specs=(vmem,) * (1 + count),
        scratch_shapes=[pltpu.VMEM((length, 1), F32)],
        compiler_params=pltpu.CompilerParams(vmem_limit_bytes=VMEM_BYTES),
        cost_estimate=pl.CostEstimate(
            flops=84 * rows * length * GROUP_WIDTH,
            bytes_accessed=rows * length,
            transcendentals=rows * length * GROUP_HEADS,
        ),
        name="attend_back",
    )(
        slopes,
        queries,
        query_pos,
        key_pos,
        out_grads,
        attended,
        log_sums,
        *earlier,
        *key_values,
        *state,
    )


def merged(parts_ref):
    return jnp.concatenate(
        [
            jnp.concatenate(
                [parts_ref[seq * GROUPS + group] for group in range(GROUPS)], axis=1
            )
            for seq in range(2)
        ]
    )


def first_norm_kernel(
    core_ref,
    mixed_ref,
    rows_ref,
    vec_ref,
    own_ref,
    swap_ref,
    low_ref,
    hidden_ref,
    normal_ref,
    scale_ref,
):
    mixed = merged(mixed_ref)
    first = core_ref[0] == 0
    own, swap = nn(mixed, own_ref[...]), nn(mixed, swap_ref[...])
    lin = jnp.concatenate([jnp.where(first, own, swap), jnp.where(first, swap, own)], axis=1)
    total = rows_ref[...].astype(F32) + (lin + vec_ref[2:3, :])
    normal, scale = normalised(total)
    hidden = normal * vec_ref[3:4, :] + vec_ref[4:5, :]
    low_ref[...] = hidden.astype(BF16)
    hidden_ref[...] = hidden
    normal_ref[...] = normal
    scale_ref[...] = scale


def normalised(values):
    centred = values - jnp.mean(values, axis=1, keepdims=True)
    variance = jnp.mean(centred * centred, axis=1, keepdims=True)
    scale = lax.rsqrt(variance + EPSILON)
    return centred * scale, scale


def norm_back(grads, normal, scale, gain):
    scaled = grads * gain
    return (
        scaled
        - jnp.mean(scaled, axis=1, keepdims=True)
        - normal * jnp.mean(scaled * normal, axis=1, keepdims=True)
    ) * scale


def column_sum(values):
    return jnp.sum(values, axis=0, keepdims=True)


def first_norm(core, mixed, rows, vectors, own, swap):
    tokens, width = rows.shape
    vmem = pl.BlockSpec(memory_space=pltpu.VMEM)
    return pl.pallas_call(
        first_norm_kernel,
        out_shape=(
            jax.ShapeDtypeStruct((tokens, width), BF16),
            jax.ShapeDtypeStruct((tokens, width), F32),
            jax.ShapeDtypeStruct((tokens, width), F32),
            jax.ShapeDtypeStruct((tokens, 1), F32),
        ),
        in_specs=[pl.BlockSpec(memory_space=pltpu.SMEM)] + [vmem] * 5,
        out_specs=(vmem,) * 4,
        compiler_params=pltpu.CompilerParams(vmem_limit_bytes=VMEM_BYTES),
        cost_estimate=pl.CostEstimate(
            flops=64 * tokens * width * width, bytes_accessed=4 * width * width, transcendentals=0
        ),
        name="first_norm",
    )(core, mixed, rows, vectors, own, swap)


def ff_forward_kernel(
    units, out_columns, core_ref, hidden_ref, bias_ref, own_ref, swap_ref, act_ref, slope_ref, gelu_ref, parts_ref
):
    tokens = hidden_ref.shape[0]
    first = core_ref[0] == 0

    def visit(tile, carry):
        at = pl.ds(pl.multiple_of(tile * FF_TILE, FF_TILE), FF_TILE)
        rows = hidden_ref[at, :]
        own = nn(rows, own_ref[:, :units])
        swap = nn(rows, swap_ref[:, :units])
        gate = jnp.where(first, own, swap) + bias_ref[0:1, :]
        up = jnp.where(first, swap, own) + bias_ref[1:2, :]
        cdf = 0.5 * (1.0 + lax.erf(gate * (0.5**0.5)))
        density = jnp.exp(-0.5 * gate * gate) * 0.3989422804014327
        gelu = gate * cdf
        act = (gelu * up).astype(BF16)
        act_ref[at, :] = act
        gelu_ref[at, :] = gelu.astype(BF16)
        slope_ref[at, :] = (up * (cdf + gate * density)).astype(BF16)
        own = nn(act, own_ref[:, out_columns]).astype(BF16)
        swap = nn(act, swap_ref[:, out_columns]).astype(BF16)
        parts_ref[at, :] = jnp.concatenate(
            [jnp.where(first, own, swap), jnp.where(first, swap, own)], axis=1
        )
        return carry

    lax.fori_loop(0, tokens // FF_TILE, visit, 0)


def ff_forward(core, hidden, bias, own, swap, out_columns):
    tokens, width = hidden.shape
    units = bias.shape[1]
    vmem = pl.BlockSpec(memory_space=pltpu.VMEM)
    return pl.pallas_call(
        functools.partial(ff_forward_kernel, units, out_columns),
        out_shape=(
            jax.ShapeDtypeStruct((tokens, units), BF16),
            jax.ShapeDtypeStruct((tokens, units), BF16),
            jax.ShapeDtypeStruct((tokens, units), BF16),
            jax.ShapeDtypeStruct((tokens, width), BF16),
        ),
        in_specs=[pl.BlockSpec(memory_space=pltpu.SMEM)] + [vmem] * 4,
        out_specs=(vmem,) * 4,
        compiler_params=pltpu.CompilerParams(vmem_limit_bytes=VMEM_BYTES),
        cost_estimate=pl.CostEstimate(
            flops=32 * tokens * width * units,
            bytes_accessed=6 * width * units,
            transcendentals=2 * tokens * units,
        ),
        name="ff_forward",
    )(core, hidden, bias, own, swap)


def second_norm_kernel(
    parts_ref, hidden_ref, cotangent_ref, vec_ref, result_ref, grad_ref, low_ref, sums_ref
):
    lin = jnp.sum(parts_ref[...].astype(F32), axis=0) + vec_ref[5:6, :]
    normal, scale = normalised(hidden_ref[...] + lin)
    gain = vec_ref[6:7, :]
    result_ref[...] = (normal * gain + vec_ref[7:8, :]).astype(BF16)
    grads = cotangent_ref[...].astype(F32)
    back = norm_back(grads, normal, scale, gain)
    low = back.astype(BF16)
    grad_ref[...] = back
    low_ref[...] = low
    sums_ref[...] = jnp.concatenate(
        [
            column_sum(low.astype(F32)),
            column_sum(grads * normal),
            column_sum(grads),
            jnp.zeros((5, back.shape[1]), F32),
        ]
    )


def second_norm(parts, hidden, cotangent, vectors):
    tokens, width = hidden.shape
    vmem = pl.BlockSpec(memory_space=pltpu.VMEM)
    return pl.pallas_call(
        second_norm_kernel,
        out_shape=(
            jax.ShapeDtypeStruct((tokens, width), BF16),
            jax.ShapeDtypeStruct((tokens, width), F32),
            jax.ShapeDtypeStruct((tokens, width), BF16),
            jax.ShapeDtypeStruct((8, width), F32),
        ),
        in_specs=[vmem] * 4,
        out_specs=(vmem,) * 4,
        compiler_params=pltpu.CompilerParams(vmem_limit_bytes=VMEM_BYTES),
        cost_estimate=pl.CostEstimate(
            flops=20000 * tokens * width, bytes_accessed=20 * tokens * width, transcendentals=0
        ),
        name="second_norm",
    )(parts, hidden, cotangent, vectors)


def ff_backward_kernel(
    units,
    out_columns,
    core_ref,
    grad_ref,
    slope_ref,
    gelu_ref,
    own_ref,
    swap_ref,
    joined_ref,
    parts_ref,
    bias_ref,
    half_ref,
):
    tokens, width = grad_ref.shape
    half = width // 2
    first = core_ref[0] == 0
    bias_ref[...] = jnp.zeros_like(bias_ref)

    def visit(tile, carry):
        at = pl.ds(pl.multiple_of(tile * FF_TILE, FF_TILE), FF_TILE)
        left, right = grad_ref[at, :half], grad_ref[at, half:]
        half_ref[0, at, :] = left
        half_ref[1, at, :] = right
        act_grad = nt(jnp.where(first, left, right), own_ref[:, out_columns]) + nt(
            jnp.where(first, right, left), swap_ref[:, out_columns]
        )
        joined = []
        for which, factor in ((0, slope_ref), (1, gelu_ref)):
            side = (act_grad * factor[at, :].astype(F32)).astype(BF16)
            joined_ref[which, at, :] = side
            bias_ref[which : which + 1, :] += column_sum(side.astype(F32))
            joined.append(side)
        parts_ref[at, :] = (
            nt(jnp.where(first, joined[0], joined[1]), own_ref[:, :units])
            + nt(jnp.where(first, joined[1], joined[0]), swap_ref[:, :units])
        ).astype(BF16)
        return carry

    lax.fori_loop(0, tokens // FF_TILE, visit, 0)


def ff_backward(core, grads, slope, gelu, own, swap, out_columns):
    tokens, width = grads.shape
    units = slope.shape[1]
    vmem = pl.BlockSpec(memory_space=pltpu.VMEM)
    return pl.pallas_call(
        functools.partial(ff_backward_kernel, units, out_columns),
        out_shape=(
            jax.ShapeDtypeStruct((2, tokens, units), BF16),
            jax.ShapeDtypeStruct((tokens, width), BF16),
            jax.ShapeDtypeStruct((2, units), F32),
            jax.ShapeDtypeStruct((2, tokens, width // 2), BF16),
        ),
        in_specs=[pl.BlockSpec(memory_space=pltpu.SMEM)] + [vmem] * 5,
        out_specs=(vmem,) * 4,
        compiler_params=pltpu.CompilerParams(vmem_limit_bytes=VMEM_BYTES),
        cost_estimate=pl.CostEstimate(
            flops=32 * tokens * width * units,
            bytes_accessed=6 * width * units,
            transcendentals=0,
        ),
        name="ff_backward",
    )(core, grads, slope, gelu, own, swap)


def ff_grads_kernel(core_ref, act_ref, half_ref, hidden_ref, joined_ref, keep_ref, give_ref):
    core = core_ref[0]
    units = joined_ref.shape[2]

    def visit(tile, carry):
        at = pl.ds(pl.multiple_of(tile * GRAD_TILE, GRAD_TILE), GRAD_TILE)
        hidden = hidden_ref[:, at]
        act = act_ref[:, at]
        give_ref[at, :units] = tn(hidden, joined_ref[1 - core]).astype(BF16)
        give_ref[at, units:] = tn(act, half_ref[1 - core]).astype(BF16)
        keep_ref[at, :units] = tn(hidden, joined_ref[core]).astype(BF16)
        keep_ref[at, units:] = tn(act, half_ref[core]).astype(BF16)
        return carry

    lax.fori_loop(0, hidden_ref.shape[1] // GRAD_TILE, visit, 0)


def ff_grads_of(core, act, halves, hidden, joined):
    width = hidden.shape[1]
    cols = joined.shape[2] + halves.shape[2]
    vmem = pl.BlockSpec(memory_space=pltpu.VMEM)
    return pl.pallas_call(
        ff_grads_kernel,
        out_shape=(jax.ShapeDtypeStruct((width, cols), BF16),) * 2,
        in_specs=[pl.BlockSpec(memory_space=pltpu.SMEM)] + [vmem] * 4,
        out_specs=(vmem,) * 2,
        compiler_params=pltpu.CompilerParams(vmem_limit_bytes=VMEM_BYTES),
        cost_estimate=pl.CostEstimate(flops=6 * 10**9, bytes_accessed=10**4, transcendentals=0),
        name="ff_grads",
    )(core, act, halves, hidden, joined)


def first_back_kernel(
    core_ref,
    parts_ref,
    second_ref,
    normal_ref,
    scale_ref,
    vec_ref,
    own_ref,
    swap_ref,
    sums_ref,
    mixed_ref,
    _,
    grad_ref,
    out_ref,
    keep_ref,
    give_ref,
):
    tokens, width = second_ref.shape
    half, count = width // 2, tokens // 2
    normal = normal_ref[...]
    grads = second_ref[...] + jnp.sum(parts_ref[...].astype(F32), axis=0)
    back = norm_back(grads, normal, scale_ref[...], vec_ref[3:4, :])
    low = back.astype(BF16)
    grad_ref[...] = back
    own_left = core_ref[0] == 0
    left, right = low[:, :half], low[:, half:]
    out_grad = nt(jnp.where(own_left, left, right), own_ref[...]) + nt(
        jnp.where(own_left, right, left), swap_ref[...]
    )
    for seq in range(2):
        for group in range(GROUPS):
            out_ref[seq * GROUPS + group] = out_grad[
                seq * count : (seq + 1) * count, group * GROUP_WIDTH : (group + 1) * GROUP_WIDTH
            ].astype(BF16)
    rows = jnp.concatenate(
        [
            column_sum(low.astype(F32)),
            column_sum(grads * normal),
            column_sum(grads),
            sums_ref[0:3, :],
            jnp.zeros((122, width), F32),
        ]
    )
    turned = rows.T.astype(BF16)
    keep_ref[:, half:] = turned
    give_ref[:, half:] = turned
    mixed = merged(mixed_ref)
    left = tn(mixed, low[:, :half]).astype(BF16)
    right = tn(mixed, low[:, half:]).astype(BF16)
    keep_ref[:, :half] = jnp.where(own_left, left, right)
    give_ref[:, :half] = jnp.where(own_left, right, left)


def first_back(
    core, parts, second_grad, normal, scale, vectors, own, swap, sums, mixed, earlier
):
    tokens, width = second_grad.shape
    vmem = pl.BlockSpec(memory_space=pltpu.VMEM)
    return pl.pallas_call(
        first_back_kernel,
        out_shape=(
            jax.ShapeDtypeStruct((tokens, width), F32),
            jax.ShapeDtypeStruct((2 * GROUPS, tokens // 2, GROUP_WIDTH), BF16),
            jax.ShapeDtypeStruct((width, width // 2 + 128), BF16),
            jax.ShapeDtypeStruct((width, width // 2 + 128), BF16),
        ),
        in_specs=[pl.BlockSpec(memory_space=pltpu.SMEM)]
        + [vmem] * 9
        + [pl.BlockSpec(memory_space=pl.ANY)],
        out_specs=(vmem,) * 4,
        compiler_params=pltpu.CompilerParams(vmem_limit_bytes=VMEM_BYTES),
        cost_estimate=pl.CostEstimate(
            flops=64 * tokens * width * width, bytes_accessed=4 * width * width, transcendentals=0
        ),
        name="first_back",
    )(core, parts, second_grad, normal, scale, vectors, own, swap, sums, mixed, earlier)


def input_back_kernel(
    place_ref, dq_ref, own_ref, c_ref, y_ref, weight_ref, keep_ref, give_ref, grad_ref
):
    kv_grad = own_ref[...].astype(F32) + c_ref[...].astype(F32) + y_ref[...].astype(F32)
    grads = jnp.concatenate([dq_ref[...], kv_grad.astype(BF16)], axis=1)
    grad_ref[...] = grads
    inputs = nt(grads, weight_ref[...]).astype(BF16)
    pairs, count = keep_ref.shape[0], keep_ref.shape[1]
    own_first = place_ref[2] == 0
    for pair in range(pairs):
        first = inputs[2 * pair * count : (2 * pair + 1) * count]
        second = inputs[(2 * pair + 1) * count : (2 * pair + 2) * count]
        keep_ref[pair] = jnp.where(own_first, first, second)
        give_ref[pair] = jnp.where(own_first, second, first)


def input_back(place, query_grads, own, from_c, from_y, weight):
    tokens = query_grads.shape[0]
    width, cols = weight.shape
    vmem = pl.BlockSpec(memory_space=pltpu.VMEM)
    return pl.pallas_call(
        input_back_kernel,
        out_shape=(
            jax.ShapeDtypeStruct((4, tokens // 8, width), BF16),
            jax.ShapeDtypeStruct((4, tokens // 8, width), BF16),
            jax.ShapeDtypeStruct((tokens, cols), BF16),
        ),
        in_specs=[pl.BlockSpec(memory_space=pltpu.SMEM)] + [vmem] * 5,
        out_specs=(vmem,) * 3,
        compiler_params=pltpu.CompilerParams(vmem_limit_bytes=VMEM_BYTES),
        cost_estimate=pl.CostEstimate(
            flops=10 * tokens * width * cols, bytes_accessed=4 * tokens * width, transcendentals=0
        ),
        name="input_back",
    )(place, query_grads, own, from_c, from_y, weight)


def qkv_weight_kernel(place_ref, chunk_ref, grad_ref, shift_ref, keep_ref, give_ref):
    grads = grad_ref[...]
    weights = tn(chunk_ref[...], grads)
    cols = weights.shape[1]
    owners, shifts = shift_ref.shape
    shard = weights.shape[0] // (4 * owners)
    sums = column_sum(grads.astype(F32))
    for y_side in range(2):
        blocks = []
        for c_side in range(2):
            first = (y_side * 2 + c_side) * shard
            here = (place_ref[1] == c_side) & (place_ref[2] == y_side)
            shift = jnp.where(here, shift_ref[...], 0.0)
            blocks.append(
                jnp.concatenate(
                    [
                        *(
                            weights[at : at + shard]
                            for at in range(first, weights.shape[0], 4 * shard)
                        ),
                        jnp.concatenate([shift, jnp.zeros((owners, cols - shifts), F32)], axis=1),
                        jnp.broadcast_to(sums, (8, cols)),
                    ]
                ).astype(BF16)
            )
        own_first = place_ref[0] == 0
        keep_ref[y_side] = jnp.where(own_first, blocks[0], blocks[1])
        give_ref[y_side] = jnp.where(own_first, blocks[1], blocks[0])


def qkv_weight(place, chunk, grads, shifts):
    tokens, width = chunk.shape
    cols = grads.shape[1]
    rows = width // 4 + shifts.shape[0] + 8
    vmem = pl.BlockSpec(memory_space=pltpu.VMEM)
    return pl.pallas_call(
        qkv_weight_kernel,
        out_shape=(jax.ShapeDtypeStruct((2, rows, cols), BF16),) * 2,
        in_specs=[pl.BlockSpec(memory_space=pltpu.SMEM)] + [vmem] * 3,
        out_specs=(vmem,) * 2,
        compiler_params=pltpu.CompilerParams(vmem_limit_bytes=VMEM_BYTES),
        cost_estimate=pl.CostEstimate(
            flops=14 * tokens * width * cols, bytes_accessed=4 * tokens * width, transcendentals=0
        ),
        name="qkv_weight",
    )(place, chunk, grads, shifts)


def spread_kernel(ring, in_ref, attn_ref, out_ref):
    units = in_ref.shape[1] // 8
    piece = units // ring
    half = attn_ref.shape[1] // 2
    for side in range(2):
        for plane in range(4):
            out_ref[2 * plane + side, :, :units] = jnp.concatenate(
                [
                    in_ref[:, at : at + piece]
                    for at in (
                        (side * ring + place) * 4 * piece + plane * piece for place in range(ring)
                    )
                ],
                axis=1,
            )
            out_ref[2 * plane + side, :, units:] = attn_ref[:, side * half : (side + 1) * half]


def spread_weights(w_in, w_attn_out, ring):
    shard, cols = w_in.shape
    vmem = pl.BlockSpec(memory_space=pltpu.VMEM)
    return pl.pallas_call(
        functools.partial(spread_kernel, ring),
        out_shape=jax.ShapeDtypeStruct((8, shard, cols // 8 + w_attn_out.shape[1] // 2), BF16),
        in_specs=[vmem] * 2,
        out_specs=vmem,
        compiler_params=pltpu.CompilerParams(vmem_limit_bytes=VMEM_BYTES),
        name="spread",
    )(w_in, w_attn_out)


def share_kernel(shard, shifts, first_ref, parts_ref, weight_ref, sums_ref, shift_ref):
    totals = [
        parts_ref[group].astype(F32) + parts_ref[GROUPS + group].astype(F32)
        for group in range(GROUPS)
    ]

    def part(number, rows):
        cols = slice(number * GROUP_WIDTH, (number + 1) * GROUP_WIDTH)
        return jnp.concatenate([total[rows, cols] for total in totals], axis=1)

    width = GROUPS * GROUP_WIDTH
    for number in range(3):
        weight_ref[:, number * width : (number + 1) * width] = part(number, slice(0, shard))
    sums = jnp.concatenate(
        [
            part(0, slice(shard, shard + 1)),
            part(2, slice(shard, shard + 1)),
            jnp.zeros((6, width), F32),
        ]
    )
    sums_ref[...] = pltpu.roll(sums, width - first_ref[0], 1)[:2, :shard]
    shift_ref[...] = sum(total[shard + 1 : shard + 2, :shifts] for total in totals)


def share(first, parts, shard, shifts):
    width = GROUPS * GROUP_WIDTH
    vmem = pl.BlockSpec(memory_space=pltpu.VMEM)
    return pl.pallas_call(
        functools.partial(share_kernel, shard, shifts),
        out_shape=(
            jax.ShapeDtypeStruct((shard, 3 * width), F32),
            jax.ShapeDtypeStruct((2, shard), F32),
            jax.ShapeDtypeStruct((1, shifts), F32),
        ),
        in_specs=[pl.BlockSpec(memory_space=pltpu.SMEM), vmem],
        out_specs=(vmem,) * 3,
        compiler_params=pltpu.CompilerParams(vmem_limit_bytes=VMEM_BYTES),
        cost_estimate=pl.CostEstimate(flops=10**10, bytes_accessed=10**6, transcendentals=0),
        name="share",
    )(first, parts)


def unpack_kernel(
    half,
    ring,
    core_ref,
    parts_ref,
    keep_ref,
    come_ref,
    _,
    __,
    in_ref,
    attn_ref,
    out_ref,
    *vec_refs,
):
    keep, come = keep_ref[...].astype(F32), come_ref[...].astype(F32)
    own_first = core_ref[0] == 0
    out_ref[:, :half] = jnp.where(own_first, keep, come)
    out_ref[:, half:] = jnp.where(own_first, come, keep)
    start = half + 128
    units = parts_ref.shape[3] - start
    piece = units // ring
    for side in range(2):
        for place in range(ring):
            at = start + place * piece
            to = (side * ring + place) * 4 * piece
            in_ref[:, to : to + 4 * piece] = jnp.concatenate(
                [parts_ref[plane, side, :, at : at + piece].astype(F32) for plane in range(4)],
                axis=1,
            )
        attn_ref[:, side * half : (side + 1) * half] = sum(
            parts_ref[plane, side, :, :half].astype(F32) for plane in range(4)
        )
    vectors = sum(parts_ref[plane, 0, :, half:start].astype(F32) for plane in range(4))
    rows = vectors.T
    for number, vec_ref in enumerate(vec_refs):
        vec_ref[...] = rows[number : number + 1]


def unpack(core, parts, keep, come, half, ring, *earlier):
    shard, cols = parts.shape[2:]
    units = cols - half - 128
    vmem = pl.BlockSpec(memory_space=pltpu.VMEM)
    return pl.pallas_call(
        functools.partial(unpack_kernel, half, ring),
        out_shape=(
            jax.ShapeDtypeStruct((shard, 8 * units), F32),
            jax.ShapeDtypeStruct((shard, 2 * half), F32),
            jax.ShapeDtypeStruct((keep.shape[0], 2 * half), F32),
        )
        + (jax.ShapeDtypeStruct((1, shard), F32),) * 6,
        in_specs=[pl.BlockSpec(memory_space=pltpu.SMEM)]
        + [vmem] * 3
        + [pl.BlockSpec(memory_space=pl.ANY)] * 2,
        out_specs=(vmem,) * 9,
        compiler_params=pltpu.CompilerParams(vmem_limit_bytes=VMEM_BYTES),
        name="unpack",
    )(core, parts, keep, come, *earlier)


def swap_sum(keep, give, axis):
    return keep.astype(F32) + lax.ppermute(give.astype(BF16), axis, SWAP).astype(F32)


def gather_plane(block):
    return lax.all_gather(block, PLANE, axis=0, tiled=True)


def spread_plane(parts):
    return lax.all_to_all(parts.reshape(4, -1, parts.shape[1]), PLANE, 0, 0, tiled=True)


def after(array, earlier):
    first = earlier[(slice(0, 1),) * earlier.ndim].reshape((1,) * array.ndim)
    return array + (first.astype(F32) * 0.0).astype(array.dtype)


def hold_kernel(*refs):
    del refs


def hold(array, earlier, cost=1):
    anywhere = pl.BlockSpec(memory_space=pl.ANY)
    return pl.pallas_call(
        hold_kernel,
        out_shape=jax.ShapeDtypeStruct(array.shape, array.dtype),
        in_specs=[anywhere] * 2,
        out_specs=anywhere,
        input_output_aliases={0: 0},
        cost_estimate=pl.CostEstimate(flops=cost, bytes_accessed=1, transcendentals=0),
        name="hold",
    )(array, earlier)


def pick_at(parts, index, axis):
    return lax.dynamic_index_in_dim(parts, index, axis, keepdims=False)


def pick(parts, index):
    return lax.dynamic_index_in_dim(parts, index, 0, keepdims=False)


def two(own, other, index):
    return jnp.where(index == 0, jnp.stack([own, other]), jnp.stack([other, own]))


def body(
    tokens,
    positions,
    w_qkv,
    qv_bias,
    w_attn_out,
    attn_out_bias,
    norm1_gain,
    norm1_bias,
    w_in,
    in_bias,
    w_out,
    out_bias,
    norm2_gain,
    norm2_bias,
    cotangent,
):
    seq_count, row_count, width = tokens.shape
    outer = lax.axis_size("e")
    seq_size = 2 * outer * GROUPS
    devices = seq_size * 4
    shard = w_qkv.shape[0]
    ff_shard = w_out.shape[0]
    ring = 4 * outer
    group = lax.axis_index(("r", "x"))
    place = lax.axis_index(("y", "c"))
    units = 2 * ring * ff_shard
    y_at, c_at = lax.axis_index("y"), lax.axis_index("c")
    qkv_cols = 3 * GROUP_WIDTH

    half = width // 2

    with jax.named_scope("gather_ff_weights"):
        if outer == 1:
            in_parts = spread_weights(w_in, w_attn_out, ring)
        else:
            in_cols = (
                w_in.reshape(shard, 2, ring, 4, 2 * ff_shard)
                .transpose(3, 1, 0, 2, 4)
                .reshape(4, 2, shard, units)
            )
            attn_cols = w_attn_out.reshape(shard, 2, half).transpose(1, 0, 2)
            in_parts = jnp.concatenate(
                [in_cols, jnp.broadcast_to(attn_cols, (4, 2, shard, half))], axis=3
            ).reshape(8, shard, units + half)
        in_parts = lax.all_to_all(
            in_parts, ("x", "y", "c"), 0, 0, tiled=True
        ).reshape(8 * shard, units + half)
        out_halves = w_out.reshape(ff_shard, 2, half).transpose(1, 0, 2)
        out_cols = two(
            pick(out_halves, c_at), lax.ppermute(pick(out_halves, 1 - c_at), "c", SWAP), c_at
        ).reshape(2 * ff_shard, half)
        packed = jnp.concatenate([in_parts, out_cols], axis=1)

    with jax.named_scope("gather_qkv_weights"):
        own_pos = lax.dynamic_slice_in_dim(positions, place * row_count, row_count, 1)
        shorts = jnp.stack(
            [
                qv_bias[0],
                qv_bias[1],
                attn_out_bias,
                norm1_gain,
                norm1_bias,
                out_bias,
                norm2_gain,
                norm2_bias,
            ]
        )
        spare = 64
        wide = qkv_cols + spare
        high = max(shard, 16)
        shift_rows = -(-2 * ff_shard // spare)
        smalls = jnp.concatenate(
            [
                jnp.broadcast_to(jnp.pad(shorts, ((0, 0), (0, spare - shard))), (2, 8, spare)),
                (own_pos >> 7).astype(BF16)[:, None],
                (own_pos & 127).astype(BF16)[:, None],
                jnp.broadcast_to(
                    jnp.pad(in_bias, (0, shift_rows * spare - 2 * ff_shard)).reshape(
                        shift_rows, spare
                    ),
                    (2, shift_rows, spare),
                ),
                jnp.zeros((2, high - 10 - shift_rows, spare), BF16),
            ],
            axis=1,
        )
        columns = (
            w_qkv.reshape(shard, 3, GROUPS, GROUP_WIDTH)
            .transpose(2, 0, 1, 3)
            .reshape(1, GROUPS, shard, qkv_cols)
        )
        columns = jnp.pad(columns, ((0, 0), (0, 0), (0, high - shard), (0, 0)))
        parcel = jnp.concatenate(
            [
                jnp.broadcast_to(columns, (2, GROUPS, high, qkv_cols)),
                jnp.broadcast_to(smalls[:, None], (2, GROUPS, high, spare)),
            ],
            axis=3,
        ).reshape(8, high, wide)
        parcel = lax.all_to_all(after(parcel, in_parts), SEQ_GROUP, 0, 0, tiled=True)

    with jax.named_scope("gather_tokens"):
        s_at, r_at, x_at = (lax.axis_index(name) for name in SEQ_GROUP)
        chunk = two(
            pick(tokens, s_at), lax.ppermute(pick(tokens, 1 - s_at), "s", SWAP), s_at
        )
        chunk = two(chunk, lax.ppermute(chunk, "r", SWAP), r_at)
        chunk = hold(chunk, packed)
        chunk = two(chunk, lax.ppermute(chunk, "x", SWAP), x_at)
        chunk = chunk.transpose(2, 1, 0, 3, 4).reshape(8 * row_count, width)

    with jax.named_scope("gather_qkv_weights"):
        parcels = lax.all_gather(hold(parcel, chunk), CHUNKS, axis=0, tiled=False)
        parcels = parcels.reshape(outer, 2, 2, 2, 2, 2, high, wide)
        order = (3, 0, 4, 5, 1, 2)
        qkv_slice = (
            parcels[..., :shard, :qkv_cols].transpose(*order, 6, 7).reshape(width, qkv_cols)
        )
        smalls = parcels[..., qkv_cols:]
        vectors = (
            smalls[..., :8, :shard].transpose(6, *order, 7).reshape(8, width).astype(F32)
        )
        pos_parts = smalls[..., 8:10, :row_count].astype(F32)
        chunk_pos = (pos_parts[..., 0, :] * 128.0 + pos_parts[..., 1, :]).reshape(
            outer, 2, 2, 8 * row_count
        )
        in_shift = pick_at(
            pick_at(smalls[..., 10 : 10 + shift_rows, :], x_at, 1), y_at, 1
        )
        in_shift = (
            in_shift.transpose(1, 0, 2, 3, 4, 5)
            .reshape(seq_size, shift_rows * spare)[:, : 2 * ff_shard]
            .reshape(2, units)
            .astype(F32)
        )

    with jax.named_scope("gather_ff_weights"):
        packed = lax.all_gather(packed, RING, axis=0, tiled=True)
        core = c_at.reshape(1).astype(jnp.int32)

    with jax.named_scope("project"):
        qv_slice = lax.dynamic_slice_in_dim(vectors[:2], group * GROUP_WIDTH, GROUP_WIDTH, 1)
        column_bias = jnp.concatenate(
            [qv_slice[0], jnp.zeros((GROUP_WIDTH,), F32), qv_slice[1]]
        )
        queries = (
            jnp.dot(chunk, qkv_slice[:, :GROUP_WIDTH], preferred_element_type=F32)
            + column_bias[:GROUP_WIDTH]
        ).astype(BF16)
        own_kv = (
            jnp.dot(chunk, qkv_slice[:, GROUP_WIDTH:], preferred_element_type=F32)
            + column_bias[GROUP_WIDTH:]
        ).astype(BF16)
    with jax.named_scope("gather_kv"):
        if outer > 1:
            own_kv = lax.all_gather(own_kv, "e", axis=0, tiled=True)
        y_kv = lax.ppermute(own_kv, "y", SWAP)
        key_values = [own_kv, lax.ppermute(own_kv, "c", SWAP)]
    ordered_pos = jnp.stack(
        [
            lax.dynamic_index_in_dim(
                lax.dynamic_index_in_dim(chunk_pos, y_at ^ ky, 1, keepdims=False),
                c_at ^ kc,
                1,
                keepdims=False,
            )
            for ky in (0, 1)
            for kc in (0, 1)
        ]
    )
    query_pos = lax.dynamic_index_in_dim(ordered_pos[0], lax.axis_index("e"), 0, keepdims=True)
    key_pos = ordered_pos.reshape(4 * outer, 8 * row_count)
    head_ids = group * GROUP_HEADS + jnp.arange(GROUP_HEADS)
    slopes = 2.0 ** (-8.0 * (head_ids + 1).astype(F32) / HEADS) * LOG2E

    with jax.named_scope("attention"):
        span = outer
        parts = ((0, 2), (2, 3), (3, 4))
        state = None
        for number, (first, last) in enumerate(parts):
            state = attend(
                slopes,
                queries,
                query_pos,
                key_pos[first * span : last * span],
                key_values[first:last],
                state,
                last=last == 4,
                earlier=(vectors, in_shift) if number == 1 else (),
            )
            if number == 0:
                y_kv = hold(y_kv, state[0])
                key_values += [y_kv, lax.ppermute(y_kv, "c", SWAP)]
        attended, log_sums, attended_low = state

    with jax.named_scope("return_attended"):
        returned = lax.all_to_all(
            attended_low.reshape(8, row_count, GROUP_WIDTH), SEQ_GROUP, 0, 0, tiled=True
        )
    with jax.named_scope("first_norm"):
        packed = hold(packed, returned)
        attn_own = packed[:, units : units + half]
        attn_swap = lax.ppermute(attn_own, "c", SWAP)
        hidden_low, hidden, normal, scale = first_norm(
            core,
            returned,
            tokens.reshape(2 * row_count, width),
            vectors,
            attn_own,
            attn_swap,
        )
        packed = hold(packed, hidden_low)
        swapped = lax.ppermute(packed, "c", SWAP)
    with jax.named_scope("gather_hidden"):
        hidden_group = gather_plane(hidden_low)
    with jax.named_scope("ff_forward"):
        activated_low, slope, gelu, ff_parts = ff_forward(
            core,
            hidden_group,
            in_shift,
            packed,
            swapped,
            slice(units + half, units + width),
        )
    with jax.named_scope("sum_ff"):
        ff_parts = spread_plane(ff_parts)
    with jax.named_scope("second_norm"):
        result, second_grad, ff_grad, sums = second_norm(
            ff_parts, hidden, cotangent.reshape(2 * row_count, width), vectors
        )
    with jax.named_scope("gather_ff_grad"):
        ff_grads = gather_plane(ff_grad)
    with jax.named_scope("ff_backward"):
        joined_grad, hidden_parts, grad_in_shift, grad_halves = ff_backward(
            core, ff_grads, slope, gelu, packed, swapped, slice(units + half, units + width)
        )
    with jax.named_scope("sum_hidden_grad"):
        hidden_parts = spread_plane(hidden_parts)
    with jax.named_scope("ff_weight_grads"):
        keep, give = ff_grads_of(core, activated_low, grad_halves, hidden_group, joined_grad)
        ff_keep, ff_give = keep, give
    with jax.named_scope("first_norm_back"):
        first_grad, out_grad, keep, give = first_back(
            core,
            hidden_parts,
            second_grad,
            normal,
            scale,
            vectors,
            attn_own,
            attn_swap,
            sums,
            returned,
            ff_keep,
        )
    with jax.named_scope("send_out_grad"):
        out_grads = lax.all_to_all(out_grad, SEQ_GROUP, 0, 0, tiled=True).reshape(
            8 * row_count, GROUP_WIDTH
        )
    with jax.named_scope("attn_weight_grad"):
        rows = jnp.concatenate(
            [swap_sum(keep, give, "c"), swap_sum(ff_keep, ff_give, "c")], axis=1
        ).astype(BF16)
        rows = hold(rows, out_grads)
        row_sums = lax.psum_scatter(rows, RING, scatter_dimension=0, tiled=True)

    with jax.named_scope("attention_back"):
        state, c_part, y_part, cy_part = attend_back(
            slopes,
            queries,
            query_pos,
            key_pos[span:],
            out_grads,
            attended,
            log_sums,
            key_values[1:],
            None,
            last=False,
            earlier=(rows,),
        )
        y_sum = swap_sum(y_part, cy_part, "c").astype(BF16)
        query_grads, own_part = attend_back(
            slopes,
            queries,
            query_pos,
            key_pos[:span],
            out_grads,
            attended,
            log_sums,
            key_values[:1],
            state,
            last=True,
            earlier=(y_sum,),
        )
    with jax.named_scope("sum_kv_grads"):
        from_c = lax.ppermute(c_part, "c", SWAP)
        from_y = lax.ppermute(y_sum, "y", SWAP)
        if outer > 1:
            total = own_part.astype(F32) + from_c.astype(F32) + from_y.astype(F32)
            own_part = lax.psum_scatter(
                total, "e", scatter_dimension=0, tiled=True
            ).astype(BF16)
            from_c = from_y = jnp.zeros_like(own_part)

    with jax.named_scope("input_back"):
        spot = jnp.stack([c_at, y_at, x_at]).astype(jnp.int32)
        input_keep, input_give, qkv_grad = input_back(
            spot, query_grads, own_part, from_c, from_y, qkv_slice
        )
    with jax.named_scope("qkv_weight_grad"):
        keep, give = qkv_weight(
            spot,
            chunk,
            qkv_grad,
            grad_in_shift.reshape(seq_size, 2 * ff_shard),
        )
        bundle = swap_sum(keep, give, "c").astype(BF16)
        from_x = lax.ppermute(input_give, "x", SWAP)
        parts = (hold(input_keep, bundle).astype(F32) + from_x.astype(F32)).reshape(
            2, 2, row_count, width
        )
        bundle = swap_sum(pick(bundle, y_at), pick(bundle, 1 - y_at), "y").astype(BF16)
        ends = width // 4 + seq_size
        shares = jnp.concatenate(
            [
                bundle[: width // 4].reshape(seq_size, shard, qkv_cols),
                jnp.broadcast_to(bundle[ends : ends + 1], (seq_size, 1, qkv_cols)),
                bundle[width // 4 : ends][:, None],
                jnp.zeros((seq_size, 6, qkv_cols), BF16),
            ],
            axis=1,
        )
    with jax.named_scope("input_grad"):
        from_r = lax.ppermute(
            hold(pick_at(parts, 1 - r_at, 1).astype(BF16), row_sums), "r", SWAP
        )
        parts = hold(pick_at(parts, r_at, 1), shares) + from_r.astype(F32)
    with jax.named_scope("qkv_weight_grad"):
        shares = lax.all_to_all(shares, SEQ_AXIS, 0, 0, tiled=True)
        from_s = lax.ppermute(
            hold(pick(parts, 1 - s_at).astype(BF16), shares), "s", SWAP
        )
    with jax.named_scope("ff_weight_grads"):
        own_cols = half + 128 + units
        row_sums = hold(row_sums, shares)
        plane_rows = row_sums[:, :own_cols].reshape(8, shard, own_cols)
    with jax.named_scope("qkv_weight_grad"):
        first_col = lax.axis_index(EVERY) * shard
        if outer == 1:
            grad_w_qkv, grad_qv, grad_in_bias = share(
                first_col.reshape(1).astype(jnp.int32), hold(shares, plane_rows), shard, 2 * ff_shard
            )
            grad_in_bias = grad_in_bias[0]
        else:
            totals = jnp.sum(
                shares.astype(F32).reshape(2 * outer, GROUPS, shard + 8, qkv_cols), axis=0
            )
            grad_w_qkv = (
                totals[:, :shard]
                .reshape(GROUPS, shard, 3, GROUP_WIDTH)
                .transpose(1, 2, 0, 3)
                .reshape(shard, 3 * width)
            )
            sums = (
                totals[:, shard].reshape(GROUPS, 3, GROUP_WIDTH).transpose(1, 0, 2).reshape(3, width)
            )
            grad_qv = lax.dynamic_slice_in_dim(sums[0::2], first_col, shard, 1)
            grad_in_bias = jnp.sum(totals[:, shard + 1, : 2 * ff_shard], axis=0)
    with jax.named_scope("input_grad"):
        input_grad = first_grad.reshape(2, row_count, width) + two(
            pick(parts, s_at), from_s.astype(F32), s_at
        )
    with jax.named_scope("ff_weight_grads"):
        exchanged = lax.all_to_all(
            plane_rows, ("x", "y", "c"), 0, 0, tiled=True
        ).reshape(4, 2, shard, own_cols)
        out_sums = row_sums[:, own_cols:].reshape(2, ff_shard, half)
        out_come = lax.ppermute(pick(out_sums, 1 - c_at), "c", SWAP)
        out_keep = pick(out_sums, c_at)
        if outer == 1:
            grad_w_in, grad_w_attn, grad_w_out, *vector_grads = unpack(
                core, exchanged, out_keep, out_come, half, ring, grad_w_qkv, input_grad
            )
            vector_grads = [row.reshape(shard) for row in vector_grads]
        else:
            grad_w_in = (
                exchanged[..., half + 128 :]
                .reshape(4, 2, shard, ring, 2 * ff_shard)
                .transpose(2, 1, 3, 0, 4)
                .reshape(shard, 2 * devices * ff_shard)
                .astype(F32)
            )
            grad_w_attn = (
                jnp.sum(exchanged[..., :half].astype(F32), axis=0)
                .transpose(1, 0, 2)
                .reshape(shard, width)
            )
            vector_grads = jnp.sum(exchanged[:, 0, :, half : half + 8].astype(F32), axis=0).T
            grad_w_out = (
                two(out_keep, out_come, c_at)
                .transpose(1, 0, 2)
                .reshape(ff_shard, width)
                .astype(F32)
            )
    return (
        result.reshape(2, row_count, width).astype(BF16),
        input_grad,
        grad_w_qkv,
        grad_qv,
        grad_w_attn,
        vector_grads[0],
        vector_grads[1],
        vector_grads[2],
        grad_w_in,
        grad_in_bias,
        grad_w_out,
        vector_grads[3],
        vector_grads[4],
        vector_grads[5],
    )


def solution(mesh):
    seq_size = mesh.shape["seq"]
    split = Mesh(mesh.devices.reshape(2, seq_size // 8, 2, 2, 2, 2), EVERY)
    tokens_at = P(None, EVERY, None)
    rows_at = P(EVERY, None)
    vector_at = P(EVERY)
    return jax.shard_map(
        body,
        mesh=split,
        in_specs=(
            tokens_at,
            P(None, SEQ_AXIS),
            rows_at,
            P(None, EVERY),
            rows_at,
            vector_at,
            vector_at,
            vector_at,
            rows_at,
            vector_at,
            rows_at,
            vector_at,
            vector_at,
            vector_at,
            tokens_at,
        ),
        out_specs=(
            tokens_at,
            tokens_at,
            rows_at,
            P(None, EVERY),
            rows_at,
            vector_at,
            vector_at,
            vector_at,
            rows_at,
            vector_at,
            rows_at,
            vector_at,
            vector_at,
            vector_at,
        ),
        check_vma=False,
    )
```

```python
import functools

import jax
import jax.numpy as jnp
from jax import lax
from jax.experimental import pallas as pl
from jax.experimental.pallas import tpu as pltpu
from jax.sharding import Mesh
from jax.sharding import PartitionSpec as P

HEADS = 12
HEAD_DIM = 64
GROUPS = 4
GROUP_HEADS = HEADS // GROUPS
GROUP_WIDTH = GROUP_HEADS * HEAD_DIM
EPSILON = 1e-12
SCORE_SCALE = 0.125
LOG2E = 1.4426950408889634
LOWEST = -1e30
GRAD_TILE = 256
KEY_BLOCK = 512
FF_TILE = 256
SEQ_GROUP = ("s", "r", "x")
CHUNKS = ("e", "y", "c")
RING = ("s", "e", "r")
PLANE = ("x", "y")
SEQ_AXIS = ("s", "e", "r", "x")
EVERY = ("s", "e", "r", "x", "y", "c")
SWAP = ((0, 1), (1, 0))
BF16 = jnp.bfloat16
F32 = jnp.float32
VMEM_BYTES = 60 * 2**20


def nt(a, b):
    return lax.dot_general(a, b, (((1,), (1,)), ((), ())), preferred_element_type=F32)


def tn(a, b):
    return lax.dot_general(a, b, (((0,), (0,)), ((), ())), preferred_element_type=F32)


def nn(a, b):
    return lax.dot_general(a, b, (((1,), (0,)), ((), ())), preferred_element_type=F32)


def head_cols(head, base=0):
    return slice(base + head * HEAD_DIM, base + (head + 1) * HEAD_DIM)


def log2_scores(keys, queries, slope, key_pos, query_pos):
    products = nt(keys, queries)
    distances = jnp.abs(key_pos * slope - query_pos * slope)
    return products * (SCORE_SCALE * LOG2E) - distances


def column(row):
    return jnp.broadcast_to(row, (8, row.shape[1])).T[:, :1]


def key_blocks(kv_refs):
    start = 0
    for piece in kv_refs:
        yield piece, start
        start += piece.shape[0]


def turn_positions(pk_ref, column_ref):
    length = pk_ref.shape[1]

    def turn(row, carry):
        at = pl.ds(pl.multiple_of(row * length, length), length)
        column_ref[at, :] = column(pk_ref[pl.ds(row, 1), :])
        return carry

    lax.fori_loop(0, pk_ref.shape[0], turn, 0)


def attend_kernel(deps, count, first, last, slopes_ref, q_ref, pq_ref, pk_ref, *refs):
    refs = refs[deps:]
    kv_refs, refs = refs[:count], refs[count:]
    if not first:
        (sum_in_ref, stat_in_ref), refs = refs[:2], refs[2:]
    sum_ref, stat_ref = refs[:2]
    column_ref = refs[-1]
    rows = q_ref.shape[0]
    query_pos = pq_ref[...]
    turn_positions(pk_ref, column_ref)
    for head in range(GROUP_HEADS):
        slope = slopes_ref[head]
        queries = q_ref[:, head_cols(head)]
        if first:
            carry = (
                jnp.full((1, rows), LOWEST, F32),
                jnp.zeros((1, rows), F32),
                jnp.zeros((HEAD_DIM, rows), F32),
            )
        else:
            carry = (
                stat_in_ref[head : head + 1, :],
                stat_in_ref[GROUP_HEADS + head : GROUP_HEADS + head + 1, :],
                sum_in_ref[head_cols(head), :],
            )
        for kv_ref, start in key_blocks(kv_refs):

            def visit(block, carry, kv_ref=kv_ref, start=start):
                top, total, summed = carry
                at = pl.ds(pl.multiple_of(block * KEY_BLOCK, KEY_BLOCK), KEY_BLOCK)
                pos_at = pl.ds(
                    pl.multiple_of(start + block * KEY_BLOCK, KEY_BLOCK), KEY_BLOCK
                )
                keys = kv_ref[at, head_cols(head)]
                values = kv_ref[at, head_cols(head, GROUP_WIDTH)]
                scores = log2_scores(keys, queries, slope, column_ref[pos_at, :], query_pos)
                new_top = jnp.maximum(top, jnp.max(scores, axis=0, keepdims=True))
                weights = jnp.exp2(scores - new_top)
                shrink = jnp.exp2(top - new_top)
                total = total * shrink + jnp.sum(weights, axis=0, keepdims=True)
                summed = summed * shrink + tn(values, weights.astype(BF16))
                return new_top, total, summed

            carry = lax.fori_loop(0, kv_ref.shape[0] // KEY_BLOCK, visit, carry)
        top, total, summed = carry
        if last:
            attended = summed / total
            sum_ref[head_cols(head), :] = attended
            refs[2][:, head_cols(head)] = attended.T.astype(BF16)
            stat_ref[head : head + 1, :] = top + jnp.log2(total)
        else:
            sum_ref[head_cols(head), :] = summed
            stat_ref[head : head + 1, :] = top
            stat_ref[GROUP_HEADS + head : GROUP_HEADS + head + 1, :] = total


def attend(slopes, queries, query_pos, key_pos, key_values, state, last, earlier):
    rows, length = queries.shape[0], key_pos.size
    vmem = pl.BlockSpec(memory_space=pltpu.VMEM)
    count = len(key_values)
    first = state is None
    state = () if first else state
    outs = [
        jax.ShapeDtypeStruct((GROUP_WIDTH, rows), F32),
        jax.ShapeDtypeStruct((GROUP_HEADS * (1 if last else 2), rows), F32),
    ]
    if last:
        outs.append(jax.ShapeDtypeStruct((rows, GROUP_WIDTH), BF16))
    return pl.pallas_call(
        functools.partial(attend_kernel, len(earlier), count, first, last),
        out_shape=tuple(outs),
        in_specs=[pl.BlockSpec(memory_space=pltpu.SMEM)]
        + [vmem] * 3
        + [pl.BlockSpec(memory_space=pl.ANY)] * len(earlier)
        + [vmem] * (count + len(state)),
        out_specs=(vmem,) * len(outs),
        scratch_shapes=[pltpu.VMEM((length, 1), F32)],
        compiler_params=pltpu.CompilerParams(vmem_limit_bytes=VMEM_BYTES),
        cost_estimate=pl.CostEstimate(
            flops=64 * rows * length * GROUP_WIDTH,
            bytes_accessed=rows * length,
            transcendentals=rows * length * GROUP_HEADS,
        ),
        name="attend",
    )(slopes, queries, query_pos, key_pos, *earlier, *key_values, *state)


def attend_back_kernel(
    deps, count, first, last, slopes_ref, q_ref, pq_ref, pk_ref, do_ref, out_ref, lse_ref, *refs
):
    refs = refs[deps:]
    kv_refs, refs = refs[:count], refs[count:]
    if not first:
        dq_in_ref, refs = refs[0], refs[1:]
    dq_ref, dkv_refs, column_ref = refs[0], refs[1 : count + 1], refs[-1]
    rows = q_ref.shape[0]
    query_pos = pq_ref[...]
    turn_positions(pk_ref, column_ref)
    for head in range(GROUP_HEADS):
        slope = slopes_ref[head]
        queries = q_ref[:, head_cols(head)]
        out_grads = do_ref[:, head_cols(head)]
        log_sum = lse_ref[head : head + 1, :]
        delta = jnp.sum(
            out_grads.astype(F32).T * out_ref[head_cols(head), :], axis=0, keepdims=True
        )
        if first:
            query_grads = jnp.zeros((HEAD_DIM, rows), F32)
        else:
            query_grads = dq_in_ref[head_cols(head), :]
        for (kv_ref, start), dkv_ref in zip(key_blocks(kv_refs), dkv_refs):

            def visit(block, query_grads, kv_ref=kv_ref, start=start, dkv_ref=dkv_ref):
                at = pl.ds(pl.multiple_of(block * KEY_BLOCK, KEY_BLOCK), KEY_BLOCK)
                pos_at = pl.ds(
                    pl.multiple_of(start + block * KEY_BLOCK, KEY_BLOCK), KEY_BLOCK
                )
                keys = kv_ref[at, head_cols(head)]
                values = kv_ref[at, head_cols(head, GROUP_WIDTH)]
                scores = log2_scores(keys, queries, slope, column_ref[pos_at, :], query_pos)
                probs = jnp.exp2(scores - log_sum)
                prob_grads = nt(values, out_grads)
                score_grads = (probs * (prob_grads - delta)).astype(BF16)
                dkv_ref[at, head_cols(head, GROUP_WIDTH)] = nn(
                    probs.astype(BF16), out_grads
                ).astype(BF16)
                dkv_ref[at, head_cols(head)] = (nn(score_grads, queries) * SCORE_SCALE).astype(
                    BF16
                )
                return query_grads + tn(keys, score_grads)

            query_grads = lax.fori_loop(0, kv_ref.shape[0] // KEY_BLOCK, visit, query_grads)
        if last:
            dq_ref[:, head_cols(head)] = (query_grads * SCORE_SCALE).T.astype(BF16)
        else:
            dq_ref[head_cols(head), :] = query_grads


def attend_back(
    slopes,
    queries,
    query_pos,
    key_pos,
    out_grads,
    attended,
    log_sums,
    key_values,
    state,
    last,
    earlier,
):
    rows, length = queries.shape[0], key_pos.size
    vmem = pl.BlockSpec(memory_space=pltpu.VMEM)
    count = len(key_values)
    first = state is None
    state = () if first else (state,)
    query_out = (
        jax.ShapeDtypeStruct((rows, GROUP_WIDTH), BF16)
        if last
        else jax.ShapeDtypeStruct((GROUP_WIDTH, rows), F32)
    )
    return pl.pallas_call(
        functools.partial(attend_back_kernel, len(earlier), count, first, last),
        out_shape=(query_out,)
        + tuple(jax.ShapeDtypeStruct(piece.shape, BF16) for piece in key_values),
        in_specs=[pl.BlockSpec(memory_space=pltpu.SMEM)]
        + [vmem] * 6
        + [pl.BlockSpec(memory_space=pl.ANY)] * len(earlier)
        + [vmem] * (count + len(state)),
        out_specs=(vmem,) * (1 + count),
        scratch_shapes=[pltpu.VMEM((length, 1), F32)],
        compiler_params=pltpu.CompilerParams(vmem_limit_bytes=VMEM_BYTES),
        cost_estimate=pl.CostEstimate(
            flops=84 * rows * length * GROUP_WIDTH,
            bytes_accessed=rows * length,
            transcendentals=rows * length * GROUP_HEADS,
        ),
        name="attend_back",
    )(
        slopes,
        queries,
        query_pos,
        key_pos,
        out_grads,
        attended,
        log_sums,
        *earlier,
        *key_values,
        *state,
    )


def merged(parts_ref):
    return jnp.concatenate(
        [
            jnp.concatenate(
                [parts_ref[seq * GROUPS + group] for group in range(GROUPS)], axis=1
            )
            for seq in range(2)
        ]
    )


def first_norm_kernel(
    core_ref,
    mixed_ref,
    rows_ref,
    vec_ref,
    own_ref,
    swap_ref,
    low_ref,
    hidden_ref,
    normal_ref,
    scale_ref,
):
    mixed = merged(mixed_ref)
    first = core_ref[0] == 0
    own, swap = nn(mixed, own_ref[...]), nn(mixed, swap_ref[...])
    lin = jnp.concatenate([jnp.where(first, own, swap), jnp.where(first, swap, own)], axis=1)
    total = rows_ref[...].astype(F32) + (lin + vec_ref[2:3, :])
    normal, scale = normalised(total)
    hidden = normal * vec_ref[3:4, :] + vec_ref[4:5, :]
    low_ref[...] = hidden.astype(BF16)
    hidden_ref[...] = hidden
    normal_ref[...] = normal
    scale_ref[...] = scale


def normalised(values):
    centred = values - jnp.mean(values, axis=1, keepdims=True)
    variance = jnp.mean(centred * centred, axis=1, keepdims=True)
    scale = lax.rsqrt(variance + EPSILON)
    return centred * scale, scale


def norm_back(grads, normal, scale, gain):
    scaled = grads * gain
    return (
        scaled
        - jnp.mean(scaled, axis=1, keepdims=True)
        - normal * jnp.mean(scaled * normal, axis=1, keepdims=True)
    ) * scale


def column_sum(values):
    return jnp.sum(values, axis=0, keepdims=True)


def first_norm(core, mixed, rows, vectors, own, swap):
    tokens, width = rows.shape
    vmem = pl.BlockSpec(memory_space=pltpu.VMEM)
    return pl.pallas_call(
        first_norm_kernel,
        out_shape=(
            jax.ShapeDtypeStruct((tokens, width), BF16),
            jax.ShapeDtypeStruct((tokens, width), F32),
            jax.ShapeDtypeStruct((tokens, width), F32),
            jax.ShapeDtypeStruct((tokens, 1), F32),
        ),
        in_specs=[pl.BlockSpec(memory_space=pltpu.SMEM)] + [vmem] * 5,
        out_specs=(vmem,) * 4,
        compiler_params=pltpu.CompilerParams(vmem_limit_bytes=VMEM_BYTES),
        cost_estimate=pl.CostEstimate(
            flops=64 * tokens * width * width, bytes_accessed=4 * width * width, transcendentals=0
        ),
        name="first_norm",
    )(core, mixed, rows, vectors, own, swap)


def ff_forward_kernel(
    units, out_columns, core_ref, hidden_ref, bias_ref, own_ref, swap_ref, act_ref, slope_ref, gelu_ref, parts_ref
):
    tokens = hidden_ref.shape[0]
    first = core_ref[0] == 0

    def visit(tile, carry):
        at = pl.ds(pl.multiple_of(tile * FF_TILE, FF_TILE), FF_TILE)
        rows = hidden_ref[at, :]
        own = nn(rows, own_ref[:, :units])
        swap = nn(rows, swap_ref[:, :units])
        gate = jnp.where(first, own, swap) + bias_ref[0:1, :]
        up = jnp.where(first, swap, own) + bias_ref[1:2, :]
        cdf = 0.5 * (1.0 + lax.erf(gate * (0.5**0.5)))
        density = jnp.exp(-0.5 * gate * gate) * 0.3989422804014327
        gelu = gate * cdf
        act = (gelu * up).astype(BF16)
        act_ref[at, :] = act
        gelu_ref[at, :] = gelu.astype(BF16)
        slope_ref[at, :] = (up * (cdf + gate * density)).astype(BF16)
        own = nn(act, own_ref[:, out_columns]).astype(BF16)
        swap = nn(act, swap_ref[:, out_columns]).astype(BF16)
        parts_ref[at, :] = jnp.concatenate(
            [jnp.where(first, own, swap), jnp.where(first, swap, own)], axis=1
        )
        return carry

    lax.fori_loop(0, tokens // FF_TILE, visit, 0)


def ff_forward(core, hidden, bias, own, swap, out_columns):
    tokens, width = hidden.shape
    units = bias.shape[1]
    vmem = pl.BlockSpec(memory_space=pltpu.VMEM)
    return pl.pallas_call(
        functools.partial(ff_forward_kernel, units, out_columns),
        out_shape=(
            jax.ShapeDtypeStruct((tokens, units), BF16),
            jax.ShapeDtypeStruct((tokens, units), BF16),
            jax.ShapeDtypeStruct((tokens, units), BF16),
            jax.ShapeDtypeStruct((tokens, width), BF16),
        ),
        in_specs=[pl.BlockSpec(memory_space=pltpu.SMEM)] + [vmem] * 4,
        out_specs=(vmem,) * 4,
        compiler_params=pltpu.CompilerParams(vmem_limit_bytes=VMEM_BYTES),
        cost_estimate=pl.CostEstimate(
            flops=32 * tokens * width * units,
            bytes_accessed=6 * width * units,
            transcendentals=2 * tokens * units,
        ),
        name="ff_forward",
    )(core, hidden, bias, own, swap)


def second_norm_kernel(
    parts_ref, hidden_ref, cotangent_ref, vec_ref, result_ref, grad_ref, low_ref, sums_ref
):
    lin = jnp.sum(parts_ref[...].astype(F32), axis=0) + vec_ref[5:6, :]
    normal, scale = normalised(hidden_ref[...] + lin)
    gain = vec_ref[6:7, :]
    result_ref[...] = (normal * gain + vec_ref[7:8, :]).astype(BF16)
    grads = cotangent_ref[...].astype(F32)
    back = norm_back(grads, normal, scale, gain)
    low = back.astype(BF16)
    grad_ref[...] = back
    low_ref[...] = low
    sums_ref[...] = jnp.concatenate(
        [
            column_sum(low.astype(F32)),
            column_sum(grads * normal),
            column_sum(grads),
            jnp.zeros((5, back.shape[1]), F32),
        ]
    )


def second_norm(parts, hidden, cotangent, vectors):
    tokens, width = hidden.shape
    vmem = pl.BlockSpec(memory_space=pltpu.VMEM)
    return pl.pallas_call(
        second_norm_kernel,
        out_shape=(
            jax.ShapeDtypeStruct((tokens, width), BF16),
            jax.ShapeDtypeStruct((tokens, width), F32),
            jax.ShapeDtypeStruct((tokens, width), BF16),
            jax.ShapeDtypeStruct((8, width), F32),
        ),
        in_specs=[vmem] * 4,
        out_specs=(vmem,) * 4,
        compiler_params=pltpu.CompilerParams(vmem_limit_bytes=VMEM_BYTES),
        cost_estimate=pl.CostEstimate(
            flops=20000 * tokens * width, bytes_accessed=20 * tokens * width, transcendentals=0
        ),
        name="second_norm",
    )(parts, hidden, cotangent, vectors)


def ff_backward_kernel(
    units,
    out_columns,
    core_ref,
    grad_ref,
    slope_ref,
    gelu_ref,
    own_ref,
    swap_ref,
    joined_ref,
    parts_ref,
    bias_ref,
    half_ref,
):
    tokens, width = grad_ref.shape
    half = width // 2
    first = core_ref[0] == 0
    bias_ref[...] = jnp.zeros_like(bias_ref)

    def visit(tile, carry):
        at = pl.ds(pl.multiple_of(tile * FF_TILE, FF_TILE), FF_TILE)
        left, right = grad_ref[at, :half], grad_ref[at, half:]
        half_ref[0, at, :] = left
        half_ref[1, at, :] = right
        act_grad = nt(jnp.where(first, left, right), own_ref[:, out_columns]) + nt(
            jnp.where(first, right, left), swap_ref[:, out_columns]
        )
        joined = []
        for which, factor in ((0, slope_ref), (1, gelu_ref)):
            side = (act_grad * factor[at, :].astype(F32)).astype(BF16)
            joined_ref[which, at, :] = side
            bias_ref[which : which + 1, :] += column_sum(side.astype(F32))
            joined.append(side)
        parts_ref[at, :] = (
            nt(jnp.where(first, joined[0], joined[1]), own_ref[:, :units])
            + nt(jnp.where(first, joined[1], joined[0]), swap_ref[:, :units])
        ).astype(BF16)
        return carry

    lax.fori_loop(0, tokens // FF_TILE, visit, 0)


def ff_backward(core, grads, slope, gelu, own, swap, out_columns):
    tokens, width = grads.shape
    units = slope.shape[1]
    vmem = pl.BlockSpec(memory_space=pltpu.VMEM)
    return pl.pallas_call(
        functools.partial(ff_backward_kernel, units, out_columns),
        out_shape=(
            jax.ShapeDtypeStruct((2, tokens, units), BF16),
            jax.ShapeDtypeStruct((tokens, width), BF16),
            jax.ShapeDtypeStruct((2, units), F32),
            jax.ShapeDtypeStruct((2, tokens, width // 2), BF16),
        ),
        in_specs=[pl.BlockSpec(memory_space=pltpu.SMEM)] + [vmem] * 5,
        out_specs=(vmem,) * 4,
        compiler_params=pltpu.CompilerParams(vmem_limit_bytes=VMEM_BYTES),
        cost_estimate=pl.CostEstimate(
            flops=32 * tokens * width * units,
            bytes_accessed=6 * width * units,
            transcendentals=0,
        ),
        name="ff_backward",
    )(core, grads, slope, gelu, own, swap)


def ff_grads_kernel(core_ref, act_ref, half_ref, hidden_ref, joined_ref, keep_ref, give_ref):
    core = core_ref[0]
    units = joined_ref.shape[2]

    def visit(tile, carry):
        at = pl.ds(pl.multiple_of(tile * GRAD_TILE, GRAD_TILE), GRAD_TILE)
        hidden = hidden_ref[:, at]
        act = act_ref[:, at]
        give_ref[at, :units] = tn(hidden, joined_ref[1 - core]).astype(BF16)
        give_ref[at, units:] = tn(act, half_ref[1 - core]).astype(BF16)
        keep_ref[at, :units] = tn(hidden, joined_ref[core]).astype(BF16)
        keep_ref[at, units:] = tn(act, half_ref[core]).astype(BF16)
        return carry

    lax.fori_loop(0, hidden_ref.shape[1] // GRAD_TILE, visit, 0)


def ff_grads_of(core, act, halves, hidden, joined):
    width = hidden.shape[1]
    cols = joined.shape[2] + halves.shape[2]
    vmem = pl.BlockSpec(memory_space=pltpu.VMEM)
    return pl.pallas_call(
        ff_grads_kernel,
        out_shape=(jax.ShapeDtypeStruct((width, cols), BF16),) * 2,
        in_specs=[pl.BlockSpec(memory_space=pltpu.SMEM)] + [vmem] * 4,
        out_specs=(vmem,) * 2,
        compiler_params=pltpu.CompilerParams(vmem_limit_bytes=VMEM_BYTES),
        cost_estimate=pl.CostEstimate(flops=6 * 10**9, bytes_accessed=10**4, transcendentals=0),
        name="ff_grads",
    )(core, act, halves, hidden, joined)


def first_back_kernel(
    core_ref,
    parts_ref,
    second_ref,
    normal_ref,
    scale_ref,
    vec_ref,
    own_ref,
    swap_ref,
    sums_ref,
    mixed_ref,
    _,
    grad_ref,
    out_ref,
    keep_ref,
    give_ref,
):
    tokens, width = second_ref.shape
    half, count = width // 2, tokens // 2
    normal = normal_ref[...]
    grads = second_ref[...] + jnp.sum(parts_ref[...].astype(F32), axis=0)
    back = norm_back(grads, normal, scale_ref[...], vec_ref[3:4, :])
    low = back.astype(BF16)
    grad_ref[...] = back
    own_left = core_ref[0] == 0
    left, right = low[:, :half], low[:, half:]
    out_grad = nt(jnp.where(own_left, left, right), own_ref[...]) + nt(
        jnp.where(own_left, right, left), swap_ref[...]
    )
    for seq in range(2):
        for group in range(GROUPS):
            out_ref[seq * GROUPS + group] = out_grad[
                seq * count : (seq + 1) * count, group * GROUP_WIDTH : (group + 1) * GROUP_WIDTH
            ].astype(BF16)
    rows = jnp.concatenate(
        [
            column_sum(low.astype(F32)),
            column_sum(grads * normal),
            column_sum(grads),
            sums_ref[0:3, :],
            jnp.zeros((122, width), F32),
        ]
    )
    turned = rows.T.astype(BF16)
    keep_ref[:, half:] = turned
    give_ref[:, half:] = turned
    mixed = merged(mixed_ref)
    left = tn(mixed, low[:, :half]).astype(BF16)
    right = tn(mixed, low[:, half:]).astype(BF16)
    keep_ref[:, :half] = jnp.where(own_left, left, right)
    give_ref[:, :half] = jnp.where(own_left, right, left)


def first_back(
    core, parts, second_grad, normal, scale, vectors, own, swap, sums, mixed, earlier
):
    tokens, width = second_grad.shape
    vmem = pl.BlockSpec(memory_space=pltpu.VMEM)
    return pl.pallas_call(
        first_back_kernel,
        out_shape=(
            jax.ShapeDtypeStruct((tokens, width), F32),
            jax.ShapeDtypeStruct((2 * GROUPS, tokens // 2, GROUP_WIDTH), BF16),
            jax.ShapeDtypeStruct((width, width // 2 + 128), BF16),
            jax.ShapeDtypeStruct((width, width // 2 + 128), BF16),
        ),
        in_specs=[pl.BlockSpec(memory_space=pltpu.SMEM)]
        + [vmem] * 9
        + [pl.BlockSpec(memory_space=pl.ANY)],
        out_specs=(vmem,) * 4,
        compiler_params=pltpu.CompilerParams(vmem_limit_bytes=VMEM_BYTES),
        cost_estimate=pl.CostEstimate(
            flops=64 * tokens * width * width, bytes_accessed=4 * width * width, transcendentals=0
        ),
        name="first_back",
    )(core, parts, second_grad, normal, scale, vectors, own, swap, sums, mixed, earlier)


def input_back_kernel(place_ref, grad_ref, weight_ref, keep_ref, give_ref):
    inputs = nt(grad_ref[...], weight_ref[...]).astype(BF16)
    pairs, count = keep_ref.shape[0], keep_ref.shape[1]
    own_first = place_ref[2] == 0
    for pair in range(pairs):
        first = inputs[2 * pair * count : (2 * pair + 1) * count]
        second = inputs[(2 * pair + 1) * count : (2 * pair + 2) * count]
        keep_ref[pair] = jnp.where(own_first, first, second)
        give_ref[pair] = jnp.where(own_first, second, first)


def input_back(place, grads, weight):
    tokens = grads.shape[0]
    width, cols = weight.shape
    vmem = pl.BlockSpec(memory_space=pltpu.VMEM)
    return pl.pallas_call(
        input_back_kernel,
        out_shape=(
            jax.ShapeDtypeStruct((4, tokens // 8, width), BF16),
            jax.ShapeDtypeStruct((4, tokens // 8, width), BF16),
        ),
        in_specs=[pl.BlockSpec(memory_space=pltpu.SMEM)] + [vmem] * 2,
        out_specs=(vmem,) * 2,
        compiler_params=pltpu.CompilerParams(vmem_limit_bytes=VMEM_BYTES),
        cost_estimate=pl.CostEstimate(
            flops=10 * tokens * width * cols, bytes_accessed=4 * tokens * width, transcendentals=0
        ),
        name="input_back",
    )(place, grads, weight)


def qkv_weight_kernel(
    place_ref,
    dq_ref,
    own_ref,
    c_ref,
    y_ref,
    chunk_ref,
    shift_ref,
    keep_ref,
    give_ref,
    grad_ref,
):
    kv_grad = own_ref[...].astype(F32) + c_ref[...].astype(F32) + y_ref[...].astype(F32)
    grads = jnp.concatenate([dq_ref[...], kv_grad.astype(BF16)], axis=1)
    grad_ref[...] = grads
    weights = tn(chunk_ref[...], grads)
    cols = weights.shape[1]
    owners, shifts = shift_ref.shape
    shard = weights.shape[0] // (4 * owners)
    sums = column_sum(grads.astype(F32))
    for y_side in range(2):
        blocks = []
        for c_side in range(2):
            first = (y_side * 2 + c_side) * shard
            here = (place_ref[1] == c_side) & (place_ref[2] == y_side)
            shift = jnp.where(here, shift_ref[...], 0.0)
            blocks.append(
                jnp.concatenate(
                    [
                        *(
                            weights[at : at + shard]
                            for at in range(first, weights.shape[0], 4 * shard)
                        ),
                        jnp.concatenate([shift, jnp.zeros((owners, cols - shifts), F32)], axis=1),
                        jnp.broadcast_to(sums, (8, cols)),
                    ]
                ).astype(BF16)
            )
        own_first = place_ref[0] == 0
        keep_ref[y_side] = jnp.where(own_first, blocks[0], blocks[1])
        give_ref[y_side] = jnp.where(own_first, blocks[1], blocks[0])


def qkv_weight(place, query_grads, own, from_c, from_y, chunk, shifts):
    tokens, width = chunk.shape
    cols = query_grads.shape[1] + own.shape[1]
    rows = width // 4 + shifts.shape[0] + 8
    vmem = pl.BlockSpec(memory_space=pltpu.VMEM)
    return pl.pallas_call(
        qkv_weight_kernel,
        out_shape=(jax.ShapeDtypeStruct((2, rows, cols), BF16),) * 2
        + (jax.ShapeDtypeStruct((tokens, cols), BF16),),
        in_specs=[pl.BlockSpec(memory_space=pltpu.SMEM)] + [vmem] * 6,
        out_specs=(vmem,) * 3,
        compiler_params=pltpu.CompilerParams(vmem_limit_bytes=VMEM_BYTES),
        cost_estimate=pl.CostEstimate(
            flops=14 * tokens * width * cols, bytes_accessed=4 * tokens * width, transcendentals=0
        ),
        name="qkv_weight",
    )(place, query_grads, own, from_c, from_y, chunk, shifts)


def spread_kernel(ring, in_ref, attn_ref, out_ref):
    units = in_ref.shape[1] // 8
    piece = units // ring
    half = attn_ref.shape[1] // 2
    for side in range(2):
        for plane in range(4):
            out_ref[2 * plane + side, :, :units] = jnp.concatenate(
                [
                    in_ref[:, at : at + piece]
                    for at in (
                        (side * ring + place) * 4 * piece + plane * piece for place in range(ring)
                    )
                ],
                axis=1,
            )
            out_ref[2 * plane + side, :, units:] = attn_ref[:, side * half : (side + 1) * half]


def spread_weights(w_in, w_attn_out, ring):
    shard, cols = w_in.shape
    vmem = pl.BlockSpec(memory_space=pltpu.VMEM)
    return pl.pallas_call(
        functools.partial(spread_kernel, ring),
        out_shape=jax.ShapeDtypeStruct((8, shard, cols // 8 + w_attn_out.shape[1] // 2), BF16),
        in_specs=[vmem] * 2,
        out_specs=vmem,
        compiler_params=pltpu.CompilerParams(vmem_limit_bytes=VMEM_BYTES),
        name="spread",
    )(w_in, w_attn_out)


def share_kernel(shard, shifts, first_ref, parts_ref, weight_ref, sums_ref, shift_ref):
    totals = [
        parts_ref[group].astype(F32) + parts_ref[GROUPS + group].astype(F32)
        for group in range(GROUPS)
    ]

    def part(number, rows):
        cols = slice(number * GROUP_WIDTH, (number + 1) * GROUP_WIDTH)
        return jnp.concatenate([total[rows, cols] for total in totals], axis=1)

    width = GROUPS * GROUP_WIDTH
    for number in range(3):
        weight_ref[:, number * width : (number + 1) * width] = part(number, slice(0, shard))
    sums = jnp.concatenate(
        [
            part(0, slice(shard, shard + 1)),
            part(2, slice(shard, shard + 1)),
            jnp.zeros((6, width), F32),
        ]
    )
    turn = jnp.where(first_ref[0] == 0, 0, width - first_ref[0])
    sums_ref[...] = pltpu.roll(sums, turn, 1)[:2, :shard]
    shift_ref[...] = sum(total[shard + 1 : shard + 2, :shifts] for total in totals)


def share(first, parts, shard, shifts):
    width = GROUPS * GROUP_WIDTH
    vmem = pl.BlockSpec(memory_space=pltpu.VMEM)
    return pl.pallas_call(
        functools.partial(share_kernel, shard, shifts),
        out_shape=(
            jax.ShapeDtypeStruct((shard, 3 * width), F32),
            jax.ShapeDtypeStruct((2, shard), F32),
            jax.ShapeDtypeStruct((1, shifts), F32),
        ),
        in_specs=[pl.BlockSpec(memory_space=pltpu.SMEM), vmem],
        out_specs=(vmem,) * 3,
        compiler_params=pltpu.CompilerParams(vmem_limit_bytes=VMEM_BYTES),
        cost_estimate=pl.CostEstimate(flops=10**10, bytes_accessed=10**6, transcendentals=0),
        name="share",
    )(first, parts)


def unpack_kernel(
    half,
    ring,
    core_ref,
    parts_ref,
    keep_ref,
    come_ref,
    _,
    __,
    in_ref,
    attn_ref,
    out_ref,
    *vec_refs,
):
    keep, come = keep_ref[...].astype(F32), come_ref[...].astype(F32)
    own_first = core_ref[0] == 0
    out_ref[:, :half] = jnp.where(own_first, keep, come)
    out_ref[:, half:] = jnp.where(own_first, come, keep)
    start = half + 128
    units = parts_ref.shape[3] - start
    piece = units // ring
    for side in range(2):
        for place in range(ring):
            at = start + place * piece
            to = (side * ring + place) * 4 * piece
            in_ref[:, to : to + 4 * piece] = jnp.concatenate(
                [parts_ref[plane, side, :, at : at + piece].astype(F32) for plane in range(4)],
                axis=1,
            )
        attn_ref[:, side * half : (side + 1) * half] = sum(
            parts_ref[plane, side, :, :half].astype(F32) for plane in range(4)
        )
    vectors = sum(parts_ref[plane, 0, :, half:start].astype(F32) for plane in range(4))
    rows = vectors.T
    for number, vec_ref in enumerate(vec_refs):
        vec_ref[...] = rows[number : number + 1]


def unpack(core, parts, keep, come, half, ring, *earlier):
    shard, cols = parts.shape[2:]
    units = cols - half - 128
    vmem = pl.BlockSpec(memory_space=pltpu.VMEM)
    return pl.pallas_call(
        functools.partial(unpack_kernel, half, ring),
        out_shape=(
            jax.ShapeDtypeStruct((shard, 8 * units), F32),
            jax.ShapeDtypeStruct((shard, 2 * half), F32),
            jax.ShapeDtypeStruct((keep.shape[0], 2 * half), F32),
        )
        + (jax.ShapeDtypeStruct((1, shard), F32),) * 6,
        in_specs=[pl.BlockSpec(memory_space=pltpu.SMEM)]
        + [vmem] * 3
        + [pl.BlockSpec(memory_space=pl.ANY)] * 2,
        out_specs=(vmem,) * 9,
        compiler_params=pltpu.CompilerParams(vmem_limit_bytes=VMEM_BYTES),
        name="unpack",
    )(core, parts, keep, come, *earlier)


def swap_sum(keep, give, axis):
    return keep.astype(F32) + lax.ppermute(give.astype(BF16), axis, SWAP).astype(F32)


def gather_plane(block):
    return lax.all_gather(block, PLANE, axis=0, tiled=True)


def spread_plane(parts):
    return lax.all_to_all(parts.reshape(4, -1, parts.shape[1]), PLANE, 0, 0, tiled=True)


def after(array, earlier):
    first = earlier[(slice(0, 1),) * earlier.ndim].reshape((1,) * array.ndim)
    return array + (first.astype(F32) * 0.0).astype(array.dtype)


def hold_kernel(*refs):
    del refs


def hold(array, earlier, cost=1):
    anywhere = pl.BlockSpec(memory_space=pl.ANY)
    return pl.pallas_call(
        hold_kernel,
        out_shape=jax.ShapeDtypeStruct(array.shape, array.dtype),
        in_specs=[anywhere] * 2,
        out_specs=anywhere,
        input_output_aliases={0: 0},
        cost_estimate=pl.CostEstimate(flops=cost, bytes_accessed=1, transcendentals=0),
        name="hold",
    )(array, earlier)


def pick_at(parts, index, axis):
    return lax.dynamic_index_in_dim(parts, index, axis, keepdims=False)


def pick(parts, index):
    return lax.dynamic_index_in_dim(parts, index, 0, keepdims=False)


def two(own, other, index):
    return jnp.where(index == 0, jnp.stack([own, other]), jnp.stack([other, own]))


def body(
    tokens,
    positions,
    w_qkv,
    qv_bias,
    w_attn_out,
    attn_out_bias,
    norm1_gain,
    norm1_bias,
    w_in,
    in_bias,
    w_out,
    out_bias,
    norm2_gain,
    norm2_bias,
    cotangent,
):
    seq_count, row_count, width = tokens.shape
    outer = lax.axis_size("e")
    seq_size = 2 * outer * GROUPS
    devices = seq_size * 4
    shard = w_qkv.shape[0]
    ff_shard = w_out.shape[0]
    ring = 4 * outer
    group = lax.axis_index(("r", "x"))
    place = lax.axis_index(("y", "c"))
    units = 2 * ring * ff_shard
    y_at, c_at = lax.axis_index("y"), lax.axis_index("c")
    qkv_cols = 3 * GROUP_WIDTH

    half = width // 2

    with jax.named_scope("gather_ff_weights"):
        if outer == 1:
            in_parts = spread_weights(w_in, w_attn_out, ring)
        else:
            in_cols = (
                w_in.reshape(shard, 2, ring, 4, 2 * ff_shard)
                .transpose(3, 1, 0, 2, 4)
                .reshape(4, 2, shard, units)
            )
            attn_cols = w_attn_out.reshape(shard, 2, half).transpose(1, 0, 2)
            in_parts = jnp.concatenate(
                [in_cols, jnp.broadcast_to(attn_cols, (4, 2, shard, half))], axis=3
            ).reshape(8, shard, units + half)
        in_parts = lax.all_to_all(
            in_parts, ("x", "y", "c"), 0, 0, tiled=True
        ).reshape(8 * shard, units + half)
        out_halves = w_out.reshape(ff_shard, 2, half).transpose(1, 0, 2)
        out_cols = two(
            pick(out_halves, c_at), lax.ppermute(pick(out_halves, 1 - c_at), "c", SWAP), c_at
        ).reshape(2 * ff_shard, half)
        packed = jnp.concatenate([in_parts, out_cols], axis=1)

    with jax.named_scope("gather_qkv_weights"):
        own_pos = lax.dynamic_slice_in_dim(positions, place * row_count, row_count, 1)
        shorts = jnp.stack(
            [
                qv_bias[0],
                qv_bias[1],
                attn_out_bias,
                norm1_gain,
                norm1_bias,
                out_bias,
                norm2_gain,
                norm2_bias,
            ]
        )
        spare = 64
        wide = qkv_cols + spare
        high = max(shard, 16)
        shift_rows = -(-2 * ff_shard // spare)
        smalls = jnp.concatenate(
            [
                jnp.broadcast_to(jnp.pad(shorts, ((0, 0), (0, spare - shard))), (2, 8, spare)),
                (own_pos >> 7).astype(BF16)[:, None],
                (own_pos & 127).astype(BF16)[:, None],
                jnp.broadcast_to(
                    jnp.pad(in_bias, (0, shift_rows * spare - 2 * ff_shard)).reshape(
                        shift_rows, spare
                    ),
                    (2, shift_rows, spare),
                ),
                jnp.zeros((2, high - 10 - shift_rows, spare), BF16),
            ],
            axis=1,
        )
        columns = (
            w_qkv.reshape(shard, 3, GROUPS, GROUP_WIDTH)
            .transpose(2, 0, 1, 3)
            .reshape(1, GROUPS, shard, qkv_cols)
        )
        columns = jnp.pad(columns, ((0, 0), (0, 0), (0, high - shard), (0, 0)))
        parcel = jnp.concatenate(
            [
                jnp.broadcast_to(columns, (2, GROUPS, high, qkv_cols)),
                jnp.broadcast_to(smalls[:, None], (2, GROUPS, high, spare)),
            ],
            axis=3,
        ).reshape(8, high, wide)
        parcel = lax.all_to_all(after(parcel, in_parts), SEQ_GROUP, 0, 0, tiled=True)

    with jax.named_scope("gather_tokens"):
        s_at, r_at, x_at = (lax.axis_index(name) for name in SEQ_GROUP)
        chunk = two(
            pick(tokens, s_at), lax.ppermute(pick(tokens, 1 - s_at), "s", SWAP), s_at
        )
        chunk = two(chunk, lax.ppermute(chunk, "r", SWAP), r_at)
        chunk = hold(chunk, packed)
        chunk = two(chunk, lax.ppermute(chunk, "x", SWAP), x_at)
        chunk = chunk.transpose(2, 1, 0, 3, 4).reshape(8 * row_count, width)

    with jax.named_scope("gather_qkv_weights"):
        parcels = lax.all_gather(hold(parcel, chunk), CHUNKS, axis=0, tiled=False)
        parcels = parcels.reshape(outer, 2, 2, 2, 2, 2, high, wide)
        order = (3, 0, 4, 5, 1, 2)
        qkv_slice = (
            parcels[..., :shard, :qkv_cols].transpose(*order, 6, 7).reshape(width, qkv_cols)
        )
        smalls = parcels[..., qkv_cols:]
        vectors = (
            smalls[..., :8, :shard].transpose(6, *order, 7).reshape(8, width).astype(F32)
        )
        pos_parts = smalls[..., 8:10, :row_count].astype(F32)
        chunk_pos = (pos_parts[..., 0, :] * 128.0 + pos_parts[..., 1, :]).reshape(
            outer, 2, 2, 8 * row_count
        )
        in_shift = pick_at(
            pick_at(smalls[..., 10 : 10 + shift_rows, :], x_at, 1), y_at, 1
        )
        in_shift = (
            in_shift.transpose(1, 0, 2, 3, 4, 5)
            .reshape(seq_size, shift_rows * spare)[:, : 2 * ff_shard]
            .reshape(2, units)
            .astype(F32)
        )

    with jax.named_scope("gather_ff_weights"):
        packed = lax.all_gather(packed, RING, axis=0, tiled=True)
        core = c_at.reshape(1).astype(jnp.int32)

    with jax.named_scope("project"):
        qv_slice = lax.dynamic_slice_in_dim(vectors[:2], group * GROUP_WIDTH, GROUP_WIDTH, 1)
        column_bias = jnp.concatenate(
            [qv_slice[0], jnp.zeros((GROUP_WIDTH,), F32), qv_slice[1]]
        )
        queries = (
            jnp.dot(chunk, qkv_slice[:, :GROUP_WIDTH], preferred_element_type=F32)
            + column_bias[:GROUP_WIDTH]
        ).astype(BF16)
        own_kv = (
            jnp.dot(chunk, qkv_slice[:, GROUP_WIDTH:], preferred_element_type=F32)
            + column_bias[GROUP_WIDTH:]
        ).astype(BF16)
    with jax.named_scope("gather_kv"):
        if outer > 1:
            own_kv = lax.all_gather(own_kv, "e", axis=0, tiled=True)
        y_kv = lax.ppermute(own_kv, "y", SWAP)
        key_values = [own_kv, lax.ppermute(own_kv, "c", SWAP)]
    ordered_pos = jnp.stack(
        [
            lax.dynamic_index_in_dim(
                lax.dynamic_index_in_dim(chunk_pos, y_at ^ ky, 1, keepdims=False),
                c_at ^ kc,
                1,
                keepdims=False,
            )
            for ky in (0, 1)
            for kc in (0, 1)
        ]
    )
    query_pos = lax.dynamic_index_in_dim(ordered_pos[0], lax.axis_index("e"), 0, keepdims=True)
    key_pos = ordered_pos.reshape(4 * outer, 8 * row_count)
    head_ids = group * GROUP_HEADS + jnp.arange(GROUP_HEADS)
    slopes = 2.0 ** (-8.0 * (head_ids + 1).astype(F32) / HEADS) * LOG2E

    with jax.named_scope("attention"):
        span = outer
        parts = ((0, 2), (2, 3), (3, 4))
        state = None
        for number, (first, last) in enumerate(parts):
            state = attend(
                slopes,
                queries,
                query_pos,
                key_pos[first * span : last * span],
                key_values[first:last],
                state,
                last=last == 4,
                earlier=(vectors, in_shift) if number == 1 else (),
            )
            if number == 0:
                y_kv = hold(y_kv, state[0])
                key_values += [y_kv, lax.ppermute(y_kv, "c", SWAP)]
        attended, log_sums, attended_low = state

    with jax.named_scope("return_attended"):
        returned = lax.all_to_all(
            attended_low.reshape(8, row_count, GROUP_WIDTH), SEQ_GROUP, 0, 0, tiled=True
        )
    with jax.named_scope("first_norm"):
        packed = hold(packed, returned)
        attn_own = packed[:, units : units + half]
        attn_swap = lax.ppermute(attn_own, "c", SWAP)
        hidden_low, hidden, normal, scale = first_norm(
            core,
            returned,
            tokens.reshape(2 * row_count, width),
            vectors,
            attn_own,
            attn_swap,
        )
        packed = hold(packed, hidden_low)
        swapped = lax.ppermute(packed, "c", SWAP)
    with jax.named_scope("gather_hidden"):
        hidden_group = gather_plane(hidden_low)
    with jax.named_scope("ff_forward"):
        activated_low, slope, gelu, ff_parts = ff_forward(
            core,
            hidden_group,
            in_shift,
            packed,
            swapped,
            slice(units + half, units + width),
        )
    with jax.named_scope("sum_ff"):
        ff_parts = spread_plane(ff_parts)
    with jax.named_scope("second_norm"):
        result, second_grad, ff_grad, sums = second_norm(
            ff_parts, hidden, cotangent.reshape(2 * row_count, width), vectors
        )
    with jax.named_scope("gather_ff_grad"):
        ff_grads = gather_plane(ff_grad)
    with jax.named_scope("ff_backward"):
        joined_grad, hidden_parts, grad_in_shift, grad_halves = ff_backward(
            core, ff_grads, slope, gelu, packed, swapped, slice(units + half, units + width)
        )
    with jax.named_scope("sum_hidden_grad"):
        hidden_parts = spread_plane(hidden_parts)
    with jax.named_scope("ff_weight_grads"):
        keep, give = ff_grads_of(core, activated_low, grad_halves, hidden_group, joined_grad)
        ff_keep, ff_give = keep, give
    with jax.named_scope("first_norm_back"):
        first_grad, out_grad, keep, give = first_back(
            core,
            hidden_parts,
            second_grad,
            normal,
            scale,
            vectors,
            attn_own,
            attn_swap,
            sums,
            returned,
            ff_keep,
        )
    with jax.named_scope("send_out_grad"):
        out_grads = lax.all_to_all(out_grad, SEQ_GROUP, 0, 0, tiled=True).reshape(
            8 * row_count, GROUP_WIDTH
        )
    with jax.named_scope("attn_weight_grad"):
        rows = jnp.concatenate(
            [swap_sum(keep, give, "c"), swap_sum(ff_keep, ff_give, "c")], axis=1
        ).astype(BF16)
        rows = hold(rows, out_grads)
        row_sums = lax.psum_scatter(rows, RING, scatter_dimension=0, tiled=True)

    with jax.named_scope("attention_back"):
        state, c_part, y_part, cy_part = attend_back(
            slopes,
            queries,
            query_pos,
            key_pos[span:],
            out_grads,
            attended,
            log_sums,
            key_values[1:],
            None,
            last=False,
            earlier=(rows,),
        )
        y_sum = swap_sum(y_part, cy_part, "c").astype(BF16)
        query_grads, own_part = attend_back(
            slopes,
            queries,
            query_pos,
            key_pos[:span],
            out_grads,
            attended,
            log_sums,
            key_values[:1],
            state,
            last=True,
            earlier=(y_sum,),
        )
    with jax.named_scope("sum_kv_grads"):
        from_c = lax.ppermute(c_part, "c", SWAP)
        from_y = lax.ppermute(y_sum, "y", SWAP)
        if outer > 1:
            total = own_part.astype(F32) + from_c.astype(F32) + from_y.astype(F32)
            own_part = lax.psum_scatter(
                total, "e", scatter_dimension=0, tiled=True
            ).astype(BF16)
            from_c = from_y = jnp.zeros_like(own_part)

    spot = jnp.stack([c_at, y_at, x_at]).astype(jnp.int32)
    with jax.named_scope("qkv_weight_grad"):
        keep, give, qkv_grad = qkv_weight(
            spot,
            query_grads,
            own_part,
            from_c,
            from_y,
            chunk,
            grad_in_shift.reshape(seq_size, 2 * ff_shard),
        )
        input_keep, input_give = input_back(spot, qkv_grad, qkv_slice)
        bundle = swap_sum(keep, give, "c").astype(BF16)
        from_x = lax.ppermute(input_give, "x", SWAP)
        parts = (hold(input_keep, bundle).astype(F32) + from_x.astype(F32)).reshape(
            2, 2, row_count, width
        )
        bundle = swap_sum(pick(bundle, y_at), pick(bundle, 1 - y_at), "y").astype(BF16)
        ends = width // 4 + seq_size
        shares = jnp.concatenate(
            [
                bundle[: width // 4].reshape(seq_size, shard, qkv_cols),
                jnp.broadcast_to(bundle[ends : ends + 1], (seq_size, 1, qkv_cols)),
                bundle[width // 4 : ends][:, None],
                jnp.zeros((seq_size, 6, qkv_cols), BF16),
            ],
            axis=1,
        )
    with jax.named_scope("input_grad"):
        from_r = lax.ppermute(
            hold(pick_at(parts, 1 - r_at, 1).astype(BF16), row_sums), "r", SWAP
        )
        parts = hold(pick_at(parts, r_at, 1), shares) + from_r.astype(F32)
    with jax.named_scope("qkv_weight_grad"):
        shares = lax.all_to_all(shares, SEQ_AXIS, 0, 0, tiled=True)
        from_s = lax.ppermute(
            hold(pick(parts, 1 - s_at).astype(BF16), shares), "s", SWAP
        )
    with jax.named_scope("ff_weight_grads"):
        own_cols = half + 128 + units
        row_sums = hold(row_sums, shares)
        plane_rows = row_sums[:, :own_cols].reshape(8, shard, own_cols)
    with jax.named_scope("qkv_weight_grad"):
        first_col = lax.axis_index(EVERY) * shard
        if outer == 1:
            grad_w_qkv, grad_qv, grad_in_bias = share(
                first_col.reshape(1).astype(jnp.int32), hold(shares, plane_rows), shard, 2 * ff_shard
            )
            grad_in_bias = grad_in_bias[0]
        else:
            totals = jnp.sum(
                shares.astype(F32).reshape(2 * outer, GROUPS, shard + 8, qkv_cols), axis=0
            )
            grad_w_qkv = (
                totals[:, :shard]
                .reshape(GROUPS, shard, 3, GROUP_WIDTH)
                .transpose(1, 2, 0, 3)
                .reshape(shard, 3 * width)
            )
            sums = (
                totals[:, shard].reshape(GROUPS, 3, GROUP_WIDTH).transpose(1, 0, 2).reshape(3, width)
            )
            grad_qv = lax.dynamic_slice_in_dim(sums[0::2], first_col, shard, 1)
            grad_in_bias = jnp.sum(totals[:, shard + 1, : 2 * ff_shard], axis=0)
    with jax.named_scope("input_grad"):
        input_grad = first_grad.reshape(2, row_count, width) + two(
            pick(parts, s_at), from_s.astype(F32), s_at
        )
    with jax.named_scope("ff_weight_grads"):
        exchanged = lax.all_to_all(
            plane_rows, ("x", "y", "c"), 0, 0, tiled=True
        ).reshape(4, 2, shard, own_cols)
        out_sums = row_sums[:, own_cols:].reshape(2, ff_shard, half)
        out_come = lax.ppermute(pick(out_sums, 1 - c_at), "c", SWAP)
        out_keep = pick(out_sums, c_at)
        if outer == 1:
            grad_w_in, grad_w_attn, grad_w_out, *vector_grads = unpack(
                core, exchanged, out_keep, out_come, half, ring, grad_w_qkv, input_grad
            )
            vector_grads = [row.reshape(shard) for row in vector_grads]
        else:
            grad_w_in = (
                exchanged[..., half + 128 :]
                .reshape(4, 2, shard, ring, 2 * ff_shard)
                .transpose(2, 1, 3, 0, 4)
                .reshape(shard, 2 * devices * ff_shard)
                .astype(F32)
            )
            grad_w_attn = (
                jnp.sum(exchanged[..., :half].astype(F32), axis=0)
                .transpose(1, 0, 2)
                .reshape(shard, width)
            )
            vector_grads = jnp.sum(exchanged[:, 0, :, half : half + 8].astype(F32), axis=0).T
            grad_w_out = (
                two(out_keep, out_come, c_at)
                .transpose(1, 0, 2)
                .reshape(ff_shard, width)
                .astype(F32)
            )
    return (
        result.reshape(2, row_count, width).astype(BF16),
        input_grad,
        grad_w_qkv,
        grad_qv,
        grad_w_attn,
        vector_grads[0],
        vector_grads[1],
        vector_grads[2],
        grad_w_in,
        grad_in_bias,
        grad_w_out,
        vector_grads[3],
        vector_grads[4],
        vector_grads[5],
    )


def solution(mesh):
    seq_size = mesh.shape["seq"]
    split = Mesh(mesh.devices.reshape(2, seq_size // 8, 2, 2, 2, 2), EVERY)
    tokens_at = P(None, EVERY, None)
    rows_at = P(EVERY, None)
    vector_at = P(EVERY)
    return jax.shard_map(
        body,
        mesh=split,
        in_specs=(
            tokens_at,
            P(None, SEQ_AXIS),
            rows_at,
            P(None, EVERY),
            rows_at,
            vector_at,
            vector_at,
            vector_at,
            rows_at,
            vector_at,
            rows_at,
            vector_at,
            vector_at,
            vector_at,
            tokens_at,
        ),
        out_specs=(
            tokens_at,
            tokens_at,
            rows_at,
            P(None, EVERY),
            rows_at,
            vector_at,
            vector_at,
            vector_at,
            rows_at,
            vector_at,
            rows_at,
            vector_at,
            vector_at,
            vector_at,
        ),
        check_vma=False,
    )
```

```python
import functools

import jax
import jax.numpy as jnp
from jax import lax
from jax.experimental import pallas as pl
from jax.experimental.pallas import tpu as pltpu
from jax.sharding import Mesh
from jax.sharding import PartitionSpec as P

HEADS = 12
HEAD_DIM = 64
GROUPS = 4
GROUP_HEADS = HEADS // GROUPS
GROUP_WIDTH = GROUP_HEADS * HEAD_DIM
EPSILON = 1e-12
SCORE_SCALE = 0.125
LOG2E = 1.4426950408889634
LOWEST = -1e30
GRAD_TILE = 256
KEY_BLOCK = 512
FF_TILE = 256
SEQ_GROUP = ("s", "r", "x")
CHUNKS = ("e", "y", "c")
RING = ("s", "e", "r")
PLANE = ("x", "y")
SEQ_AXIS = ("s", "e", "r", "x")
EVERY = ("s", "e", "r", "x", "y", "c")
SWAP = ((0, 1), (1, 0))
BF16 = jnp.bfloat16
F32 = jnp.float32
VMEM_BYTES = 60 * 2**20


def nt(a, b):
    return lax.dot_general(a, b, (((1,), (1,)), ((), ())), preferred_element_type=F32)


def tn(a, b):
    return lax.dot_general(a, b, (((0,), (0,)), ((), ())), preferred_element_type=F32)


def nn(a, b):
    return lax.dot_general(a, b, (((1,), (0,)), ((), ())), preferred_element_type=F32)


def head_cols(head, base=0):
    return slice(base + head * HEAD_DIM, base + (head + 1) * HEAD_DIM)


def log2_scores(keys, queries, slope, key_pos, query_pos):
    products = nt(keys, queries)
    distances = jnp.abs(key_pos * slope - query_pos * slope)
    return products * (SCORE_SCALE * LOG2E) - distances


def column(row):
    return jnp.broadcast_to(row, (8, row.shape[1])).T[:, :1]


def key_blocks(kv_refs):
    start = 0
    for piece in kv_refs:
        yield piece, start
        start += piece.shape[0]


def turn_positions(pk_ref, column_ref):
    length = pk_ref.shape[1]

    def turn(row, carry):
        at = pl.ds(pl.multiple_of(row * length, length), length)
        column_ref[at, :] = column(pk_ref[pl.ds(row, 1), :])
        return carry

    lax.fori_loop(0, pk_ref.shape[0], turn, 0)


def attend_kernel(deps, count, first, last, slopes_ref, q_ref, pq_ref, pk_ref, *refs):
    refs = refs[deps:]
    kv_refs, refs = refs[:count], refs[count:]
    if not first:
        (sum_in_ref, stat_in_ref), refs = refs[:2], refs[2:]
    sum_ref, stat_ref = refs[:2]
    column_ref = refs[-1]
    rows = q_ref.shape[0]
    query_pos = pq_ref[...]
    turn_positions(pk_ref, column_ref)
    for head in range(GROUP_HEADS):
        slope = slopes_ref[head]
        queries = q_ref[:, head_cols(head)]
        if first:
            carry = (
                jnp.full((1, rows), LOWEST, F32),
                jnp.zeros((1, rows), F32),
                jnp.zeros((HEAD_DIM, rows), F32),
            )
        else:
            carry = (
                stat_in_ref[head : head + 1, :],
                stat_in_ref[GROUP_HEADS + head : GROUP_HEADS + head + 1, :],
                sum_in_ref[head_cols(head), :],
            )
        for kv_ref, start in key_blocks(kv_refs):

            def visit(block, carry, kv_ref=kv_ref, start=start):
                top, total, summed = carry
                at = pl.ds(pl.multiple_of(block * KEY_BLOCK, KEY_BLOCK), KEY_BLOCK)
                pos_at = pl.ds(
                    pl.multiple_of(start + block * KEY_BLOCK, KEY_BLOCK), KEY_BLOCK
                )
                keys = kv_ref[at, head_cols(head)]
                values = kv_ref[at, head_cols(head, GROUP_WIDTH)]
                scores = log2_scores(keys, queries, slope, column_ref[pos_at, :], query_pos)
                new_top = jnp.maximum(top, jnp.max(scores, axis=0, keepdims=True))
                weights = jnp.exp2(scores - new_top)
                shrink = jnp.exp2(top - new_top)
                total = total * shrink + jnp.sum(weights, axis=0, keepdims=True)
                summed = summed * shrink + tn(values, weights.astype(BF16))
                return new_top, total, summed

            carry = lax.fori_loop(0, kv_ref.shape[0] // KEY_BLOCK, visit, carry)
        top, total, summed = carry
        if last:
            attended = summed / total
            sum_ref[head_cols(head), :] = attended
            refs[2][:, head_cols(head)] = attended.T.astype(BF16)
            stat_ref[head : head + 1, :] = top + jnp.log2(total)
        else:
            sum_ref[head_cols(head), :] = summed
            stat_ref[head : head + 1, :] = top
            stat_ref[GROUP_HEADS + head : GROUP_HEADS + head + 1, :] = total


def attend(slopes, queries, query_pos, key_pos, key_values, state, last, earlier):
    rows, length = queries.shape[0], key_pos.size
    vmem = pl.BlockSpec(memory_space=pltpu.VMEM)
    count = len(key_values)
    first = state is None
    state = () if first else state
    outs = [
        jax.ShapeDtypeStruct((GROUP_WIDTH, rows), F32),
        jax.ShapeDtypeStruct((GROUP_HEADS * (1 if last else 2), rows), F32),
    ]
    if last:
        outs.append(jax.ShapeDtypeStruct((rows, GROUP_WIDTH), BF16))
    return pl.pallas_call(
        functools.partial(attend_kernel, len(earlier), count, first, last),
        out_shape=tuple(outs),
        in_specs=[pl.BlockSpec(memory_space=pltpu.SMEM)]
        + [vmem] * 3
        + [pl.BlockSpec(memory_space=pl.ANY)] * len(earlier)
        + [vmem] * (count + len(state)),
        out_specs=(vmem,) * len(outs),
        scratch_shapes=[pltpu.VMEM((length, 1), F32)],
        compiler_params=pltpu.CompilerParams(vmem_limit_bytes=VMEM_BYTES),
        cost_estimate=pl.CostEstimate(
            flops=64 * rows * length * GROUP_WIDTH,
            bytes_accessed=rows * length,
            transcendentals=rows * length * GROUP_HEADS,
        ),
        name="attend",
    )(slopes, queries, query_pos, key_pos, *earlier, *key_values, *state)


def attend_back_kernel(
    deps, count, first, last, slopes_ref, q_ref, pq_ref, pk_ref, do_ref, out_ref, lse_ref, *refs
):
    refs = refs[deps:]
    kv_refs, refs = refs[:count], refs[count:]
    if not first:
        dq_in_ref, refs = refs[0], refs[1:]
    dq_ref, dkv_refs, column_ref = refs[0], refs[1 : count + 1], refs[-1]
    rows = q_ref.shape[0]
    query_pos = pq_ref[...]
    turn_positions(pk_ref, column_ref)
    for head in range(GROUP_HEADS):
        slope = slopes_ref[head]
        queries = q_ref[:, head_cols(head)]
        out_grads = do_ref[:, head_cols(head)]
        log_sum = lse_ref[head : head + 1, :]
        delta = jnp.sum(
            out_grads.astype(F32).T * out_ref[head_cols(head), :], axis=0, keepdims=True
        )
        if first:
            query_grads = jnp.zeros((HEAD_DIM, rows), F32)
        else:
            query_grads = dq_in_ref[head_cols(head), :]
        for (kv_ref, start), dkv_ref in zip(key_blocks(kv_refs), dkv_refs):

            def visit(block, query_grads, kv_ref=kv_ref, start=start, dkv_ref=dkv_ref):
                at = pl.ds(pl.multiple_of(block * KEY_BLOCK, KEY_BLOCK), KEY_BLOCK)
                pos_at = pl.ds(
                    pl.multiple_of(start + block * KEY_BLOCK, KEY_BLOCK), KEY_BLOCK
                )
                keys = kv_ref[at, head_cols(head)]
                values = kv_ref[at, head_cols(head, GROUP_WIDTH)]
                scores = log2_scores(keys, queries, slope, column_ref[pos_at, :], query_pos)
                probs = jnp.exp2(scores - log_sum)
                prob_grads = nt(values, out_grads)
                score_grads = (probs * (prob_grads - delta)).astype(BF16)
                dkv_ref[at, head_cols(head, GROUP_WIDTH)] = nn(
                    probs.astype(BF16), out_grads
                ).astype(BF16)
                dkv_ref[at, head_cols(head)] = (nn(score_grads, queries) * SCORE_SCALE).astype(
                    BF16
                )
                return query_grads + tn(keys, score_grads)

            query_grads = lax.fori_loop(0, kv_ref.shape[0] // KEY_BLOCK, visit, query_grads)
        if last:
            dq_ref[:, head_cols(head)] = (query_grads * SCORE_SCALE).T.astype(BF16)
        else:
            dq_ref[head_cols(head), :] = query_grads


def attend_back(
    slopes,
    queries,
    query_pos,
    key_pos,
    out_grads,
    attended,
    log_sums,
    key_values,
    state,
    last,
    earlier,
):
    rows, length = queries.shape[0], key_pos.size
    vmem = pl.BlockSpec(memory_space=pltpu.VMEM)
    count = len(key_values)
    first = state is None
    state = () if first else (state,)
    query_out = (
        jax.ShapeDtypeStruct((rows, GROUP_WIDTH), BF16)
        if last
        else jax.ShapeDtypeStruct((GROUP_WIDTH, rows), F32)
    )
    return pl.pallas_call(
        functools.partial(attend_back_kernel, len(earlier), count, first, last),
        out_shape=(query_out,)
        + tuple(jax.ShapeDtypeStruct(piece.shape, BF16) for piece in key_values),
        in_specs=[pl.BlockSpec(memory_space=pltpu.SMEM)]
        + [vmem] * 6
        + [pl.BlockSpec(memory_space=pl.ANY)] * len(earlier)
        + [vmem] * (count + len(state)),
        out_specs=(vmem,) * (1 + count),
        scratch_shapes=[pltpu.VMEM((length, 1), F32)],
        compiler_params=pltpu.CompilerParams(vmem_limit_bytes=VMEM_BYTES),
        cost_estimate=pl.CostEstimate(
            flops=84 * rows * length * GROUP_WIDTH,
            bytes_accessed=rows * length,
            transcendentals=rows * length * GROUP_HEADS,
        ),
        name="attend_back",
    )(
        slopes,
        queries,
        query_pos,
        key_pos,
        out_grads,
        attended,
        log_sums,
        *earlier,
        *key_values,
        *state,
    )


def merged(parts_ref):
    return jnp.concatenate(
        [
            jnp.concatenate(
                [parts_ref[seq * GROUPS + group] for group in range(GROUPS)], axis=1
            )
            for seq in range(2)
        ]
    )


def first_norm_kernel(
    core_ref,
    mixed_ref,
    rows_ref,
    vec_ref,
    own_ref,
    swap_ref,
    low_ref,
    hidden_ref,
    normal_ref,
    scale_ref,
):
    mixed = merged(mixed_ref)
    first = core_ref[0] == 0
    own, swap = nn(mixed, own_ref[...]), nn(mixed, swap_ref[...])
    lin = jnp.concatenate([jnp.where(first, own, swap), jnp.where(first, swap, own)], axis=1)
    total = rows_ref[...].astype(F32) + (lin + vec_ref[2:3, :])
    normal, scale = normalised(total)
    hidden = normal * vec_ref[3:4, :] + vec_ref[4:5, :]
    low_ref[...] = hidden.astype(BF16)
    hidden_ref[...] = hidden
    normal_ref[...] = normal
    scale_ref[...] = scale


def normalised(values):
    centred = values - jnp.mean(values, axis=1, keepdims=True)
    variance = jnp.mean(centred * centred, axis=1, keepdims=True)
    scale = lax.rsqrt(variance + EPSILON)
    return centred * scale, scale


def norm_back(grads, normal, scale, gain):
    scaled = grads * gain
    return (
        scaled
        - jnp.mean(scaled, axis=1, keepdims=True)
        - normal * jnp.mean(scaled * normal, axis=1, keepdims=True)
    ) * scale


def column_sum(values):
    return jnp.sum(values, axis=0, keepdims=True)


def first_norm(core, mixed, rows, vectors, own, swap):
    tokens, width = rows.shape
    vmem = pl.BlockSpec(memory_space=pltpu.VMEM)
    return pl.pallas_call(
        first_norm_kernel,
        out_shape=(
            jax.ShapeDtypeStruct((tokens, width), BF16),
            jax.ShapeDtypeStruct((tokens, width), F32),
            jax.ShapeDtypeStruct((tokens, width), F32),
            jax.ShapeDtypeStruct((tokens, 1), F32),
        ),
        in_specs=[pl.BlockSpec(memory_space=pltpu.SMEM)] + [vmem] * 5,
        out_specs=(vmem,) * 4,
        compiler_params=pltpu.CompilerParams(vmem_limit_bytes=VMEM_BYTES),
        cost_estimate=pl.CostEstimate(
            flops=64 * tokens * width * width, bytes_accessed=4 * width * width, transcendentals=0
        ),
        name="first_norm",
    )(core, mixed, rows, vectors, own, swap)


def ff_forward_kernel(
    units, out_columns, core_ref, hidden_ref, bias_ref, own_ref, swap_ref, act_ref, slope_ref, gelu_ref, parts_ref
):
    tokens = hidden_ref.shape[0]
    first = core_ref[0] == 0

    def visit(tile, carry):
        at = pl.ds(pl.multiple_of(tile * FF_TILE, FF_TILE), FF_TILE)
        rows = hidden_ref[at, :]
        own = nn(rows, own_ref[:, :units])
        swap = nn(rows, swap_ref[:, :units])
        gate = jnp.where(first, own, swap) + bias_ref[0:1, :]
        up = jnp.where(first, swap, own) + bias_ref[1:2, :]
        cdf = 0.5 * (1.0 + lax.erf(gate * (0.5**0.5)))
        density = jnp.exp(-0.5 * gate * gate) * 0.3989422804014327
        gelu = gate * cdf
        act = (gelu * up).astype(BF16)
        act_ref[at, :] = act
        gelu_ref[at, :] = gelu.astype(BF16)
        slope_ref[at, :] = (up * (cdf + gate * density)).astype(BF16)
        own = nn(act, own_ref[:, out_columns]).astype(BF16)
        swap = nn(act, swap_ref[:, out_columns]).astype(BF16)
        parts_ref[at, :] = jnp.concatenate(
            [jnp.where(first, own, swap), jnp.where(first, swap, own)], axis=1
        )
        return carry

    lax.fori_loop(0, tokens // FF_TILE, visit, 0)


def ff_forward(core, hidden, bias, own, swap, out_columns):
    tokens, width = hidden.shape
    units = bias.shape[1]
    vmem = pl.BlockSpec(memory_space=pltpu.VMEM)
    return pl.pallas_call(
        functools.partial(ff_forward_kernel, units, out_columns),
        out_shape=(
            jax.ShapeDtypeStruct((tokens, units), BF16),
            jax.ShapeDtypeStruct((tokens, units), BF16),
            jax.ShapeDtypeStruct((tokens, units), BF16),
            jax.ShapeDtypeStruct((tokens, width), BF16),
        ),
        in_specs=[pl.BlockSpec(memory_space=pltpu.SMEM)] + [vmem] * 4,
        out_specs=(vmem,) * 4,
        compiler_params=pltpu.CompilerParams(vmem_limit_bytes=VMEM_BYTES),
        cost_estimate=pl.CostEstimate(
            flops=32 * tokens * width * units,
            bytes_accessed=6 * width * units,
            transcendentals=2 * tokens * units,
        ),
        name="ff_forward",
    )(core, hidden, bias, own, swap)


def second_norm_kernel(
    parts_ref, hidden_ref, cotangent_ref, vec_ref, result_ref, grad_ref, low_ref, sums_ref
):
    lin = jnp.sum(parts_ref[...].astype(F32), axis=0) + vec_ref[5:6, :]
    normal, scale = normalised(hidden_ref[...] + lin)
    gain = vec_ref[6:7, :]
    result_ref[...] = (normal * gain + vec_ref[7:8, :]).astype(BF16)
    grads = cotangent_ref[...].astype(F32)
    back = norm_back(grads, normal, scale, gain)
    low = back.astype(BF16)
    grad_ref[...] = back
    low_ref[...] = low
    sums_ref[...] = jnp.concatenate(
        [
            column_sum(low.astype(F32)),
            column_sum(grads * normal),
            column_sum(grads),
            jnp.zeros((5, back.shape[1]), F32),
        ]
    )


def second_norm(parts, hidden, cotangent, vectors):
    tokens, width = hidden.shape
    vmem = pl.BlockSpec(memory_space=pltpu.VMEM)
    return pl.pallas_call(
        second_norm_kernel,
        out_shape=(
            jax.ShapeDtypeStruct((tokens, width), BF16),
            jax.ShapeDtypeStruct((tokens, width), F32),
            jax.ShapeDtypeStruct((tokens, width), BF16),
            jax.ShapeDtypeStruct((8, width), F32),
        ),
        in_specs=[vmem] * 4,
        out_specs=(vmem,) * 4,
        compiler_params=pltpu.CompilerParams(vmem_limit_bytes=VMEM_BYTES),
        cost_estimate=pl.CostEstimate(
            flops=20000 * tokens * width, bytes_accessed=20 * tokens * width, transcendentals=0
        ),
        name="second_norm",
    )(parts, hidden, cotangent, vectors)


def ff_backward_kernel(
    units,
    out_columns,
    core_ref,
    grad_ref,
    slope_ref,
    gelu_ref,
    own_ref,
    swap_ref,
    joined_ref,
    parts_ref,
    bias_ref,
    half_ref,
):
    tokens, width = grad_ref.shape
    half = width // 2
    first = core_ref[0] == 0
    bias_ref[...] = jnp.zeros_like(bias_ref)

    def visit(tile, carry):
        at = pl.ds(pl.multiple_of(tile * FF_TILE, FF_TILE), FF_TILE)
        left, right = grad_ref[at, :half], grad_ref[at, half:]
        half_ref[0, at, :] = left
        half_ref[1, at, :] = right
        act_grad = nt(jnp.where(first, left, right), own_ref[:, out_columns]) + nt(
            jnp.where(first, right, left), swap_ref[:, out_columns]
        )
        joined = []
        for which, factor in ((0, slope_ref), (1, gelu_ref)):
            side = (act_grad * factor[at, :].astype(F32)).astype(BF16)
            joined_ref[which, at, :] = side
            bias_ref[which : which + 1, :] += column_sum(side.astype(F32))
            joined.append(side)
        parts_ref[at, :] = (
            nt(jnp.where(first, joined[0], joined[1]), own_ref[:, :units])
            + nt(jnp.where(first, joined[1], joined[0]), swap_ref[:, :units])
        ).astype(BF16)
        return carry

    lax.fori_loop(0, tokens // FF_TILE, visit, 0)


def ff_backward(core, grads, slope, gelu, own, swap, out_columns):
    tokens, width = grads.shape
    units = slope.shape[1]
    vmem = pl.BlockSpec(memory_space=pltpu.VMEM)
    return pl.pallas_call(
        functools.partial(ff_backward_kernel, units, out_columns),
        out_shape=(
            jax.ShapeDtypeStruct((2, tokens, units), BF16),
            jax.ShapeDtypeStruct((tokens, width), BF16),
            jax.ShapeDtypeStruct((2, units), F32),
            jax.ShapeDtypeStruct((2, tokens, width // 2), BF16),
        ),
        in_specs=[pl.BlockSpec(memory_space=pltpu.SMEM)] + [vmem] * 5,
        out_specs=(vmem,) * 4,
        compiler_params=pltpu.CompilerParams(vmem_limit_bytes=VMEM_BYTES),
        cost_estimate=pl.CostEstimate(
            flops=32 * tokens * width * units,
            bytes_accessed=6 * width * units,
            transcendentals=0,
        ),
        name="ff_backward",
    )(core, grads, slope, gelu, own, swap)


def ff_grads_kernel(core_ref, act_ref, half_ref, hidden_ref, joined_ref, keep_ref, give_ref):
    core = core_ref[0]
    units = joined_ref.shape[2]

    def visit(tile, carry):
        at = pl.ds(pl.multiple_of(tile * GRAD_TILE, GRAD_TILE), GRAD_TILE)
        hidden = hidden_ref[:, at]
        act = act_ref[:, at]
        give_ref[at, :units] = tn(hidden, joined_ref[1 - core]).astype(BF16)
        give_ref[at, units:] = tn(act, half_ref[1 - core]).astype(BF16)
        keep_ref[at, :units] = tn(hidden, joined_ref[core]).astype(BF16)
        keep_ref[at, units:] = tn(act, half_ref[core]).astype(BF16)
        return carry

    lax.fori_loop(0, hidden_ref.shape[1] // GRAD_TILE, visit, 0)


def ff_grads_of(core, act, halves, hidden, joined):
    width = hidden.shape[1]
    cols = joined.shape[2] + halves.shape[2]
    vmem = pl.BlockSpec(memory_space=pltpu.VMEM)
    return pl.pallas_call(
        ff_grads_kernel,
        out_shape=(jax.ShapeDtypeStruct((width, cols), BF16),) * 2,
        in_specs=[pl.BlockSpec(memory_space=pltpu.SMEM)] + [vmem] * 4,
        out_specs=(vmem,) * 2,
        compiler_params=pltpu.CompilerParams(vmem_limit_bytes=VMEM_BYTES),
        cost_estimate=pl.CostEstimate(flops=6 * 10**9, bytes_accessed=10**4, transcendentals=0),
        name="ff_grads",
    )(core, act, halves, hidden, joined)


def first_back_kernel(
    core_ref,
    parts_ref,
    second_ref,
    normal_ref,
    scale_ref,
    vec_ref,
    own_ref,
    swap_ref,
    sums_ref,
    mixed_ref,
    _,
    grad_ref,
    out_ref,
    keep_ref,
    give_ref,
):
    tokens, width = second_ref.shape
    half, count = width // 2, tokens // 2
    normal = normal_ref[...]
    grads = second_ref[...] + jnp.sum(parts_ref[...].astype(F32), axis=0)
    back = norm_back(grads, normal, scale_ref[...], vec_ref[3:4, :])
    low = back.astype(BF16)
    grad_ref[...] = back
    own_left = core_ref[0] == 0
    left, right = low[:, :half], low[:, half:]
    out_grad = nt(jnp.where(own_left, left, right), own_ref[...]) + nt(
        jnp.where(own_left, right, left), swap_ref[...]
    )
    for seq in range(2):
        for group in range(GROUPS):
            out_ref[seq * GROUPS + group] = out_grad[
                seq * count : (seq + 1) * count, group * GROUP_WIDTH : (group + 1) * GROUP_WIDTH
            ].astype(BF16)
    rows = jnp.concatenate(
        [
            column_sum(low.astype(F32)),
            column_sum(grads * normal),
            column_sum(grads),
            sums_ref[0:3, :],
            jnp.zeros((122, width), F32),
        ]
    )
    turned = rows.T.astype(BF16)
    keep_ref[:, half:] = turned
    give_ref[:, half:] = turned
    mixed = merged(mixed_ref)
    left = tn(mixed, low[:, :half]).astype(BF16)
    right = tn(mixed, low[:, half:]).astype(BF16)
    keep_ref[:, :half] = jnp.where(own_left, left, right)
    give_ref[:, :half] = jnp.where(own_left, right, left)


def first_back(
    core, parts, second_grad, normal, scale, vectors, own, swap, sums, mixed, earlier
):
    tokens, width = second_grad.shape
    vmem = pl.BlockSpec(memory_space=pltpu.VMEM)
    return pl.pallas_call(
        first_back_kernel,
        out_shape=(
            jax.ShapeDtypeStruct((tokens, width), F32),
            jax.ShapeDtypeStruct((2 * GROUPS, tokens // 2, GROUP_WIDTH), BF16),
            jax.ShapeDtypeStruct((width, width // 2 + 128), BF16),
            jax.ShapeDtypeStruct((width, width // 2 + 128), BF16),
        ),
        in_specs=[pl.BlockSpec(memory_space=pltpu.SMEM)]
        + [vmem] * 9
        + [pl.BlockSpec(memory_space=pl.ANY)],
        out_specs=(vmem,) * 4,
        compiler_params=pltpu.CompilerParams(vmem_limit_bytes=VMEM_BYTES),
        cost_estimate=pl.CostEstimate(
            flops=64 * tokens * width * width, bytes_accessed=4 * width * width, transcendentals=0
        ),
        name="first_back",
    )(core, parts, second_grad, normal, scale, vectors, own, swap, sums, mixed, earlier)


def input_back_kernel(place_ref, grad_ref, weight_ref, keep_ref, give_ref):
    inputs = nt(grad_ref[...], weight_ref[...]).astype(BF16)
    pairs, count = keep_ref.shape[0], keep_ref.shape[1]
    own_first = place_ref[2] == 0
    for pair in range(pairs):
        first = inputs[2 * pair * count : (2 * pair + 1) * count]
        second = inputs[(2 * pair + 1) * count : (2 * pair + 2) * count]
        keep_ref[pair] = jnp.where(own_first, first, second)
        give_ref[pair] = jnp.where(own_first, second, first)


def input_back(place, grads, weight):
    tokens = grads.shape[0]
    width, cols = weight.shape
    vmem = pl.BlockSpec(memory_space=pltpu.VMEM)
    return pl.pallas_call(
        input_back_kernel,
        out_shape=(
            jax.ShapeDtypeStruct((4, tokens // 8, width), BF16),
            jax.ShapeDtypeStruct((4, tokens // 8, width), BF16),
        ),
        in_specs=[pl.BlockSpec(memory_space=pltpu.SMEM)] + [vmem] * 2,
        out_specs=(vmem,) * 2,
        compiler_params=pltpu.CompilerParams(vmem_limit_bytes=VMEM_BYTES),
        cost_estimate=pl.CostEstimate(
            flops=10 * tokens * width * cols, bytes_accessed=4 * tokens * width, transcendentals=0
        ),
        name="input_back",
    )(place, grads, weight)


def qkv_weight_kernel(
    place_ref,
    dq_ref,
    own_ref,
    c_ref,
    y_ref,
    chunk_ref,
    shift_ref,
    keep_ref,
    give_ref,
    grad_ref,
):
    kv_grad = own_ref[...].astype(F32) + c_ref[...].astype(F32) + y_ref[...].astype(F32)
    grads = jnp.concatenate([dq_ref[...], kv_grad.astype(BF16)], axis=1)
    grad_ref[...] = grads
    weights = tn(chunk_ref[...], grads)
    cols = weights.shape[1]
    owners, shifts = shift_ref.shape
    shard = weights.shape[0] // (4 * owners)
    sums = column_sum(grads.astype(F32))
    for y_side in range(2):
        blocks = []
        for c_side in range(2):
            first = (y_side * 2 + c_side) * shard
            here = (place_ref[1] == c_side) & (place_ref[2] == y_side)
            shift = jnp.where(here, shift_ref[...], 0.0)
            blocks.append(
                jnp.concatenate(
                    [
                        *(
                            weights[at : at + shard]
                            for at in range(first, weights.shape[0], 4 * shard)
                        ),
                        jnp.concatenate([shift, jnp.zeros((owners, cols - shifts), F32)], axis=1),
                        jnp.broadcast_to(sums, (8, cols)),
                    ]
                ).astype(BF16)
            )
        own_first = place_ref[0] == 0
        keep_ref[y_side] = jnp.where(own_first, blocks[0], blocks[1])
        give_ref[y_side] = jnp.where(own_first, blocks[1], blocks[0])


def qkv_weight(place, query_grads, own, from_c, from_y, chunk, shifts):
    tokens, width = chunk.shape
    cols = query_grads.shape[1] + own.shape[1]
    rows = width // 4 + shifts.shape[0] + 8
    vmem = pl.BlockSpec(memory_space=pltpu.VMEM)
    return pl.pallas_call(
        qkv_weight_kernel,
        out_shape=(jax.ShapeDtypeStruct((2, rows, cols), BF16),) * 2
        + (jax.ShapeDtypeStruct((tokens, cols), BF16),),
        in_specs=[pl.BlockSpec(memory_space=pltpu.SMEM)] + [vmem] * 6,
        out_specs=(vmem,) * 3,
        compiler_params=pltpu.CompilerParams(vmem_limit_bytes=VMEM_BYTES),
        cost_estimate=pl.CostEstimate(
            flops=14 * tokens * width * cols, bytes_accessed=4 * tokens * width, transcendentals=0
        ),
        name="qkv_weight",
    )(place, query_grads, own, from_c, from_y, chunk, shifts)


def spread_kernel(ring, in_ref, attn_ref, out_ref):
    units = in_ref.shape[1] // 8
    piece = units // ring
    half = attn_ref.shape[1] // 2
    for side in range(2):
        for plane in range(4):
            out_ref[2 * plane + side, :, :units] = jnp.concatenate(
                [
                    in_ref[:, at : at + piece]
                    for at in (
                        (side * ring + place) * 4 * piece + plane * piece for place in range(ring)
                    )
                ],
                axis=1,
            )
            out_ref[2 * plane + side, :, units:] = attn_ref[:, side * half : (side + 1) * half]


def spread_weights(w_in, w_attn_out, ring):
    shard, cols = w_in.shape
    vmem = pl.BlockSpec(memory_space=pltpu.VMEM)
    return pl.pallas_call(
        functools.partial(spread_kernel, ring),
        out_shape=jax.ShapeDtypeStruct((8, shard, cols // 8 + w_attn_out.shape[1] // 2), BF16),
        in_specs=[vmem] * 2,
        out_specs=vmem,
        compiler_params=pltpu.CompilerParams(vmem_limit_bytes=VMEM_BYTES),
        name="spread",
    )(w_in, w_attn_out)


def share_kernel(shard, shifts, first_ref, parts_ref, weight_ref, sums_ref, shift_ref):
    totals = [
        parts_ref[group].astype(F32) + parts_ref[GROUPS + group].astype(F32)
        for group in range(GROUPS)
    ]

    def part(number, rows):
        cols = slice(number * GROUP_WIDTH, (number + 1) * GROUP_WIDTH)
        return jnp.concatenate([total[rows, cols] for total in totals], axis=1)

    width = GROUPS * GROUP_WIDTH
    for number in range(3):
        weight_ref[:, number * width : (number + 1) * width] = part(number, slice(0, shard))
    sums = jnp.concatenate(
        [
            part(0, slice(shard, shard + 1)),
            part(2, slice(shard, shard + 1)),
            jnp.zeros((6, width), F32),
        ]
    )
    turn = jnp.where(first_ref[0] == 0, 0, width - first_ref[0])
    sums_ref[...] = pltpu.roll(sums, turn, 1)[:2, :shard]
    shift_ref[...] = sum(total[shard + 1 : shard + 2, :shifts] for total in totals)


def share(first, parts, shard, shifts):
    width = GROUPS * GROUP_WIDTH
    vmem = pl.BlockSpec(memory_space=pltpu.VMEM)
    return pl.pallas_call(
        functools.partial(share_kernel, shard, shifts),
        out_shape=(
            jax.ShapeDtypeStruct((shard, 3 * width), F32),
            jax.ShapeDtypeStruct((2, shard), F32),
            jax.ShapeDtypeStruct((1, shifts), F32),
        ),
        in_specs=[pl.BlockSpec(memory_space=pltpu.SMEM), vmem],
        out_specs=(vmem,) * 3,
        compiler_params=pltpu.CompilerParams(vmem_limit_bytes=VMEM_BYTES),
        cost_estimate=pl.CostEstimate(flops=10**10, bytes_accessed=10**6, transcendentals=0),
        name="share",
    )(first, parts)


def unpack_kernel(
    half,
    ring,
    core_ref,
    parts_ref,
    keep_ref,
    come_ref,
    _,
    __,
    in_ref,
    attn_ref,
    out_ref,
    *vec_refs,
):
    keep, come = keep_ref[...].astype(F32), come_ref[...].astype(F32)
    own_first = core_ref[0] == 0
    out_ref[:, :half] = jnp.where(own_first, keep, come)
    out_ref[:, half:] = jnp.where(own_first, come, keep)
    start = half + 128
    units = parts_ref.shape[3] - start
    piece = units // ring
    for side in range(2):
        for place in range(ring):
            at = start + place * piece
            to = (side * ring + place) * 4 * piece
            in_ref[:, to : to + 4 * piece] = jnp.concatenate(
                [parts_ref[plane, side, :, at : at + piece].astype(F32) for plane in range(4)],
                axis=1,
            )
        attn_ref[:, side * half : (side + 1) * half] = sum(
            parts_ref[plane, side, :, :half].astype(F32) for plane in range(4)
        )
    vectors = sum(parts_ref[plane, 0, :, half:start].astype(F32) for plane in range(4))
    rows = vectors.T
    for number, vec_ref in enumerate(vec_refs):
        vec_ref[...] = rows[number : number + 1]


def unpack(core, parts, keep, come, half, ring, *earlier):
    shard, cols = parts.shape[2:]
    units = cols - half - 128
    vmem = pl.BlockSpec(memory_space=pltpu.VMEM)
    return pl.pallas_call(
        functools.partial(unpack_kernel, half, ring),
        out_shape=(
            jax.ShapeDtypeStruct((shard, 8 * units), F32),
            jax.ShapeDtypeStruct((shard, 2 * half), F32),
            jax.ShapeDtypeStruct((keep.shape[0], 2 * half), F32),
        )
        + (jax.ShapeDtypeStruct((1, shard), F32),) * 6,
        in_specs=[pl.BlockSpec(memory_space=pltpu.SMEM)]
        + [vmem] * 3
        + [pl.BlockSpec(memory_space=pl.ANY)] * 2,
        out_specs=(vmem,) * 9,
        compiler_params=pltpu.CompilerParams(vmem_limit_bytes=VMEM_BYTES),
        name="unpack",
    )(core, parts, keep, come, *earlier)


def swap_sum(keep, give, axis):
    return keep.astype(F32) + lax.ppermute(give.astype(BF16), axis, SWAP).astype(F32)


def gather_plane(block):
    return lax.all_gather(block, PLANE, axis=0, tiled=True)


def spread_plane(parts):
    return lax.all_to_all(parts.reshape(4, -1, parts.shape[1]), PLANE, 0, 0, tiled=True)


def after(array, earlier):
    first = earlier[(slice(0, 1),) * earlier.ndim].reshape((1,) * array.ndim)
    return array + (first.astype(F32) * 0.0).astype(array.dtype)


def hold_kernel(*refs):
    del refs


def hold(array, earlier, cost=1):
    anywhere = pl.BlockSpec(memory_space=pl.ANY)
    return pl.pallas_call(
        hold_kernel,
        out_shape=jax.ShapeDtypeStruct(array.shape, array.dtype),
        in_specs=[anywhere] * 2,
        out_specs=anywhere,
        input_output_aliases={0: 0},
        cost_estimate=pl.CostEstimate(flops=cost, bytes_accessed=1, transcendentals=0),
        name="hold",
    )(array, earlier)


def pick_at(parts, index, axis):
    return lax.dynamic_index_in_dim(parts, index, axis, keepdims=False)


def pick(parts, index):
    return lax.dynamic_index_in_dim(parts, index, 0, keepdims=False)


def two(own, other, index):
    return jnp.where(index == 0, jnp.stack([own, other]), jnp.stack([other, own]))


def body(
    tokens,
    positions,
    w_qkv,
    qv_bias,
    w_attn_out,
    attn_out_bias,
    norm1_gain,
    norm1_bias,
    w_in,
    in_bias,
    w_out,
    out_bias,
    norm2_gain,
    norm2_bias,
    cotangent,
):
    seq_count, row_count, width = tokens.shape
    outer = lax.axis_size("e")
    seq_size = 2 * outer * GROUPS
    devices = seq_size * 4
    shard = w_qkv.shape[0]
    ff_shard = w_out.shape[0]
    ring = 4 * outer
    group = lax.axis_index(("r", "x"))
    place = lax.axis_index(("y", "c"))
    units = 2 * ring * ff_shard
    y_at, c_at = lax.axis_index("y"), lax.axis_index("c")
    qkv_cols = 3 * GROUP_WIDTH

    half = width // 2

    with jax.named_scope("gather_ff_weights"):
        if outer == 1:
            in_parts = spread_weights(w_in, w_attn_out, ring)
        else:
            in_cols = (
                w_in.reshape(shard, 2, ring, 4, 2 * ff_shard)
                .transpose(3, 1, 0, 2, 4)
                .reshape(4, 2, shard, units)
            )
            attn_cols = w_attn_out.reshape(shard, 2, half).transpose(1, 0, 2)
            in_parts = jnp.concatenate(
                [in_cols, jnp.broadcast_to(attn_cols, (4, 2, shard, half))], axis=3
            ).reshape(8, shard, units + half)
        in_parts = lax.all_to_all(
            in_parts, ("x", "y", "c"), 0, 0, tiled=True
        ).reshape(8 * shard, units + half)
        out_halves = w_out.reshape(ff_shard, 2, half).transpose(1, 0, 2)
        out_cols = two(
            pick(out_halves, c_at), lax.ppermute(pick(out_halves, 1 - c_at), "c", SWAP), c_at
        ).reshape(2 * ff_shard, half)
        packed = jnp.concatenate([in_parts, out_cols], axis=1)

    with jax.named_scope("gather_qkv_weights"):
        own_pos = lax.dynamic_slice_in_dim(positions, place * row_count, row_count, 1)
        shorts = jnp.stack(
            [
                qv_bias[0],
                qv_bias[1],
                attn_out_bias,
                norm1_gain,
                norm1_bias,
                out_bias,
                norm2_gain,
                norm2_bias,
            ]
        )
        spare = 64
        wide = qkv_cols + spare
        high = max(shard, 16)
        shift_rows = -(-2 * ff_shard // spare)
        smalls = jnp.concatenate(
            [
                jnp.broadcast_to(jnp.pad(shorts, ((0, 0), (0, spare - shard))), (2, 8, spare)),
                (own_pos >> 7).astype(BF16)[:, None],
                (own_pos & 127).astype(BF16)[:, None],
                jnp.broadcast_to(
                    jnp.pad(in_bias, (0, shift_rows * spare - 2 * ff_shard)).reshape(
                        shift_rows, spare
                    ),
                    (2, shift_rows, spare),
                ),
                jnp.zeros((2, high - 10 - shift_rows, spare), BF16),
            ],
            axis=1,
        )
        columns = (
            w_qkv.reshape(shard, 3, GROUPS, GROUP_WIDTH)
            .transpose(2, 0, 1, 3)
            .reshape(1, GROUPS, shard, qkv_cols)
        )
        columns = jnp.pad(columns, ((0, 0), (0, 0), (0, high - shard), (0, 0)))
        parcel = jnp.concatenate(
            [
                jnp.broadcast_to(columns, (2, GROUPS, high, qkv_cols)),
                jnp.broadcast_to(smalls[:, None], (2, GROUPS, high, spare)),
            ],
            axis=3,
        ).reshape(8, high, wide)
        parcel = lax.all_to_all(after(parcel, in_parts), SEQ_GROUP, 0, 0, tiled=True)

    with jax.named_scope("gather_tokens"):
        s_at, r_at, x_at = (lax.axis_index(name) for name in SEQ_GROUP)
        chunk = two(
            pick(tokens, s_at), lax.ppermute(pick(tokens, 1 - s_at), "s", SWAP), s_at
        )
        chunk = two(chunk, lax.ppermute(chunk, "r", SWAP), r_at)
        chunk = hold(chunk, packed)
        chunk = two(chunk, lax.ppermute(chunk, "x", SWAP), x_at)
        chunk = chunk.transpose(2, 1, 0, 3, 4).reshape(8 * row_count, width)

    with jax.named_scope("gather_qkv_weights"):
        parcels = lax.all_gather(hold(parcel, chunk), CHUNKS, axis=0, tiled=False)
        parcels = parcels.reshape(outer, 2, 2, 2, 2, 2, high, wide)
        order = (3, 0, 4, 5, 1, 2)
        qkv_slice = (
            parcels[..., :shard, :qkv_cols].transpose(*order, 6, 7).reshape(width, qkv_cols)
        )
        smalls = parcels[..., qkv_cols:]
        vectors = (
            smalls[..., :8, :shard].transpose(6, *order, 7).reshape(8, width).astype(F32)
        )
        pos_parts = smalls[..., 8:10, :row_count].astype(F32)
        chunk_pos = (pos_parts[..., 0, :] * 128.0 + pos_parts[..., 1, :]).reshape(
            outer, 2, 2, 8 * row_count
        )
        in_shift = pick_at(
            pick_at(smalls[..., 10 : 10 + shift_rows, :], x_at, 1), y_at, 1
        )
        in_shift = (
            in_shift.transpose(1, 0, 2, 3, 4, 5)
            .reshape(seq_size, shift_rows * spare)[:, : 2 * ff_shard]
            .reshape(2, units)
            .astype(F32)
        )

    with jax.named_scope("gather_ff_weights"):
        packed = lax.all_gather(packed, RING, axis=0, tiled=True)
        core = c_at.reshape(1).astype(jnp.int32)

    with jax.named_scope("project"):
        qv_slice = lax.dynamic_slice_in_dim(vectors[:2], group * GROUP_WIDTH, GROUP_WIDTH, 1)
        column_bias = jnp.concatenate(
            [qv_slice[0], jnp.zeros((GROUP_WIDTH,), F32), qv_slice[1]]
        )
        queries = (
            jnp.dot(chunk, qkv_slice[:, :GROUP_WIDTH], preferred_element_type=F32)
            + column_bias[:GROUP_WIDTH]
        ).astype(BF16)
        own_kv = (
            jnp.dot(chunk, qkv_slice[:, GROUP_WIDTH:], preferred_element_type=F32)
            + column_bias[GROUP_WIDTH:]
        ).astype(BF16)
    with jax.named_scope("gather_kv"):
        if outer > 1:
            own_kv = lax.all_gather(own_kv, "e", axis=0, tiled=True)
        y_kv = lax.ppermute(own_kv, "y", SWAP)
        key_values = [own_kv, lax.ppermute(own_kv, "c", SWAP)]
    ordered_pos = jnp.stack(
        [
            lax.dynamic_index_in_dim(
                lax.dynamic_index_in_dim(chunk_pos, y_at ^ ky, 1, keepdims=False),
                c_at ^ kc,
                1,
                keepdims=False,
            )
            for ky in (0, 1)
            for kc in (0, 1)
        ]
    )
    query_pos = lax.dynamic_index_in_dim(ordered_pos[0], lax.axis_index("e"), 0, keepdims=True)
    key_pos = ordered_pos.reshape(4 * outer, 8 * row_count)
    head_ids = group * GROUP_HEADS + jnp.arange(GROUP_HEADS)
    slopes = 2.0 ** (-8.0 * (head_ids + 1).astype(F32) / HEADS) * LOG2E

    with jax.named_scope("attention"):
        span = outer
        parts = ((0, 2), (2, 3), (3, 4))
        state = None
        for number, (first, last) in enumerate(parts):
            state = attend(
                slopes,
                queries,
                query_pos,
                key_pos[first * span : last * span],
                key_values[first:last],
                state,
                last=last == 4,
                earlier=(vectors, in_shift) if number == 1 else (),
            )
            if number == 0:
                y_kv = hold(y_kv, state[0])
                key_values += [y_kv, lax.ppermute(y_kv, "c", SWAP)]
        attended, log_sums, attended_low = state

    with jax.named_scope("return_attended"):
        returned = lax.all_to_all(
            attended_low.reshape(8, row_count, GROUP_WIDTH), SEQ_GROUP, 0, 0, tiled=True
        )
    with jax.named_scope("first_norm"):
        packed = hold(packed, returned)
        attn_own = packed[:, units : units + half]
        attn_swap = lax.ppermute(attn_own, "c", SWAP)
        hidden_low, hidden, normal, scale = first_norm(
            core,
            returned,
            tokens.reshape(2 * row_count, width),
            vectors,
            attn_own,
            attn_swap,
        )
        packed = hold(packed, hidden_low)
        swapped = lax.ppermute(packed, "c", SWAP)
    with jax.named_scope("gather_hidden"):
        hidden_group = gather_plane(hidden_low)
    with jax.named_scope("ff_forward"):
        activated_low, slope, gelu, ff_parts = ff_forward(
            core,
            hidden_group,
            in_shift,
            packed,
            swapped,
            slice(units + half, units + width),
        )
    with jax.named_scope("sum_ff"):
        ff_parts = spread_plane(ff_parts)
    with jax.named_scope("second_norm"):
        result, second_grad, ff_grad, sums = second_norm(
            ff_parts, hidden, cotangent.reshape(2 * row_count, width), vectors
        )
    with jax.named_scope("gather_ff_grad"):
        ff_grads = gather_plane(ff_grad)
    with jax.named_scope("ff_backward"):
        joined_grad, hidden_parts, grad_in_shift, grad_halves = ff_backward(
            core, ff_grads, slope, gelu, packed, swapped, slice(units + half, units + width)
        )
    with jax.named_scope("sum_hidden_grad"):
        hidden_parts = spread_plane(hidden_parts)
    with jax.named_scope("ff_weight_grads"):
        keep, give = ff_grads_of(core, activated_low, grad_halves, hidden_group, joined_grad)
        ff_keep, ff_give = keep, give
    with jax.named_scope("first_norm_back"):
        first_grad, out_grad, keep, give = first_back(
            core,
            hidden_parts,
            second_grad,
            normal,
            scale,
            vectors,
            attn_own,
            attn_swap,
            sums,
            returned,
            ff_keep,
        )
    with jax.named_scope("send_out_grad"):
        out_grads = lax.all_to_all(out_grad, SEQ_GROUP, 0, 0, tiled=True).reshape(
            8 * row_count, GROUP_WIDTH
        )
    with jax.named_scope("attn_weight_grad"):
        rows = jnp.concatenate(
            [swap_sum(keep, give, "c"), swap_sum(ff_keep, ff_give, "c")], axis=1
        ).astype(BF16)
        row_sums = lax.psum_scatter(rows, RING, scatter_dimension=0, tiled=True)

    with jax.named_scope("attention_back"):
        state, c_part, y_part, cy_part = attend_back(
            slopes,
            queries,
            query_pos,
            key_pos[span:],
            out_grads,
            attended,
            log_sums,
            key_values[1:],
            None,
            last=False,
            earlier=(rows,),
        )
        y_sum = swap_sum(y_part, cy_part, "c").astype(BF16)
        query_grads, own_part = attend_back(
            slopes,
            queries,
            query_pos,
            key_pos[:span],
            out_grads,
            attended,
            log_sums,
            key_values[:1],
            state,
            last=True,
            earlier=(y_sum,),
        )
    with jax.named_scope("sum_kv_grads"):
        from_c = lax.ppermute(c_part, "c", SWAP)
        from_y = lax.ppermute(y_sum, "y", SWAP)
        if outer > 1:
            total = own_part.astype(F32) + from_c.astype(F32) + from_y.astype(F32)
            own_part = lax.psum_scatter(
                total, "e", scatter_dimension=0, tiled=True
            ).astype(BF16)
            from_c = from_y = jnp.zeros_like(own_part)

    spot = jnp.stack([c_at, y_at, x_at]).astype(jnp.int32)
    with jax.named_scope("qkv_weight_grad"):
        keep, give, qkv_grad = qkv_weight(
            spot,
            query_grads,
            own_part,
            from_c,
            from_y,
            chunk,
            grad_in_shift.reshape(seq_size, 2 * ff_shard),
        )
        input_keep, input_give = input_back(spot, qkv_grad, qkv_slice)
        bundle = swap_sum(keep, give, "c").astype(BF16)
        from_x = lax.ppermute(input_give, "x", SWAP)
        parts = (hold(input_keep, bundle).astype(F32) + from_x.astype(F32)).reshape(
            2, 2, row_count, width
        )
        bundle = swap_sum(pick(bundle, y_at), pick(bundle, 1 - y_at), "y").astype(BF16)
        ends = width // 4 + seq_size
        shares = jnp.concatenate(
            [
                bundle[: width // 4].reshape(seq_size, shard, qkv_cols),
                jnp.broadcast_to(bundle[ends : ends + 1], (seq_size, 1, qkv_cols)),
                bundle[width // 4 : ends][:, None],
                jnp.zeros((seq_size, 6, qkv_cols), BF16),
            ],
            axis=1,
        )
    with jax.named_scope("input_grad"):
        from_r = lax.ppermute(
            hold(pick_at(parts, 1 - r_at, 1).astype(BF16), row_sums), "r", SWAP
        )
        parts = hold(pick_at(parts, r_at, 1), shares) + from_r.astype(F32)
    with jax.named_scope("qkv_weight_grad"):
        shares = lax.all_to_all(shares, SEQ_AXIS, 0, 0, tiled=True)
        from_s = lax.ppermute(
            hold(pick(parts, 1 - s_at).astype(BF16), shares), "s", SWAP
        )
    with jax.named_scope("ff_weight_grads"):
        own_cols = half + 128 + units
        row_sums = hold(row_sums, shares)
        plane_rows = row_sums[:, :own_cols].reshape(8, shard, own_cols)
    with jax.named_scope("qkv_weight_grad"):
        first_col = lax.axis_index(EVERY) * shard
        if outer == 1:
            grad_w_qkv, grad_qv, grad_in_bias = share(
                first_col.reshape(1).astype(jnp.int32), hold(shares, plane_rows), shard, 2 * ff_shard
            )
            grad_in_bias = grad_in_bias[0]
        else:
            totals = jnp.sum(
                shares.astype(F32).reshape(2 * outer, GROUPS, shard + 8, qkv_cols), axis=0
            )
            grad_w_qkv = (
                totals[:, :shard]
                .reshape(GROUPS, shard, 3, GROUP_WIDTH)
                .transpose(1, 2, 0, 3)
                .reshape(shard, 3 * width)
            )
            sums = (
                totals[:, shard].reshape(GROUPS, 3, GROUP_WIDTH).transpose(1, 0, 2).reshape(3, width)
            )
            grad_qv = lax.dynamic_slice_in_dim(sums[0::2], first_col, shard, 1)
            grad_in_bias = jnp.sum(totals[:, shard + 1, : 2 * ff_shard], axis=0)
    with jax.named_scope("input_grad"):
        input_grad = first_grad.reshape(2, row_count, width) + two(
            pick(parts, s_at), from_s.astype(F32), s_at
        )
    with jax.named_scope("ff_weight_grads"):
        exchanged = lax.all_to_all(
            plane_rows, ("x", "y", "c"), 0, 0, tiled=True
        ).reshape(4, 2, shard, own_cols)
        out_sums = row_sums[:, own_cols:].reshape(2, ff_shard, half)
        out_come = lax.ppermute(pick(out_sums, 1 - c_at), "c", SWAP)
        out_keep = pick(out_sums, c_at)
        if outer == 1:
            grad_w_in, grad_w_attn, grad_w_out, *vector_grads = unpack(
                core, exchanged, out_keep, out_come, half, ring, grad_w_qkv, input_grad
            )
            vector_grads = [row.reshape(shard) for row in vector_grads]
        else:
            grad_w_in = (
                exchanged[..., half + 128 :]
                .reshape(4, 2, shard, ring, 2 * ff_shard)
                .transpose(2, 1, 3, 0, 4)
                .reshape(shard, 2 * devices * ff_shard)
                .astype(F32)
            )
            grad_w_attn = (
                jnp.sum(exchanged[..., :half].astype(F32), axis=0)
                .transpose(1, 0, 2)
                .reshape(shard, width)
            )
            vector_grads = jnp.sum(exchanged[:, 0, :, half : half + 8].astype(F32), axis=0).T
            grad_w_out = (
                two(out_keep, out_come, c_at)
                .transpose(1, 0, 2)
                .reshape(ff_shard, width)
                .astype(F32)
            )
    return (
        result.reshape(2, row_count, width).astype(BF16),
        input_grad,
        grad_w_qkv,
        grad_qv,
        grad_w_attn,
        vector_grads[0],
        vector_grads[1],
        vector_grads[2],
        grad_w_in,
        grad_in_bias,
        grad_w_out,
        vector_grads[3],
        vector_grads[4],
        vector_grads[5],
    )


def solution(mesh):
    seq_size = mesh.shape["seq"]
    split = Mesh(mesh.devices.reshape(2, seq_size // 8, 2, 2, 2, 2), EVERY)
    tokens_at = P(None, EVERY, None)
    rows_at = P(EVERY, None)
    vector_at = P(EVERY)
    return jax.shard_map(
        body,
        mesh=split,
        in_specs=(
            tokens_at,
            P(None, SEQ_AXIS),
            rows_at,
            P(None, EVERY),
            rows_at,
            vector_at,
            vector_at,
            vector_at,
            rows_at,
            vector_at,
            rows_at,
            vector_at,
            vector_at,
            vector_at,
            tokens_at,
        ),
        out_specs=(
            tokens_at,
            tokens_at,
            rows_at,
            P(None, EVERY),
            rows_at,
            vector_at,
            vector_at,
            vector_at,
            rows_at,
            vector_at,
            rows_at,
            vector_at,
            vector_at,
            vector_at,
        ),
        check_vma=False,
    )
```
